32 devices in a mesh: dp: 8 (over z, y), mp: 4 (over x, core).
Axes of the slice: x: 2, y: 2, z: 4, core: 2. Of those that a mesh axis runs over, the one named last changes fastest.
Arguments:
- hidden_in: bfloat16 [32, 256, 1152], P(('dp', 'mp')), may hold values from -6 to 6
- conditioning: bfloat16 [32, 1152], P(('dp', 'mp')), may hold values from -6 to 6
- live_images: int32 [32], P(('dp', 'mp')), may hold values 0 or 1
- out_grad: bfloat16 [32, 256, 1152], P(('dp', 'mp')), may hold values from -6 to 6
- ada_weight: bfloat16 [1152, 6912], P(None, 'mp'), may hold values from -0.1875 to 0.1875
- ada_bias: bfloat16 [6912], P('mp'), may hold values from -3 to 3
- qkv_weight: bfloat16 [1152, 3456], replicated, may hold values from -0.1875 to 0.1875
- qv_bias: bfloat16 [2304], replicated, may hold values from -3 to 3
- proj_weight: bfloat16 [1152, 1152], replicated, may hold values from -0.75 to 0.75
- proj_bias: bfloat16 [1152], replicated, may hold values from -3 to 3
- up_weight: bfloat16 [1152, 4608], replicated, may hold values from -0.1875 to 0.1875
- up_bias: bfloat16 [4608], replicated, may hold values from -3 to 3
- down_weight: bfloat16 [4608, 1152], replicated, may hold values from -0.09375 to 0.09375
- down_bias: bfloat16 [1152], replicated, may hold values from -3 to 3
Outputs:
- mixed: bfloat16 [32, 256, 1152], P(('dp', 'mp'))
- grad_hidden: float32 [32, 256, 1152], P(('dp', 'mp'))
- grad_conditioning: float32 [32, 1152], P(('dp', 'mp'))
- grad_ada_weight: float32 [1152, 6912], P('dp', 'mp')
- grad_ada_bias: float32 [6912], P('mp')
- grad_qkv_weight: float32 [1152, 3456], P('dp', 'mp')
- grad_qv_bias: float32 [2304], P('mp')
- grad_proj_weight: float32 [1152, 1152], P('dp', 'mp')
- grad_proj_bias: float32 [1152], P('mp')
- grad_up_weight: float32 [1152, 4608], P('dp', 'mp')
- grad_up_bias: float32 [4608], P('mp')
- grad_down_weight: float32 [4608, 1152], P('dp', 'mp')
- grad_down_bias: float32 [1152], P('mp')
The draws below stay inside these ranges and needn't reach their ends.
All inputs are finite; a program needn't handle non-finite values. No bound on the sum of `live_images` on one device may be relied on, other than what follows from the above.
Results may differ from the reference program's by a relative error of at most 0.015.
The reference program's roundings to bfloat16 on the way count: a program that leaves them out, or rounds other values in their place, can miss the bound.
Values may be sent and summed in bfloat16 or wider, within the bound.
A program may use at most 256 MiB of HBM per device.

```python
from functools import partial
import jax
import jax.numpy as jnp
from jax import lax

D = 1152
HEADS = 16
HEAD_DIM = 72
FF = 4608
SEQ = 256
IMAGES = 32


def set_ends(values, key, low, high):
    shape = values.shape
    place = [jax.random.randint(jax.random.fold_in(key, axis), (), 0, shape[axis]) for axis in range(len(shape))]
    values = values.at[tuple(place)].set(low)
    longest = shape.index(max(shape))
    place[longest] = (place[longest] + 1) % shape[longest]
    return values.at[tuple(place)].set(high)


def block_levels(stream_key, dims, shards, low, largest):
    loudness = 1.0
    for axis_at, blocks in shards:
        steps = jax.random.uniform(jax.random.fold_in(jax.random.fold_in(stream_key, 6), axis_at), (blocks,), jnp.float32, low / len(shards), largest / len(shards))
        loudness = loudness * jnp.repeat(jnp.exp(steps), dims[axis_at] // blocks).reshape((-1,) + (1,) * (len(dims) - 1 - axis_at))
    return loudness


def gaussian(rng, dims, deviation, most, cuts=(), dtype=jnp.bfloat16):
    drawn = deviation * jax.random.normal(rng, dims, jnp.float32)
    if cuts:
        drawn = drawn * block_levels(rng, dims, cuts, -0.22, 0.18)
    return jnp.clip(drawn, -most, most).astype(dtype)


def setup_inputs(seed: int = 0) -> dict:
    arg_keys = jax.random.split(jax.random.key(seed), 15)
    return {
        "hidden_in": gaussian(arg_keys[0], (IMAGES, SEQ, D), 1.0, 6.0, ((0, 32),)),
        "conditioning": gaussian(arg_keys[1], (IMAGES, D), 1.0, 6.0, ((0, 32),)),
        "live_images": set_ends((jax.random.randint(arg_keys[2], (IMAGES,), 0, 4) < 3).astype(jnp.int32), jax.random.fold_in(arg_keys[2], 1), 0, 1),
        "out_grad": gaussian(arg_keys[3], (IMAGES, SEQ, D), 1.0, 6.0, ((0, 32),)),
        "ada_weight": gaussian(arg_keys[4], (D, 6 * D), D ** -0.5, 0.1875, ((1, 4),)),
        "ada_bias": gaussian(arg_keys[5], (6 * D,), 0.5, 3.0, ((0, 4),)),
        "qkv_weight": gaussian(arg_keys[6], (D, 3 * D), D ** -0.5, 0.1875),
        "qv_bias": gaussian(arg_keys[7], (2 * D,), 0.5, 3.0),
        "proj_weight": gaussian(arg_keys[8], (D, D), HEAD_DIM ** -0.5, 0.75),
        "proj_bias": gaussian(arg_keys[9], (D,), 0.5, 3.0),
        "up_weight": gaussian(arg_keys[10], (D, FF), D ** -0.5, 0.1875),
        "up_bias": gaussian(arg_keys[11], (FF,), 0.5, 3.0),
        "down_weight": gaussian(arg_keys[12], (FF, D), FF ** -0.5, 0.09375),
        "down_bias": gaussian(arg_keys[13], (D,), 0.5, 3.0),
    }


@jax.custom_vjp
def low(v):
    return lax.optimization_barrier(v.astype(jnp.bfloat16)).astype(jnp.float32)

@jax.custom_vjp
def low_back(v):
    return v

def low_keep(v):
    return (low(v), None)

def low_pass(kept, grad):
    return (grad,)

def back_keep(v):
    return (v, None)

def back_low(kept, grad):
    return (low(grad),)
low.defvjp(low_keep, low_pass)
low_back.defvjp(back_keep, back_low)
HIGHEST = lax.Precision.HIGHEST

def layer_norm(values):
    center = values - lax.optimization_barrier(jnp.mean(values, axis=-1, keepdims=True))
    spread = lax.optimization_barrier(jnp.mean(center * center, axis=-1, keepdims=True))
    return center * lax.rsqrt(spread + 1e-06)

def trunk(hidden, modulation, qkv_weight, qv_bias, proj_weight, proj_bias, up_weight, up_bias, down_weight, down_bias):
    images = hidden.shape[0]
    pieces = [modulation[:, None, index * D:(index + 1) * D] for index in range(6)]
    shift_a, scale_a, gate_a, shift_m, scale_m, gate_m = pieces
    mod_a = low(layer_norm(hidden) * (1.0 + scale_a) + shift_a)
    zero_bias = jnp.zeros((D,), jnp.float32)
    full_bias = jnp.concatenate([qv_bias[:D], zero_bias, qv_bias[D:]])
    qkv = jnp.einsum('bld,de->ble', mod_a, qkv_weight, precision=HIGHEST) + full_bias
    qkv = low(low_back(qkv))
    queries = qkv[..., :D].reshape(images, SEQ, HEADS, HEAD_DIM)
    key_rows = qkv[..., D:2 * D].reshape(images, SEQ, HEADS, HEAD_DIM)
    value_rows = qkv[..., 2 * D:].reshape(images, SEQ, HEADS, HEAD_DIM)
    scores = jnp.einsum('bqhe,bkhe->bhqk', queries, key_rows, precision=HIGHEST) * HEAD_DIM ** (-0.5)
    scores = low_back(scores)
    probs = low(jax.nn.softmax(scores, axis=-1))
    attended = jnp.einsum('bhqk,bkhe->bqhe', probs, value_rows, precision=HIGHEST).reshape(images, SEQ, D)
    attended = low(low_back(attended))
    attn_out = low_back(jnp.einsum('bld,de->ble', attended, proj_weight, precision=HIGHEST) + proj_bias)
    after = hidden + gate_a * attn_out
    mod_m = low(layer_norm(after) * (1.0 + scale_m) + shift_m)
    pre_act = low_back(jnp.einsum('bld,df->blf', mod_m, up_weight, precision=HIGHEST) + up_bias)
    act_rows = low(jax.nn.gelu(pre_act, approximate=True))
    branch = low_back(jnp.einsum('blf,fd->bld', act_rows, down_weight, precision=HIGHEST) + down_bias)
    return after + gate_m * branch

def block(hidden, condition, ada_weight, ada_bias, qkv_weight, qv_bias, proj_weight, proj_bias, up_weight, up_bias, down_weight, down_bias):
    silu_cond = low(jax.nn.silu(condition))
    modulation = low(low_back(jnp.dot(silu_cond, ada_weight, precision=HIGHEST) + ada_bias))
    step_fn = jax.checkpoint(partial(trunk, qkv_weight=qkv_weight, qv_bias=qv_bias, proj_weight=proj_weight, proj_bias=proj_bias, up_weight=up_weight, up_bias=up_bias, down_weight=down_weight, down_bias=down_bias))
    grouped = (hidden.reshape(-1, 8, SEQ, D), modulation.reshape(-1, 8, 6 * D))
    result = lax.map(lambda pair: step_fn(pair[0], pair[1]), grouped)
    return result.reshape(hidden.shape)

def reference(hidden_in, conditioning, live_images, out_grad, ada_weight, ada_bias, qkv_weight, qv_bias, proj_weight, proj_bias, up_weight, up_bias, down_weight, down_bias):
    primals = tuple((array.astype(jnp.float32) for array in (hidden_in, conditioning, ada_weight, ada_bias, qkv_weight, qv_bias, proj_weight, proj_bias, up_weight, up_bias, down_weight, down_bias)))
    output, pull_back = jax.vjp(block, *primals)
    cotangent = out_grad.astype(jnp.float32) * live_images.astype(jnp.float32)[:, None, None]
    grads = pull_back(cotangent)
    return (output.astype(jnp.bfloat16), grads[0], grads[1], grads[2], grads[3], grads[4], grads[5], grads[6], grads[7], grads[8], grads[9], grads[10], grads[11])
```

```python
from functools import partial

import jax
import jax.numpy as jnp
from jax import lax
from jax.experimental import pallas as pl
from jax.experimental.pallas import tpu as pltpu
from jax.sharding import PartitionSpec as P

D = 1152
HEADS = 16
HEAD_DIM = 72
SEQ = 256


def norm_rows(values):
    center = values - jnp.mean(values, axis=-1, keepdims=True)
    inverse = lax.rsqrt(jnp.mean(center * center, axis=-1, keepdims=True) + 1e-06)
    return (center * inverse, inverse)


def norm_back(grad_normed, normed, inverse):
    mean_grad = jnp.mean(grad_normed, axis=-1, keepdims=True)
    mean_prod = jnp.mean(grad_normed * normed, axis=-1, keepdims=True)
    return inverse * (grad_normed - mean_grad - normed * mean_prod)


MESH_ID = pl.DeviceIdType.MESH
BF16 = jnp.bfloat16
F32 = jnp.float32
INNER = 8
BLOCK = 144
TOKENS = 4 * SEQ
PEERS = ("c", "x", "xc", "y", "yc", "l", "h", "yl", "yh", "lh", "ylh")
FAR = ("y", "l", "h", "yl", "yh", "lh", "ylh")


class Place:
    def __init__(self, outer):
        data, model = lax.axis_index("dp"), lax.axis_index("mp")
        self.outer = outer
        self.low = data % outer
        self.h_index = data // outer
        self.m_index = model
        self.bits = {
            "h": self.h_index // 4,
            "l": (self.h_index // 2) % 2,
            "y": self.h_index % 2,
            "x": model // 2,
            "c": model % 2,
        }

    def flipped(self, names):
        return {key: (1 - bit if key in names else bit) for key, bit in self.bits.items()}

    def h_at(self, names):
        bits = self.flipped(names)
        return bits["h"] * 4 + bits["l"] * 2 + bits["y"]

    def m_at(self, names):
        bits = self.flipped(names)
        return bits["x"] * 2 + bits["c"]

    def device(self, names):
        return (self.h_at(names) * self.outer + self.low, self.m_at(names))


class Links:
    def __init__(self, place, send_sems, recv_sems):
        self.place = place
        self.send_sems = send_sems
        self.recv_sems = recv_sems
        self.copies = {}

    def send(self, name, source, target, to):
        index = len(self.copies)
        copy = pltpu.make_async_remote_copy(
            src_ref=source,
            dst_ref=target,
            send_sem=self.send_sems.at[index],
            recv_sem=self.recv_sems.at[index],
            device_id=self.place.device(to),
            device_id_type=MESH_ID,
        )
        copy.start()
        self.copies[name] = copy

    def arrived(self, name):
        self.copies[name].wait_recv()

    def drain(self):
        for copy in self.copies.values():
            copy.wait_send()


def scatter_first(links, name, axes, grad, first, pair):
    b1, b2 = pair
    links.send((name, 0, b1, b2), grad.at[1, b1, b2], first.at[b1, b2], axes[0])


def scatter_second(links, name, axes, grad, first, second, b2):
    links.arrived((name, 0, 1, b2))
    grad[0, 1, b2] = (grad[0, 1, b2].astype(F32) + first[1, b2].astype(F32)).astype(BF16)
    links.send((name, 1, b2), grad.at[0, 1, b2], second.at[b2], axes[1])


def scatter_third(links, name, axes, grad, first, second, third):
    links.arrived((name, 0, 0, 1))
    links.arrived((name, 1, 1))
    grad[0, 0, 1] = (
        grad[0, 0, 1].astype(F32) + first[0, 1].astype(F32) + second[1].astype(F32)
    ).astype(BF16)
    links.send((name, 2), grad.at[0, 0, 1], third, axes[2])


def scatter_last(links, name, grad, first, second, third, out):
    links.arrived((name, 0, 0, 0))
    links.arrived((name, 1, 0))
    links.arrived((name, 2))
    out[...] = (
        grad[0, 0, 0].astype(F32)
        + first[0, 0].astype(F32)
        + second[0].astype(F32)
        + third[...].astype(F32)
    )


ORDER = ((1, 1), (1, 0), (0, 1), (0, 0))


def trunk_kernel(
    outer,
    mod_a_t,
    att_t,
    mod_m_t,
    act_half,
    g_branch_t,
    g_pre,
    g_qp,
    rows,
    cond,
    out_down,
    out_up,
    out_qp,
    out_rows,
    left_a,
    left_t,
    left_m,
    right_act,
    left_b,
    right_u,
    right_q,
    row_group,
    row_all,
    grad_d,
    grad_u,
    grad_q,
    first_d,
    first_u,
    first_q,
    second_d,
    second_u,
    second_q,
    third_d,
    third_u,
    third_q,
    send_sems,
    recv_sems,
    local_sems,
):
    place = Place(outer)
    barrier = pltpu.get_barrier_semaphore()
    for names in PEERS:
        pl.semaphore_signal(
            barrier, inc=1, device_id=place.device(names), device_id_type=MESH_ID
        )
    pl.semaphore_wait(barrier, len(PEERS))
    links = Links(place, send_sems, recv_sems)
    bits = place.bits
    m_here = place.m_index
    yc_here = bits["y"] * 2 + bits["c"]

    def spot(index):
        return pl.ds(pl.multiple_of(index * SEQ, SEQ), SEQ)

    def yc_at(names):
        flipped = place.flipped(names)
        return flipped["y"] * 2 + flipped["c"]

    here, here_yc = spot(m_here), spot(yc_here)
    local = []

    def keep(source, target):
        copy = pltpu.make_async_copy(source, target, local_sems.at[len(local)])
        copy.start()
        local.append(copy)

    y_here, y_there = bits["y"], 1 - bits["y"]
    halves = [pl.ds(0, 1152), pl.ds(1152, 1152)]
    for h in range(2):
        links.send(
            ("act", "y", h), act_half.at[y_there, :, halves[h]],
            right_act.at[here_yc, halves[h]], "y",
        )
        links.send(
            ("act", "c", h), act_half.at[y_here, :, halves[h]],
            right_act.at[here_yc, halves[h]], "c",
        )
        keep(act_half.at[y_here, :, halves[h]], right_act.at[here_yc, halves[h]])
    for to in ("y", "c", "yc"):
        core = place.flipped(to)["c"]
        for x in range(2):
            links.send(
                ("gb", to, x), g_branch_t.at[2 * x + core], left_b.at[x, :, here_yc], to
            )
    for x in range(2):
        keep(g_branch_t.at[2 * x + bits["c"]], left_b.at[x, :, here_yc])
    for name, source, target in (
        ("m", mod_m_t, left_m), ("a", mod_a_t, left_a), ("t", att_t, left_t),
    ):
        for to in ("x", "c"):
            links.send((name, to), source, target.at[:, here], to)
        keep(source, target.at[:, here])
        if name == "m":
            for to in ("xc", "x", "c"):
                links.send(("u", to), g_pre.at[place.m_at(to)], right_u.at[here], to)
            keep(g_pre.at[m_here], right_u.at[here])
    for to in ("xc", "x", "c"):
        links.send(("q", to), g_qp.at[place.m_at(to)], right_q.at[here], to)
        links.send(("row", to), rows.at[place.m_at(to)], row_group.at[m_here, pl.ds(0, 32)], to)
    keep(g_qp.at[m_here], right_q.at[here])
    keep(rows.at[m_here], row_group.at[m_here, pl.ds(0, 32)])
    for image in range(4):
        keep(cond.at[image], row_group.at[image, pl.ds(32, 16)])

    for copy in local:
        copy.wait()
    for to in ("xc", "x", "c"):
        links.arrived(("row", to))
    row_all[place.h_index] = row_group[...]
    for to in FAR:
        links.send(("rows", to), row_group, row_all.at[place.h_index], to)

    spot_y = spot(yc_at("y"))
    for h in range(2):
        links.arrived(("act", "y", h))
        links.send(
            ("act", "f", h), right_act.at[spot_y, halves[h]], right_act.at[spot_y, halves[h]], "c"
        )
    for to in ("y", "c", "yc"):
        for x in range(2):
            links.arrived(("gb", to, x))
    for h in range(2):
        links.arrived(("act", "c", h))
        links.arrived(("act", "f", h))

    for step, (b1, b2) in enumerate(ORDER):
        h = place.flipped("h" if b1 else "")["h"]
        x = place.flipped("x" if b2 else "")["x"]
        wide = jnp.dot(
            left_b[x],
            right_act[:, pl.ds(pl.multiple_of(h * 1152, 1152), 1152)],
            preferred_element_type=F32,
        ).astype(BF16)
        top, bottom = wide[:BLOCK], wide[BLOCK:]
        grad_d[bits["l"], b1, b2] = jnp.concatenate([top[:, :576], bottom[:, :576]], axis=1)
        grad_d[1 - bits["l"], b1, b2] = jnp.concatenate([top[:, 576:], bottom[:, 576:]], axis=1)
        scatter_first(links, "d", "lhx", grad_d, first_d, (b1, b2))

    spot_x = spot(place.m_at("x"))
    for name, target in (("m", left_m), ("a", left_a), ("t", left_t)):
        links.arrived((name, "x"))
        links.send((name, "f"), target.at[:, spot_x], target.at[:, spot_x], "c")
        if name == "m":
            for b2 in (1, 0):
                scatter_second(links, "d", "lhx", grad_d, first_d, second_d, b2)
            for to in ("xc", "x", "c"):
                links.arrived(("u", to))
            links.arrived(("m", "c"))
            links.arrived(("m", "f"))
            for b0 in (1, 0):
                for b1, b2 in ORDER:
                    flips = "y" * b0 + "l" * b1 + "h" * b2
                    start = pl.multiple_of(place.h_at(flips) * BLOCK, BLOCK)
                    grad_u[b0, b1, b2] = jnp.dot(
                        left_m[pl.ds(start, BLOCK), :], right_u[...], preferred_element_type=F32
                    ).astype(BF16)
                    if b0:
                        scatter_first(links, "u", "ylh", grad_u, first_u, (b1, b2))
            scatter_third(links, "d", "lhx", grad_d, first_d, second_d, third_d)
    for to in ("xc", "x", "c"):
        links.arrived(("q", to))
    for name in ("a", "t"):
        links.arrived((name, "c"))
        links.arrived((name, "f"))
    lanes = lax.broadcasted_iota(jnp.int32, (BLOCK, 128), 1)
    for b0 in (1, 0):
        for b1, b2 in ORDER:
            flips = "y" * b0 + "l" * b1 + "h" * b2
            start = pl.multiple_of(place.h_at(flips) * BLOCK, BLOCK)
            qkv_part = jnp.dot(
                left_a[pl.ds(start, BLOCK), :], right_q[:, :896], preferred_element_type=F32
            )
            proj_part = jnp.dot(
                left_t[pl.ds(start, BLOCK), :], right_q[:, 768:], preferred_element_type=F32
            )
            grad_q[b0, b1, b2, :, :768] = qkv_part[:, :768].astype(BF16)
            grad_q[b0, b1, b2, :, 768:896] = jnp.where(
                lanes < 96, qkv_part[:, 768:], proj_part[:, :128]
            ).astype(BF16)
            grad_q[b0, b1, b2, :, 896:] = proj_part[:, 128:].astype(BF16)
            if b0:
                scatter_first(links, "q", "ylh", grad_q, first_q, (b1, b2))
        if b0:
            for b2 in (1, 0):
                scatter_second(links, "u", "ylh", grad_u, first_u, second_u, b2)
    scatter_last(links, "d", grad_d, first_d, second_d, third_d, out_down)
    scatter_third(links, "u", "ylh", grad_u, first_u, second_u, third_u)
    for b2 in (1, 0):
        scatter_second(links, "q", "ylh", grad_q, first_q, second_q, b2)
    scatter_last(links, "u", grad_u, first_u, second_u, third_u, out_up)
    scatter_third(links, "q", "ylh", grad_q, first_q, second_q, third_q)
    for to in FAR:
        links.arrived(("rows", to))
    out_rows[...] = row_all[...]
    scatter_last(links, "q", grad_q, first_q, second_q, third_q, out_qp)
    links.drain()


def trunk_grads(outer, *operands):
    grid_block = (2, 2, 2, BLOCK, 1152)
    vmem = pl.BlockSpec(memory_space=pltpu.VMEM)
    return pl.pallas_call(
        partial(trunk_kernel, outer),
        out_shape=[jax.ShapeDtypeStruct((BLOCK, 1152), F32)] * 3
        + [jax.ShapeDtypeStruct((INNER, 4, 48, 128), BF16)],
        in_specs=[pl.BlockSpec(memory_space=pl.ANY)] * 9,
        out_specs=[vmem] * 4,
        scratch_shapes=[pltpu.VMEM((1152, TOKENS), BF16)] * 3
        + [
            pltpu.VMEM((TOKENS, 2304), BF16),
            pltpu.VMEM((2, 288, TOKENS), BF16),
            pltpu.VMEM((TOKENS, 1152), BF16),
            pltpu.VMEM((TOKENS, 1152), BF16),
            pltpu.VMEM((4, 48, 128), BF16),
            pltpu.VMEM((INNER, 4, 48, 128), BF16),
        ]
        + [pltpu.VMEM(grid_block, BF16)] * 3
        + [pltpu.VMEM(grid_block[1:], BF16)] * 3
        + [pltpu.VMEM(grid_block[2:], BF16)] * 3
        + [pltpu.VMEM(grid_block[3:], BF16)] * 3
        + [
            pltpu.SemaphoreType.DMA((64,)),
            pltpu.SemaphoreType.DMA((64,)),
            pltpu.SemaphoreType.DMA((20,)),
        ],
        compiler_params=pltpu.CompilerParams(
            collective_id=0, has_side_effects=True, vmem_limit_bytes=52 * 2**20
        ),
    )(*operands)


def on_device(
    outer,
    hidden_in,
    conditioning,
    live_images,
    out_grad,
    ada_weight,
    ada_bias,
    qkv_weight,
    qv_bias,
    proj_weight,
    proj_bias,
    up_weight,
    up_bias,
    down_weight,
    down_bias,
):
    images = hidden_in.shape[0]
    cond_float = conditioning.astype(jnp.float32)
    cond_group = lax.all_gather(conditioning, "mp", axis=0, tiled=True)
    silu_rows = jax.nn.silu(cond_group.astype(jnp.float32)).astype(jnp.bfloat16)
    mod_cols = jnp.dot(silu_rows, ada_weight, preferred_element_type=jnp.float32) + ada_bias.astype(
        jnp.float32
    )
    modulation = lax.all_to_all(
        mod_cols.astype(jnp.bfloat16), "mp", split_axis=0, concat_axis=1, tiled=True
    )
    mod_float = modulation.astype(jnp.float32)[:, None, :]
    shift_a, scale_a, gate_a, shift_m, scale_m, gate_m = [
        mod_float[:, :, index * D : (index + 1) * D] for index in range(6)
    ]
    hidden = hidden_in.astype(jnp.float32)
    norm_a, inv_a = norm_rows(hidden)
    mod_a = (norm_a * (1.0 + scale_a) + shift_a).astype(jnp.bfloat16)
    qv_float = qv_bias.astype(jnp.float32)
    full_qkv_bias = jnp.concatenate([qv_float[:D], jnp.zeros((D,), jnp.float32), qv_float[D:]])
    qkv = (
        jnp.einsum("bld,de->ble", mod_a, qkv_weight, preferred_element_type=jnp.float32)
        + full_qkv_bias
    ).astype(jnp.bfloat16)
    queries = qkv[..., :D].reshape(images, SEQ, HEADS, HEAD_DIM)
    key_rows = qkv[..., D : 2 * D].reshape(images, SEQ, HEADS, HEAD_DIM)
    value_rows = qkv[..., 2 * D :].reshape(images, SEQ, HEADS, HEAD_DIM)
    scale_factor = HEAD_DIM ** (-0.5)

    def score_rows():
        return (
            jnp.einsum("bqhe,bkhe->bhqk", queries, key_rows, preferred_element_type=jnp.float32)
            * scale_factor
        )

    scores = score_rows()
    top_score = jnp.max(scores, axis=-1, keepdims=True)
    log_total = top_score + jnp.log(jnp.sum(jnp.exp(scores - top_score), axis=-1, keepdims=True))
    probs = jnp.exp(scores - log_total).astype(jnp.bfloat16)
    attended = jnp.einsum("bhqk,bkhe->bqhe", probs, value_rows, preferred_element_type=jnp.float32)
    attended = attended.reshape(images, SEQ, D).astype(jnp.bfloat16)
    attn_out = jnp.einsum(
        "bld,de->ble", attended, proj_weight, preferred_element_type=jnp.float32
    ) + proj_bias.astype(jnp.float32)
    after = hidden + gate_a * attn_out
    norm_m, inv_m = norm_rows(after)
    mod_m = (norm_m * (1.0 + scale_m) + shift_m).astype(jnp.bfloat16)
    pre_act = jnp.einsum(
        "bld,df->blf", mod_m, up_weight, preferred_element_type=jnp.float32
    ) + up_bias.astype(jnp.float32)
    act_rows = jax.nn.gelu(pre_act, approximate=True).astype(jnp.bfloat16)
    branch = jnp.einsum(
        "blf,fd->bld", act_rows, down_weight, preferred_element_type=jnp.float32
    ) + down_bias.astype(jnp.float32)
    mixed = (after + gate_m * branch).astype(jnp.bfloat16)
    cotangent = out_grad.astype(jnp.float32) * live_images.astype(jnp.float32)[:, None, None]
    g_branch = (cotangent * gate_m).astype(jnp.bfloat16)
    g_gate_m = jnp.sum(cotangent * branch, axis=1)
    grad_down_b = jnp.sum(g_branch.astype(jnp.float32), axis=(0, 1))
    g_act = jnp.einsum("bld,fd->blf", g_branch, down_weight, preferred_element_type=jnp.float32)
    gelu_value, gelu_back = jax.vjp(partial(jax.nn.gelu, approximate=True), pre_act)
    g_pre = gelu_back(g_act)[0].astype(jnp.bfloat16)
    grad_up_b = jnp.sum(g_pre.astype(jnp.float32), axis=(0, 1))
    g_mod_m = jnp.einsum("blf,df->bld", g_pre, up_weight, preferred_element_type=jnp.float32)
    g_shift_m = jnp.sum(g_mod_m, axis=1)
    g_scale_m = jnp.sum(g_mod_m * norm_m, axis=1)
    g_after = cotangent + norm_back(g_mod_m * (1.0 + scale_m), norm_m, inv_m)
    g_attn = (g_after * gate_a).astype(jnp.bfloat16)
    g_gate_a = jnp.sum(g_after * attn_out, axis=1)
    grad_proj_b = jnp.sum(g_attn.astype(jnp.float32), axis=(0, 1))
    g_attended = jnp.einsum("ble,de->bld", g_attn, proj_weight, preferred_element_type=jnp.float32)
    g_attended = g_attended.astype(jnp.bfloat16).reshape(images, SEQ, HEADS, HEAD_DIM)
    probs_again = jnp.exp(score_rows() - log_total)
    g_probs = jnp.einsum(
        "bqhe,bkhe->bhqk", g_attended, value_rows, preferred_element_type=jnp.float32
    )
    g_values = jnp.einsum(
        "bhqk,bqhe->bkhe",
        probs_again.astype(jnp.bfloat16),
        g_attended,
        preferred_element_type=jnp.float32,
    )
    row_dot = jnp.sum(probs_again * g_probs, axis=-1, keepdims=True)
    g_scores = (probs_again * (g_probs - row_dot)).astype(jnp.bfloat16)
    g_queries = (
        jnp.einsum("bhqk,bkhe->bqhe", g_scores, key_rows, preferred_element_type=jnp.float32)
        * scale_factor
    )
    g_keys = (
        jnp.einsum("bhqk,bqhe->bkhe", g_scores, queries, preferred_element_type=jnp.float32)
        * scale_factor
    )
    g_qkv = jnp.concatenate(
        [
            g_queries.reshape(images, SEQ, D),
            g_keys.reshape(images, SEQ, D),
            g_values.reshape(images, SEQ, D),
        ],
        axis=-1,
    ).astype(jnp.bfloat16)
    g_qkv_float = g_qkv.astype(jnp.float32)
    grad_qv_b = jnp.concatenate(
        [
            jnp.sum(g_qkv_float[..., :D], axis=(0, 1)),
            jnp.sum(g_qkv_float[..., 2 * D :], axis=(0, 1)),
        ]
    )
    g_mod_a = jnp.einsum("ble,de->bld", g_qkv, qkv_weight, preferred_element_type=jnp.float32)
    g_shift_a = jnp.sum(g_mod_a, axis=1)
    g_scale_a = jnp.sum(g_mod_a * norm_a, axis=1)
    grad_hidden = g_after + norm_back(g_mod_a * (1.0 + scale_a), norm_a, inv_a)
    g_modulation = jnp.concatenate(
        [g_shift_a, g_scale_a, g_gate_a, g_shift_m, g_scale_m, g_gate_m], axis=-1
    ).astype(jnp.bfloat16)
    mp_blocks = lambda row, width: row.reshape(4, width)
    row_cols = jnp.concatenate(
        [
            mp_blocks(g_modulation, 1728),
            mp_blocks(grad_qv_b.astype(BF16), 576),
            mp_blocks(grad_proj_b.astype(BF16), 288),
            mp_blocks(grad_up_b.astype(BF16), 1152),
            mp_blocks(grad_down_b.astype(BF16), 288),
            jnp.zeros((4, 64), BF16),
        ],
        axis=1,
    ).reshape(4, 32, 128)
    cond_rows = jnp.pad(silu_rows, ((0, 0), (0, 896))).reshape(4, 16, 128)
    act_half = act_rows.reshape(SEQ, 4, 2, 576).transpose(2, 0, 1, 3).reshape(2, SEQ, 2304)
    g_qp = jnp.concatenate(
        [g_qkv.reshape(SEQ, 4, 864), g_attn.reshape(SEQ, 4, 288)], axis=2
    ).transpose(1, 0, 2)
    down_pack, out_up_w, qp_pack, all_rows = trunk_grads(
        outer,
        mod_a[0].T,
        attended[0].T,
        mod_m[0].T,
        act_half,
        g_branch[0].T.reshape(4, 288, SEQ),
        g_pre.reshape(SEQ, 4, 1152).transpose(1, 0, 2),
        g_qp,
        row_cols,
        cond_rows,
    )
    out_down_w = jnp.concatenate([down_pack[:, :576], down_pack[:, 576:]], axis=0).T
    out_qkv_w, out_proj_w = qp_pack[:, :864], qp_pack[:, 864:]
    if outer > 1:
        groups = [[h * outer + low for low in range(outer)] for h in range(INNER)]
        out_down_w, out_up_w, out_qkv_w, out_proj_w = (
            lax.psum_scatter(
                part, "dp", scatter_dimension=0, tiled=True, axis_index_groups=groups
            )
            for part in (out_down_w, out_up_w, out_qkv_w, out_proj_w)
        )
        all_rows = lax.all_gather(all_rows, "dp", axis=0, tiled=True, axis_index_groups=groups)
    gathered = all_rows.reshape(4 * INNER * outer, 48 * 128)
    all_cols = gathered[:, :1728]
    all_silu = gathered[:, 4096 : 4096 + D]
    sums = jnp.sum(gathered[:, :4032].astype(F32), axis=0)
    rows_here = D // (INNER * outer)
    silu_here = lax.dynamic_slice_in_dim(
        all_silu, lax.axis_index("dp") * rows_here, rows_here, axis=1
    )
    out_ada_w = jnp.einsum("gd,gc->dc", silu_here, all_cols, preferred_element_type=F32)
    out_ada_b, out_qv_b, out_proj_b, out_up_b, out_down_b = (
        sums[:1728], sums[1728:2304], sums[2304:2592], sums[2592:3744], sums[3744:],
    )
    group_rows = lax.dynamic_slice_in_dim(
        gathered.reshape(-1, 4, 48 * 128),
        (lax.axis_index("dp") % outer) * INNER + lax.axis_index("dp") // outer,
        1,
        axis=0,
    )[0]
    cond_part = jnp.einsum(
        "gc,dc->gd", group_rows[:, :1728], ada_weight, preferred_element_type=F32
    )
    cond_sum = lax.psum_scatter(cond_part, "mp", scatter_dimension=0, tiled=True)
    silu_value, silu_back = jax.vjp(jax.nn.silu, cond_float)
    grad_cond = silu_back(cond_sum)[0]
    return (
        mixed,
        grad_hidden,
        grad_cond,
        out_ada_w,
        out_ada_b,
        out_qkv_w,
        out_qv_b,
        out_proj_w,
        out_proj_b,
        out_up_w,
        out_up_b,
        out_down_w,
        out_down_b,
    )


def solution(mesh):
    in_specs = (
        P(("dp", "mp"), None, None),
        P(("dp", "mp"), None),
        P(("dp", "mp")),
        P(("dp", "mp"), None, None),
        P(None, "mp"),
        P("mp"),
        P(),
        P(),
        P(),
        P(),
        P(),
        P(),
        P(),
        P(),
    )
    out_specs = (
        P(("dp", "mp"), None, None),
        P(("dp", "mp"), None, None),
        P(("dp", "mp"), None),
        P("dp", "mp"),
        P("mp"),
        P("dp", "mp"),
        P("mp"),
        P("dp", "mp"),
        P("mp"),
        P("dp", "mp"),
        P("mp"),
        P("dp", "mp"),
        P("mp"),
    )
    return jax.shard_map(
        partial(on_device, mesh.shape["dp"] // INNER), mesh=mesh, in_specs=in_specs, out_specs=out_specs, check_vma=False
    )
```

```python
from functools import partial

import jax
import jax.numpy as jnp
from jax import lax
from jax.experimental import pallas as pl
from jax.experimental.pallas import tpu as pltpu
from jax.sharding import PartitionSpec as P

D = 1152
HEADS = 16
HEAD_DIM = 72
FF = 4608
SEQ = 256
ADA = 1728
MESH_ID = pl.DeviceIdType.MESH
BF16 = jnp.bfloat16
F32 = jnp.float32
INNER = 8
BLOCK = D // INNER
GROUP = 4
TOKENS = GROUP * SEQ
WINDOW = 640
SLOTS = 3
ROWS = 4096
SCALE = HEAD_DIM ** (-0.5)
PEERS = ("c", "x", "xc", "y", "yc", "l", "h", "yl", "yh", "lh", "ylh")
FAR = ("y", "l", "h", "yl", "yh", "lh", "ylh")
NEAR = ("xc", "x", "c")
ORDER = ((1, 1), (1, 0), (0, 1), (0, 0))


def dot(left, right):
    return jnp.dot(left, right, preferred_element_type=F32)


def dot_rows(left, right):
    return lax.dot_general(left, right, (((1,), (1,)), ((), ())), preferred_element_type=F32)


def norm_rows(values):
    center = values - jnp.mean(values, axis=-1, keepdims=True)
    inverse = lax.rsqrt(jnp.mean(center * center, axis=-1, keepdims=True) + 1e-06)
    return center * inverse, inverse


def norm_back(grad_normed, normed, inverse):
    mean_grad = jnp.mean(grad_normed, axis=-1, keepdims=True)
    mean_prod = jnp.mean(grad_normed * normed, axis=-1, keepdims=True)
    return inverse * (grad_normed - mean_grad - normed * mean_prod)


def sum_rows(values):
    return jnp.sum(values, axis=0, keepdims=True)


class Place:
    def __init__(self, outer):
        data, model = lax.axis_index("dp"), lax.axis_index("mp")
        self.outer = outer
        self.low = data % outer
        self.h_index = data // outer
        self.m_index = model
        self.bits = {
            "h": self.h_index // 4,
            "l": (self.h_index // 2) % 2,
            "y": self.h_index % 2,
            "x": model // 2,
            "c": model % 2,
        }

    def flipped(self, names):
        return {key: (1 - bit if key in names else bit) for key, bit in self.bits.items()}

    def h_at(self, names):
        bits = self.flipped(names)
        return bits["h"] * 4 + bits["l"] * 2 + bits["y"]

    def m_at(self, names):
        bits = self.flipped(names)
        return bits["x"] * 2 + bits["c"]

    def yc_at(self, names):
        bits = self.flipped(names)
        return bits["y"] * 2 + bits["c"]

    def device(self, names):
        return (self.h_at(names) * self.outer + self.low, self.m_at(names))


class Links:
    def __init__(self, place, send_sems, recv_sems):
        self.place = place
        self.send_sems = send_sems
        self.recv_sems = recv_sems
        self.builders = {}
        self.gone = set()

    def send(self, name, to, ends):
        index = len(self.builders)

        def build(landed=False):
            source, target = ends()
            if landed:
                source = target
            return pltpu.make_async_remote_copy(
                src_ref=source,
                dst_ref=target,
                send_sem=self.send_sems.at[index],
                recv_sem=self.recv_sems.at[index],
                device_id=self.place.device(to),
                device_id_type=MESH_ID,
            )

        self.builders[name] = build
        build().start()

    def arrived(self, name):
        self.builders[name](landed=True).wait_recv()

    def left(self, name):
        self.gone.add(name)
        self.builders[name]().wait_send()

    def drain(self):
        for name in self.builders:
            if name not in self.gone:
                self.left(name)


class Ring:
    def __init__(self, parts, slots, sems):
        self.parts = parts
        self.slots = slots
        self.sems = sems
        for index in range(SLOTS):
            self.start(index)

    def copy(self, index):
        slot = index % SLOTS
        return pltpu.make_async_copy(self.parts[index], self.slots.at[slot], self.sems.at[slot])

    def start(self, index):
        if index < len(self.parts):
            self.copy(index).start()

    def get(self, index):
        self.copy(index).wait()
        return self.slots.at[index % SLOTS]

    def done(self, index):
        self.start(index + SLOTS)


class Scatter:
    def __init__(self, links, name, axes, grad, first, second, third):
        self.links, self.name, self.axes = links, name, axes
        self.grad, self.first, self.second, self.third = grad, first, second, third

    def send_first(self, pair):
        b1, b2 = pair
        self.links.send(
            (self.name, 0, b1, b2),
            self.axes[0],
            lambda: (self.grad.at[1, b1, b2], self.first.at[b1, b2]),
        )

    def send_second(self, b2):
        self.links.arrived((self.name, 0, 1, b2))
        self.grad[0, 1, b2] = (
            self.grad[0, 1, b2].astype(F32) + self.first[1, b2].astype(F32)
        ).astype(BF16)
        self.links.send(
            (self.name, 1, b2), self.axes[1], lambda: (self.grad.at[0, 1, b2], self.second.at[b2])
        )

    def send_third(self):
        self.links.arrived((self.name, 0, 0, 1))
        self.links.arrived((self.name, 1, 1))
        self.grad[0, 0, 1] = (
            self.grad[0, 0, 1].astype(F32)
            + self.first[0, 1].astype(F32)
            + self.second[1].astype(F32)
        ).astype(BF16)
        self.links.send((self.name, 2), self.axes[2], lambda: (self.grad.at[0, 0, 1], self.third))

    def finish(self, out):
        self.links.arrived((self.name, 0, 0, 0))
        self.links.arrived((self.name, 1, 0))
        self.links.arrived((self.name, 2))
        out[...] = (
            self.grad[0, 0, 0].astype(F32)
            + self.first[0, 0].astype(F32)
            + self.second[0].astype(F32)
            + self.third[...].astype(F32)
        )


def head_window(head):
    start = (head * 9) // 16 - head // 15
    offset = head * HEAD_DIM - start * 128
    lanes = lax.broadcasted_iota(jnp.int32, (SEQ, 256), 1)
    inside = (lanes >= offset) & (lanes < offset + HEAD_DIM)
    return pl.ds(pl.multiple_of(start * 128, 128), 256), inside


def head_probs(qkv, window, inside):
    queries = jnp.where(inside, qkv[0, :, window], 0)
    scores = dot_rows(queries, qkv[1, :, window]) * SCALE
    shifted = jnp.exp(scores - jnp.max(scores, axis=-1, keepdims=True))
    return queries, shifted * (1.0 / jnp.sum(shifted, axis=-1, keepdims=True))


def block_kernel(
    outer,
    hidden,
    cond,
    live,
    out_grad,
    biases,
    ada_w,
    qkv_w,
    proj_w,
    up_w,
    down_w,
    mixed,
    grad_hidden,
    grad_cond,
    out_ada,
    out_sums,
    out_down,
    out_up,
    out_qp,
    ring_slots,
    cond_rows,
    mod_out,
    mod_in,
    mods,
    left_a,
    left_t,
    left_m,
    right_act,
    left_b,
    right_u,
    right_q,
    gb_t,
    g_branch,
    natural,
    qkv,
    attn_out,
    sums,
    row_stage,
    row_group,
    row_all,
    cond_stage,
    cond_in,
    grad_d,
    grad_u,
    first_d,
    first_u,
    first_q,
    second_d,
    second_u,
    second_q,
    third_d,
    third_u,
    third_q,
    send_sems,
    recv_sems,
    ring_sems,
    ada_sem,
):
    place = Place(outer)
    bits = place.bits
    m_here = place.m_index
    links = Links(place, send_sems, recv_sems)

    def spot(index):
        return pl.ds(pl.multiple_of(index * SEQ, SEQ), SEQ)

    here, here_yc = spot(m_here), spot(place.yc_at(""))
    ff_order = [place.m_at(to) for to in NEAR] + [m_here]

    def ff_part(index):
        return pl.ds(pl.multiple_of(index * D, D), D)

    qkv_parts = [qkv_w.at[:, pl.ds(index * D, D)] for index in range(3)]
    ff_parts = []
    for index in ff_order:
        ff_parts += [up_w.at[:, ff_part(index)], down_w.at[ff_part(index), :]]
    barrier = pltpu.get_barrier_semaphore()
    for names in PEERS:
        pl.semaphore_signal(
            barrier, inc=1, device_id=place.device(names), device_id_type=MESH_ID
        )
    ring = Ring(qkv_parts + [proj_w] + ff_parts + [proj_w] + qkv_parts, ring_slots, ring_sems)
    row_tiles = [pl.ds(start, 64) for start in range(0, SEQ, 64)]

    def bias(start, width=D):
        return biases[:, pl.ds(start, width)]

    def modulation(ada):
        load = pltpu.make_async_copy(ada_w, ada, ada_sem)
        load.start()
        silu_row = jax.nn.silu(cond[...].astype(F32))
        cond_rows[m_here] = jnp.broadcast_to(silu_row, (16, D)).astype(BF16)
        pl.semaphore_wait(barrier, len(PEERS))
        for to in NEAR:
            links.send(("cond", to), to, lambda: (cond_rows.at[m_here], cond_rows.at[m_here]))
        for rows in row_tiles:
            grad_hidden[rows, :] = norm_rows(hidden[0, rows, :].astype(F32))[0]
        load.wait()
        for to in NEAR:
            links.arrived(("cond", to))
        columns = dot(cond_rows[...].reshape(64, D), ada[...]) + bias(9 * D, ADA)
        mod_out[:, :, :ADA] = columns.astype(BF16).reshape(GROUP, 16, ADA)
        for to in NEAR:
            links.send(
                ("mod", to), to, lambda to=to: (mod_out.at[place.m_at(to)], mod_in.at[m_here])
            )
        mod_in[m_here] = mod_out[m_here]

    pl.run_scoped(modulation, pltpu.VMEM((D, ADA), BF16))
    for to in NEAR:
        links.arrived(("mod", to))
    parts = [mod_in[index].astype(F32)[:1] for index in range(GROUP)]
    for index in range(2):
        low, high = parts[2 * index], parts[2 * index + 1]
        mods[3 * index : 3 * index + 1] = low[:, :D]
        mods[3 * index + 1 : 3 * index + 2] = jnp.concatenate(
            [low[:, D:ADA], high[:, : D // 2]], axis=1
        )
        mods[3 * index + 2 : 3 * index + 3] = high[:, D // 2 : ADA]
    shift_a, scale_a, gate_a, shift_m, scale_m, gate_m = range(6)

    def mod(index):
        return mods[index : index + 1]

    live_factor = live[0, 0]
    for rows in row_tiles:
        natural[rows, :] = (
            grad_hidden[rows, :] * (1.0 + mod(scale_a)) + mod(shift_a)
        ).astype(BF16)
        g_branch[rows, :] = (
            out_grad[0, rows, :].astype(F32) * live_factor * mod(gate_m)
        ).astype(BF16)
    left_a[:, here] = natural[...].T
    for to in ("x", "c"):
        links.send(("a", to), to, lambda: (left_a.at[:, here], left_a.at[:, here]))
    gb_t[...] = g_branch[...].T

    def gb_rows(to, x):
        return pl.ds(pl.multiple_of((2 * x + place.flipped(to)["c"]) * 288, 288), 288)

    for to in ("y", "yc", "c"):
        for x in range(2):
            links.send(
                ("gb", to, x),
                to,
                lambda to=to, x=x: (gb_t.at[gb_rows(to, x), :], left_b.at[x, :, here_yc]),
            )
    for x in range(2):
        left_b[x, :, here_yc] = gb_t[gb_rows("", x), :]
    sums[9:10] = sum_rows(g_branch[...].astype(F32))

    for index in range(3):
        part = ring.get(index)
        qkv[index] = (dot(natural[...], part[...]) + bias(index * D)).astype(BF16)
        ring.done(index)

    def attend(head, carry):
        window, inside = head_window(head)
        _, probs = head_probs(qkv, window, inside)
        mixed_values = dot(probs.astype(BF16), qkv[2, :, window]).astype(BF16)
        natural[:, window] = jnp.where(inside, mixed_values, natural[:, window])
        return carry

    lax.fori_loop(0, HEADS, attend, 0, unroll=UNROLL)
    left_t[:, here] = natural[...].T
    for to in ("x", "c"):
        links.send(("t", to), to, lambda: (left_t.at[:, here], left_t.at[:, here]))
    part = ring.get(3)
    attn_out[...] = dot(natural[...], part[...]) + bias(3 * D)
    ring.done(3)

    def act_lanes(to):
        return pl.ds(pl.multiple_of(place.flipped(to)["y"] * 512, 512), WINDOW)

    def feed_forward(after, branch, g_mod, act_stage, pre_stage):
        slope = grad_hidden
        for rows in row_tiles:
            after[rows, :] = hidden[0, rows, :].astype(F32) + mod(gate_a) * attn_out[rows, :]
            normed, _ = norm_rows(after[rows, :])
            natural[rows, :] = (normed * (1.0 + mod(scale_m)) + mod(shift_m)).astype(BF16)
        left_m[:, here] = natural[...].T
        for to in ("x", "c"):
            links.send(("m", to), to, lambda: (left_m.at[:, here], left_m.at[:, here]))
        for step in range(4):
            index = ff_order[step]
            up, down = ring.get(4 + 2 * step), ring.get(5 + 2 * step)
            for tile in range(3):
                lanes = pl.ds(tile * 384, 384)
                offset = pl.multiple_of(4 * D + index * D + tile * 384, 128)
                pre = dot(natural[...], up[:, lanes]) + biases[:, pl.ds(offset, 384)]
                square = pre * pre
                slant = jnp.tanh(0.7978845608028654 * pre * (1.0 + 0.044715 * square))
                half = 0.5 * (1.0 + slant)
                act_stage[step, :, lanes] = (pre * half).astype(BF16)
                slope[:, lanes] = half + 0.5 * pre * (1.0 - slant * slant) * (
                    0.7978845608028654 * (1.0 + 0.134145 * square)
                )
            for to in ("y", "c"):
                links.send(
                    ("act", to, step),
                    to,
                    lambda to=to, step=step: (
                        act_stage.at[step, :, act_lanes(to)],
                        right_act.at[ff_order[step], here_yc],
                    ),
                )
            right_act[index, here_yc] = act_stage[step, :, act_lanes("")]
            for tile in range(3):
                lanes = pl.ds(tile * 384, 384)
                g_pre = (dot_rows(g_branch[...], down[lanes, :]) * slope[:, lanes]).astype(BF16)
                sums[pl.ds(10 + index, 1), lanes] = sum_rows(g_pre.astype(F32))
                if step < 3:
                    pre_stage[step, :, lanes] = g_pre
                else:
                    right_u[here, lanes] = g_pre
            if step < 3:
                g_pre_ref = pre_stage.at[step]
                links.send(
                    ("u", NEAR[step]),
                    NEAR[step],
                    lambda step=step: (pre_stage.at[step], right_u.at[here]),
                )
            else:
                g_pre_ref = right_u.at[here]
            new_mod = dot_rows(g_pre_ref[...], up[...])
            g_mod[...] = new_mod + g_mod[...] if step else new_mod
            ring.done(4 + 2 * step)
            new_branch = dot(act_stage[step], down[...])
            branch[...] = new_branch + (branch[...] if step else bias(8 * D))
            ring.done(5 + 2 * step)
            if step == 2:
                forward("a")
        zero = jnp.zeros((1, D), F32)
        gate_m_sum = scale_m_sum = shift_m_sum = gate_a_sum = proj_sum = zero
        for rows in row_tiles:
            cotangent = out_grad[0, rows, :].astype(F32) * live_factor
            mixed[rows, :] = (after[rows, :] + mod(gate_m) * branch[rows, :]).astype(BF16)
            gate_m_sum += sum_rows(cotangent * branch[rows, :])
            normed, inverse = norm_rows(after[rows, :])
            grads = g_mod[rows, :]
            shift_m_sum += sum_rows(grads)
            scale_m_sum += sum_rows(grads * normed)
            g_after = cotangent + norm_back(grads * (1.0 + mod(scale_m)), normed, inverse)
            grad_hidden[rows, :] = g_after
            gate_a_sum += sum_rows(g_after * attn_out[rows, :])
            g_attn = (g_after * mod(gate_a)).astype(BF16)
            natural[rows, :] = g_attn
            proj_sum += sum_rows(g_attn.astype(F32))
        sums[2:3] = gate_a_sum
        sums[3:4] = shift_m_sum
        sums[4:5] = scale_m_sum
        sums[5:6] = gate_m_sum
        sums[8:9] = proj_sum
        forward("t")
        forward("m")
        for step in range(4):
            forward_act(step)
        for step in range(4):
            for to in ("y", "c"):
                links.left(("act", to, step))
        for to in NEAR:
            links.left(("u", to))

    spot_x, spot_y = spot(place.m_at("x")), spot(place.yc_at("y"))

    def forward(name):
        target = {"a": left_a, "t": left_t, "m": left_m}[name]
        links.arrived((name, "x"))
        links.send((name, "f"), "c", lambda: (target.at[:, spot_x], target.at[:, spot_x]))

    def forward_act(step):
        def target():
            return right_act.at[ff_order[step], spot_y]

        links.arrived(("act", "y", step))
        links.send(("act", "f", step), "c", lambda: (target(), target()))

    f32_rows = pltpu.VMEM((SEQ, D), F32)
    pl.run_scoped(
        feed_forward,
        f32_rows,
        f32_rows,
        f32_rows,
        pltpu.VMEM((4, SEQ, D), BF16),
        pltpu.VMEM((3, SEQ, D), BF16),
    )

    scatter_d = Scatter(links, "d", "lhx", grad_d, first_d, second_d, third_d)
    scatter_u = Scatter(links, "u", "ylh", grad_u, first_u, second_u, third_u)

    def form_down():
        for to in ("y", "c", "yc"):
            for x in range(2):
                links.arrived(("gb", to, x))
        for step in range(4):
            links.arrived(("act", "c", step))
            links.arrived(("act", "f", step))
        for b0 in (1, 0):
            for b1, b2 in ORDER:
                flips = "l" * b0 + "h" * b1 + "x" * b2
                there = place.flipped(flips)
                wide = dot(left_b[there["x"]], right_act[there["h"] * 2 + there["l"]])
                block = jnp.where(bits["y"] == 0, wide[:, :576], wide[:, 64:]).astype(BF16)
                grad_d[b0, b1, b2] = jnp.concatenate([block[:BLOCK], block[BLOCK:]], axis=1)
                if b0:
                    scatter_d.send_first((b1, b2))

    def grad_rows(flips):
        return pl.ds(pl.multiple_of(place.h_at(flips) * BLOCK, BLOCK), BLOCK)

    def form_up():
        for to in NEAR:
            links.arrived(("u", to))
        links.arrived(("m", "c"))
        links.arrived(("m", "f"))
        for b0 in (1, 0):
            for b1, b2 in ORDER:
                rows = grad_rows("y" * b0 + "l" * b1 + "h" * b2)
                grad_u[b0, b1, b2] = dot(left_m[rows, :], right_u[...]).astype(BF16)
                if b0:
                    scatter_u.send_first((b1, b2))

    def attention_back(g_qkv, q_stage):
        part = ring.get(12)
        g_att = q_stage.at[0]
        g_att[...] = dot_rows(natural[...], part[...]).astype(BF16)
        ring.done(12)

        def back(head, carry):
            window, inside = head_window(head)
            queries, probs = head_probs(qkv, window, inside)
            grads = jnp.where(inside, g_att[:, window], 0)
            g_probs = dot_rows(grads, qkv[2, :, window])
            g_values = dot(probs.astype(BF16).T, grads).astype(BF16)
            row_dot = jnp.sum(probs * g_probs, axis=-1, keepdims=True)
            g_scores = (probs * (g_probs - row_dot)).astype(BF16)
            g_queries = (dot(g_scores, qkv[1, :, window]) * SCALE).astype(BF16)
            g_keys = (dot(g_scores.T, queries) * SCALE).astype(BF16)
            for index, value in enumerate((g_queries, g_keys, g_values)):
                g_qkv[index, :, window] = jnp.where(inside, value, g_qkv[index, :, window])
            return carry

        lax.fori_loop(0, HEADS, back, 0, unroll=UNROLL)
        sums[6:7] = sum_rows(g_qkv[0].astype(F32))
        sums[7:8] = sum_rows(g_qkv[2].astype(F32))
        for index in range(GROUP):
            start, pieces = index * 864, []
            while start < index * 864 + 864:
                stop = min(index * 864 + 864, (start // D + 1) * D)
                pieces.append(g_qkv[start // D][:, start % D : start % D + stop - start])
                start = stop
            pieces.append(natural[...][:, index * 288 : index * 288 + 288])
            q_stage[index] = jnp.concatenate(pieces, axis=1)
        for to in NEAR:
            links.send(
                ("q", to), to, lambda to=to: (q_stage.at[place.m_at(to)], right_q.at[here])
            )
        right_q[here, :] = q_stage[m_here]
        form_down()

        for index in range(3):
            part = ring.get(13 + index)
            product = dot_rows(g_qkv[index], part[...])
            attn_out[...] = attn_out[...] + product if index else product
        zero = jnp.zeros((1, D), F32)
        shift_sum = scale_sum = zero
        for rows in row_tiles:
            normed, inverse = norm_rows(hidden[0, rows, :].astype(F32))
            grads = attn_out[rows, :]
            shift_sum += sum_rows(grads)
            scale_sum += sum_rows(grads * normed)
            grad_hidden[rows, :] = grad_hidden[rows, :] + norm_back(
                grads * (1.0 + mod(scale_a)), normed, inverse
            )
        sums[0:1] = shift_sum
        sums[1:2] = scale_sum
        send_rows()
        for to in NEAR:
            links.left(("q", to))

    def reduce_rest(grad_q, ada, spread, cond_all):
        scatter_q = Scatter(links, "q", "ylh", grad_q, first_q, second_q, third_q)
        load = pltpu.make_async_copy(ada_w, ada, ada_sem)
        load.start()
        form_up()
        for b2 in (1, 0):
            scatter_d.send_second(b2)
        ada_grads(load, ada, spread, cond_all)
        scatter_d.send_third()
        for to in NEAR:
            links.arrived(("q", to))
        for name in ("a", "t"):
            links.arrived((name, "c"))
            links.arrived((name, "f"))
        lanes = lax.broadcasted_iota(jnp.int32, (BLOCK, 128), 1)
        for b0 in (1, 0):
            for b1, b2 in ORDER:
                rows = grad_rows("y" * b0 + "l" * b1 + "h" * b2)
                qkv_part = dot(left_a[rows, :], right_q[:, :896])
                proj_part = dot(left_t[rows, :], right_q[:, 768:])
                grad_q[b0, b1, b2, :, :768] = qkv_part[:, :768].astype(BF16)
                grad_q[b0, b1, b2, :, 768:896] = jnp.where(
                    lanes < 96, qkv_part[:, 768:], proj_part[:, :128]
                ).astype(BF16)
                grad_q[b0, b1, b2, :, 896:] = proj_part[:, 128:].astype(BF16)
                if b0:
                    scatter_q.send_first((b1, b2))
            if b0:
                for b2 in (1, 0):
                    scatter_u.send_second(b2)
        scatter_d.finish(out_down)
        scatter_u.send_third()
        for b2 in (1, 0):
            scatter_q.send_second(b2)
        scatter_u.finish(out_up)
        scatter_q.send_third()
        scatter_q.finish(out_qp)
        links.drain()

    def send_rows():
        grads = jnp.concatenate([sums[index : index + 1] for index in range(6)], axis=1)
        qv = jnp.concatenate([sums[6:7], sums[7:8]], axis=1)
        for index in range(GROUP):
            row = jnp.concatenate(
                [
                    grads[:, ADA * index : ADA * index + ADA],
                    qv[:, 576 * index : 576 * index + 576],
                    sums[8:9][:, 288 * index : 288 * index + 288],
                    sums[10 + index : 11 + index],
                    sums[9:10][:, 288 * index : 288 * index + 288],
                    jnp.zeros((1, 64), F32),
                ],
                axis=1,
            )
            row_stage[index] = jnp.concatenate(
                [row[:, 128 * tile : 128 * tile + 128] for tile in range(32)], axis=0
            ).astype(BF16)
            silu_row = cond_rows[index].astype(F32)[:1]
            row_group[index, 32:48] = jnp.concatenate(
                [silu_row[:, 128 * tile : 128 * tile + 128] for tile in range(9)]
                + [jnp.zeros((7, 128), F32)],
                axis=0,
            ).astype(BF16)
        for to in NEAR:
            links.send(
                ("row", to),
                to,
                lambda to=to: (row_stage.at[place.m_at(to)], row_group.at[m_here, pl.ds(0, 32)]),
            )
        row_group[m_here, 0:32] = row_stage[m_here]
        for to in NEAR:
            links.arrived(("row", to))
        row_all[place.h_index] = row_group[...]
        for to in FAR:
            links.send(("rows", to), to, lambda: (row_group, row_all.at[place.h_index]))

    def ada_grads(load, ada, spread, cond_all):
        for to in FAR:
            links.arrived(("rows", to))
        images = GROUP * INNER
        spread[...] = row_all[...].astype(F32).reshape(images * 48, 128)

        def tile(index):
            return spread[pl.ds(index, images, stride=48), :]

        columns = jnp.concatenate([tile(index) for index in range(14)], axis=1)[:, :ADA]
        columns = columns.astype(BF16)
        for index in range(32):
            out_sums[:, 128 * index : 128 * index + 128] = sum_rows(tile(index))
        for to in ("y", "yc", "c"):
            for x in range(2):
                links.left(("gb", to, x))
        silu_all = jnp.concatenate([tile(32 + index) for index in range(9)], axis=1)
        gb_t[:, :images] = silu_all.T.astype(BF16)
        rows = pl.ds(pl.multiple_of(place.h_index * BLOCK, BLOCK), BLOCK)
        out_ada[...] = dot(gb_t[rows, :images], columns)
        load.wait()
        cond_all[...] = dot_rows(columns, ada[...])
        for to in NEAR:
            row = place.h_index * GROUP + place.m_at(to)
            cond_stage[place.m_at(to)] = jnp.broadcast_to(cond_all[pl.ds(row, 1), :], (8, D))
            links.send(
                ("gc", to), to, lambda to=to: (cond_stage.at[place.m_at(to)], cond_in.at[m_here])
            )
        total = cond_all[pl.ds(place.h_index * GROUP + m_here, 1), :]
        for to in NEAR:
            links.arrived(("gc", to))
            total += cond_in[place.m_at(to)][:1]
        values = cond[...].astype(F32)
        sigmoid = jax.nn.sigmoid(values)
        grad_cond[...] = total * (sigmoid * (1.0 + values * (1.0 - sigmoid)))

    pl.run_scoped(
        attention_back, pltpu.VMEM((3, SEQ, D), BF16), pltpu.VMEM((GROUP, SEQ, D), BF16)
    )
    pl.run_scoped(
        reduce_rest,
        pltpu.VMEM((2, 2, 2, BLOCK, D), BF16),
        pltpu.VMEM((D, ADA), BF16),
        pltpu.VMEM((GROUP * INNER * 48, 128), F32),
        pltpu.VMEM((GROUP * INNER, D), F32),
    )


UNROLL = 2


def run_block(outer, *operands):
    vmem = pl.BlockSpec(memory_space=pltpu.VMEM)
    anywhere = pl.BlockSpec(memory_space=pl.ANY)
    smem = pl.BlockSpec(memory_space=pltpu.SMEM)
    grid_block = (2, 2, 2, BLOCK, D)
    scratch = [
        ((SLOTS, D, D), BF16),
        ((GROUP, 16, D), BF16),
        ((GROUP, 16, 1792), BF16),
        ((GROUP, 16, 1792), BF16),
        ((8, D), F32),
        ((D, TOKENS), BF16),
        ((D, TOKENS), BF16),
        ((D, TOKENS), BF16),
        ((4, TOKENS, WINDOW), BF16),
        ((2, 288, TOKENS), BF16),
        ((TOKENS, D), BF16),
        ((TOKENS, D), BF16),
        ((D, SEQ), BF16),
        ((SEQ, D), BF16),
        ((SEQ, D), BF16),
        ((3, SEQ, D), BF16),
        ((SEQ, D), F32),
        ((16, D), F32),
        ((GROUP, 32, 128), BF16),
        ((GROUP, 48, 128), BF16),
        ((INNER, GROUP, 48, 128), BF16),
        ((GROUP, 8, D), F32),
        ((GROUP, 8, D), F32),
    ]
    scratch += [(grid_block, BF16)] * 2
    scratch += [(grid_block[1:], BF16)] * 3
    scratch += [(grid_block[2:], BF16)] * 3
    scratch += [(grid_block[3:], BF16)] * 3
    outs = [
        ((SEQ, D), BF16),
        ((SEQ, D), F32),
        ((1, D), F32),
        ((BLOCK, ADA), F32),
        ((1, ROWS), F32),
        ((BLOCK, D), F32),
        ((BLOCK, D), F32),
        ((BLOCK, D), F32),
    ]
    return pl.pallas_call(
        partial(block_kernel, outer),
        out_shape=[jax.ShapeDtypeStruct(*out) for out in outs],
        in_specs=[vmem, vmem, smem, vmem, vmem] + [anywhere] * 5,
        out_specs=[vmem] * len(outs),
        scratch_shapes=[pltpu.VMEM(*each) for each in scratch]
        + [
            pltpu.SemaphoreType.DMA((96,)),
            pltpu.SemaphoreType.DMA((96,)),
            pltpu.SemaphoreType.DMA((SLOTS,)),
            pltpu.SemaphoreType.DMA,
        ],
        compiler_params=pltpu.CompilerParams(
            collective_id=0, has_side_effects=True, vmem_limit_bytes=63 * 2**20 + 900 * 2**10
        ),
    )(*operands)


def on_device(
    outer,
    hidden_in,
    conditioning,
    live_images,
    out_grad,
    ada_weight,
    ada_bias,
    qkv_weight,
    qv_bias,
    proj_weight,
    proj_bias,
    up_weight,
    up_bias,
    down_weight,
    down_bias,
):
    biases = jnp.concatenate(
        [qv_bias[:D], jnp.zeros((D,), BF16), qv_bias[D:], proj_bias, up_bias, down_bias, ada_bias]
    )
    (
        mixed,
        grad_hidden,
        grad_cond,
        out_ada_w,
        sums,
        down_pack,
        out_up_w,
        qp_pack,
    ) = run_block(
        outer,
        hidden_in,
        conditioning,
        live_images.astype(F32).reshape(1, 1),
        out_grad,
        biases.astype(F32).reshape(1, -1),
        ada_weight,
        qkv_weight,
        proj_weight,
        up_weight,
        down_weight,
    )
    out_down_w = jnp.concatenate([down_pack[:, :576], down_pack[:, 576:]], axis=0).T
    out_qkv_w, out_proj_w = qp_pack[:, :864], qp_pack[:, 864:]
    if outer > 1:
        groups = [[h * outer + low for low in range(outer)] for h in range(INNER)]
        out_ada_w, out_down_w, out_up_w, out_qkv_w, out_proj_w = (
            lax.psum_scatter(
                part, "dp", scatter_dimension=0, tiled=True, axis_index_groups=groups
            )
            for part in (out_ada_w, out_down_w, out_up_w, out_qkv_w, out_proj_w)
        )
        sums = jnp.sum(
            lax.all_gather(sums, "dp", axis=0, tiled=True, axis_index_groups=groups),
            axis=0,
            keepdims=True,
        )
    sums = sums[0]
    return (
        mixed[None],
        grad_hidden[None],
        grad_cond,
        out_ada_w,
        sums[:1728],
        out_qkv_w,
        sums[1728:2304],
        out_proj_w,
        sums[2304:2592],
        out_up_w,
        sums[2592:3744],
        out_down_w,
        sums[3744:4032],
    )


def solution(mesh):
    in_specs = (
        P(("dp", "mp"), None, None),
        P(("dp", "mp"), None),
        P(("dp", "mp")),
        P(("dp", "mp"), None, None),
        P(None, "mp"),
        P("mp"),
        P(),
        P(),
        P(),
        P(),
        P(),
        P(),
        P(),
        P(),
    )
    out_specs = (
        P(("dp", "mp"), None, None),
        P(("dp", "mp"), None, None),
        P(("dp", "mp"), None),
        P("dp", "mp"),
        P("mp"),
        P("dp", "mp"),
        P("mp"),
        P("dp", "mp"),
        P("mp"),
        P("dp", "mp"),
        P("mp"),
        P("dp", "mp"),
        P("mp"),
    )
    return jax.shard_map(
        partial(on_device, mesh.shape["dp"] // INNER),
        mesh=mesh,
        in_specs=in_specs,
        out_specs=out_specs,
        check_vma=False,
    )
```

```python
from functools import partial

import jax
import jax.numpy as jnp
from jax import lax
from jax.experimental import pallas as pl
from jax.experimental.pallas import tpu as pltpu
from jax.sharding import PartitionSpec as P

D = 1152
HEADS = 16
HEAD_DIM = 72
FF = 4608
SEQ = 256
ADA = 1728
MESH_ID = pl.DeviceIdType.MESH
BF16 = jnp.bfloat16
F32 = jnp.float32
INNER = 8
BLOCK = D // INNER
GROUP = 4
TOKENS = GROUP * SEQ
WINDOW = 640
SLOTS = 3
SCALE = HEAD_DIM ** (-0.5)
PEERS = ("c", "x", "xc", "y", "yc", "l", "lc", "h", "yl", "yh", "lh", "ylh")
FAR = ("y", "l", "h", "yl", "yh", "lh", "ylh")
NEAR = ("xc", "x", "c")
ORDER = ((1, 1), (1, 0), (0, 1), (0, 0))


def dot(left, right):
    return jnp.dot(left, right, preferred_element_type=F32)


def dot_rows(left, right):
    return lax.dot_general(left, right, (((1,), (1,)), ((), ())), preferred_element_type=F32)


def norm_rows(values):
    center = values - jnp.mean(values, axis=-1, keepdims=True)
    inverse = lax.rsqrt(jnp.mean(center * center, axis=-1, keepdims=True) + 1e-06)
    return center * inverse, inverse


def norm_back(grad_normed, normed, inverse):
    mean_grad = jnp.mean(grad_normed, axis=-1, keepdims=True)
    mean_prod = jnp.mean(grad_normed * normed, axis=-1, keepdims=True)
    return inverse * (grad_normed - mean_grad - normed * mean_prod)


def sum_rows(values):
    return jnp.sum(values, axis=0, keepdims=True)


class Place:
    def __init__(self, outer):
        data, model = lax.axis_index("dp"), lax.axis_index("mp")
        self.outer = outer
        self.low = data % outer
        self.h_index = data // outer
        self.m_index = model
        self.bits = {
            "h": self.h_index // 4,
            "l": (self.h_index // 2) % 2,
            "y": self.h_index % 2,
            "x": model // 2,
            "c": model % 2,
        }

    def flipped(self, names):
        return {key: (1 - bit if key in names else bit) for key, bit in self.bits.items()}

    def h_at(self, names):
        bits = self.flipped(names)
        return bits["h"] * 4 + bits["l"] * 2 + bits["y"]

    def m_at(self, names):
        bits = self.flipped(names)
        return bits["x"] * 2 + bits["c"]

    def pair_at(self, axis, names):
        bits = self.flipped(names)
        return bits[axis] * 2 + bits["c"]

    def device(self, names):
        return (self.h_at(names) * self.outer + self.low, self.m_at(names))


class Links:
    def __init__(self, place, send_sems, recv_sems):
        self.place = place
        self.send_sems = send_sems
        self.recv_sems = recv_sems
        self.builders = {}
        self.gone = set()

    def send(self, name, to, ends):
        index = len(self.builders)

        def build(landed=False):
            source, target = ends()
            if landed:
                source = target
            return pltpu.make_async_remote_copy(
                src_ref=source,
                dst_ref=target,
                send_sem=self.send_sems.at[index],
                recv_sem=self.recv_sems.at[index],
                device_id=self.place.device(to),
                device_id_type=MESH_ID,
            )

        self.builders[name] = build
        build().start()

    def arrived(self, name):
        self.builders[name](landed=True).wait_recv()

    def left(self, name):
        self.gone.add(name)
        self.builders[name]().wait_send()

    def drain(self):
        for name in self.builders:
            if name not in self.gone:
                self.left(name)


class Ring:
    def __init__(self, parts, slots, sems):
        self.parts = parts
        self.slots = slots
        self.sems = sems
        for index in range(SLOTS):
            self.start(index)

    def copy(self, index):
        slot = index % SLOTS
        return pltpu.make_async_copy(self.parts[index], self.slots.at[slot], self.sems.at[slot])

    def start(self, index):
        if index < len(self.parts):
            self.copy(index).start()

    def get(self, index):
        self.copy(index).wait()
        return self.slots.at[index % SLOTS]

    def done(self, index):
        self.start(index + SLOTS)


class Scatter:
    def __init__(self, links, name, axes, grad, first, second, third):
        self.links, self.name, self.axes = links, name, axes
        self.grad, self.first, self.second, self.third = grad, first, second, third

    def send_first(self, pair):
        b1, b2 = pair
        self.links.send(
            (self.name, 0, b1, b2),
            self.axes[0],
            lambda: (self.grad.at[1, b1, b2], self.first.at[b1, b2]),
        )

    def send_second(self, b2):
        self.links.arrived((self.name, 0, 1, b2))
        self.grad[0, 1, b2] = (
            self.grad[0, 1, b2].astype(F32) + self.first[1, b2].astype(F32)
        ).astype(BF16)
        self.links.send(
            (self.name, 1, b2), self.axes[1], lambda: (self.grad.at[0, 1, b2], self.second.at[b2])
        )

    def send_third(self):
        self.links.arrived((self.name, 0, 0, 1))
        self.links.arrived((self.name, 1, 1))
        self.grad[0, 0, 1] = (
            self.grad[0, 0, 1].astype(F32)
            + self.first[0, 1].astype(F32)
            + self.second[1].astype(F32)
        ).astype(BF16)
        self.links.send((self.name, 2), self.axes[2], lambda: (self.grad.at[0, 0, 1], self.third))

    def total(self):
        self.links.arrived((self.name, 0, 0, 0))
        self.links.arrived((self.name, 1, 0))
        self.links.arrived((self.name, 2))
        return (
            self.grad[0, 0, 0].astype(F32)
            + self.first[0, 0].astype(F32)
            + self.second[0].astype(F32)
            + self.third[...].astype(F32)
        )


def head_window(head):
    start = (head * 9) // 16 - head // 15
    offset = head * HEAD_DIM - start * 128
    lanes = lax.broadcasted_iota(jnp.int32, (SEQ, 256), 1)
    inside = (lanes >= offset) & (lanes < offset + HEAD_DIM)
    return pl.ds(pl.multiple_of(start * 128, 128), 256), inside


def each(function, *lists):
    return [function(*items) for items in zip(*lists)]


def head_probs(qkv, heads):
    windows, insides = zip(*each(head_window, heads))
    queries = each(lambda at, inside: jnp.where(inside, qkv[0, :, at], 0), windows, insides)
    scores = each(lambda query, at: dot_rows(query, qkv[1, :, at]), queries, windows)
    tops = each(lambda score: jnp.max(score, axis=-1, keepdims=True), scores)
    shifted = each(lambda score, top: jnp.exp((score - top) * SCALE), scores, tops)
    totals = each(lambda value: 1.0 / jnp.sum(value, axis=-1, keepdims=True), shifted)
    probs = each(lambda value, total: value * total, shifted, totals)
    return windows, insides, queries, probs


def block_kernel(
    outer,
    hidden,
    cond,
    live,
    out_grad,
    ada_bias,
    qv_bias,
    proj_bias,
    up_bias,
    down_bias,
    ada_w,
    qkv_w,
    proj_w,
    up_w,
    down_w,
    mixed,
    grad_hidden,
    grad_cond,
    out_ada,
    out_ada_b,
    out_qkv,
    out_qv_b,
    out_proj,
    out_proj_b,
    out_up,
    out_up_b,
    out_down,
    out_down_b,
    biases,
    ring_slots,
    cond_rows,
    mod_in,
    mods,
    left_a,
    left_t,
    left_m,
    right_act,
    left_b,
    right_u,
    right_q,
    right_t,
    gb_t,
    g_branch,
    natural,
    att_t,
    qkv,
    attn_out,
    sums,
    row_stage,
    row_group,
    row_all,
    cond_in,
    grad_d,
    grad_u,
    first_d,
    first_u,
    second_d,
    second_u,
    third_d,
    third_u,
    first_q,
    second_q,
    third_q,
    grad_t,
    first_t,
    second_t,
    third_t,
    send_sems,
    recv_sems,
    ring_sems,
    ada_sem,
):
    place = Place(outer)
    bits = place.bits
    m_here = place.m_index
    links = Links(place, send_sems, recv_sems)

    def spot(index):
        return pl.ds(pl.multiple_of(index * SEQ, SEQ), SEQ)

    here, here_yc, here_lc = spot(m_here), spot(place.pair_at("y", "")), spot(place.pair_at("l", ""))
    ff_order = [place.m_at(to) for to in NEAR] + [m_here]

    def ff_part(index):
        return pl.ds(pl.multiple_of(index * D, D), D)

    qkv_parts = [qkv_w.at[:, pl.ds(index * D, D)] for index in range(3)]
    ff_parts = []
    for index in ff_order:
        ff_parts += [up_w.at[:, ff_part(index)], down_w.at[ff_part(index), :]]
    barrier = pltpu.get_barrier_semaphore()
    for names in PEERS:
        pl.semaphore_signal(
            barrier, inc=1, device_id=place.device(names), device_id_type=MESH_ID
        )
    ring = Ring(qkv_parts + [proj_w] + ff_parts + [proj_w] + qkv_parts, ring_slots, ring_sems)
    row_tiles = [pl.ds(start, 64) for start in range(0, SEQ, 64)]

    def bias(start, width=D):
        return biases[:, pl.ds(start, width)]

    def modulation(ada, mod_out):
        load = pltpu.make_async_copy(ada_w, ada, ada_sem)
        load.start()
        silu_row = jax.nn.silu(cond[...].astype(F32))
        cond_rows[m_here] = jnp.broadcast_to(silu_row, (16, D)).astype(BF16)
        pl.semaphore_wait(barrier, len(PEERS))
        for to in NEAR:
            links.send(("cond", to), to, lambda: (cond_rows.at[m_here], cond_rows.at[m_here]))
        for start, part in ((2, qv_bias), (3, proj_bias), (4, up_bias), (8, down_bias), (9, ada_bias)):
            row = part[...].astype(F32)[None, :]
            if start == 2:
                biases[:, : 2 * D] = jnp.concatenate([row[:, :D], jnp.zeros((1, D), F32)], axis=1)
                row = row[:, D:]
            biases[:, start * D : start * D + row.shape[1]] = row
        for rows in row_tiles:
            grad_hidden[rows, :] = norm_rows(hidden[0, rows, :].astype(F32))[0]
        load.wait()
        for to in NEAR:
            links.arrived(("cond", to))
        columns = dot_rows(cond_rows[...].reshape(64, D), ada[...]) + bias(9 * D, ADA)
        mod_out[:, :, :ADA] = columns.astype(BF16).reshape(GROUP, 16, ADA)
        for to in NEAR:
            links.send(
                ("mod", to), to, lambda to=to: (mod_out.at[place.m_at(to)], mod_in.at[m_here])
            )
        mod_in[m_here] = mod_out[m_here]
        for to in NEAR:
            links.left(("mod", to))

    pl.run_scoped(
        modulation, pltpu.VMEM((ADA, D), BF16), pltpu.VMEM((GROUP, 16, 1792), BF16)
    )
    for to in NEAR:
        links.arrived(("mod", to))
    parts = [mod_in[index].astype(F32)[:1] for index in range(GROUP)]
    for index in range(2):
        low, high = parts[2 * index], parts[2 * index + 1]
        mods[3 * index : 3 * index + 1] = low[:, :D]
        mods[3 * index + 1 : 3 * index + 2] = jnp.concatenate(
            [low[:, D:ADA], high[:, : D // 2]], axis=1
        )
        mods[3 * index + 2 : 3 * index + 3] = high[:, D // 2 : ADA]
    shift_a, scale_a, gate_a, shift_m, scale_m, gate_m = range(6)

    def mod(index):
        return mods[index : index + 1]

    live_factor = live[0].astype(F32)
    for rows in row_tiles:
        natural[rows, :] = (
            grad_hidden[rows, :] * (1.0 + mod(scale_a)) + mod(shift_a)
        ).astype(BF16)
        g_branch[rows, :] = (
            out_grad[0, rows, :].astype(F32) * live_factor * mod(gate_m)
        ).astype(BF16)
    left_a[:, here] = natural[...].T
    for to in ("x", "c"):
        links.send(("a", to), to, lambda: (left_a.at[:, here], left_a.at[:, here]))
    gb_t[...] = g_branch[...].T

    def gb_rows(to, x):
        return pl.ds(pl.multiple_of((2 * x + place.flipped(to)["c"]) * 288, 288), 288)

    for to in ("y", "yc", "c"):
        for x in range(2):
            links.send(
                ("gb", to, x),
                to,
                lambda to=to, x=x: (gb_t.at[gb_rows(to, x), :], left_b.at[x, :, here_yc]),
            )
    for x in range(2):
        left_b[x, :, here_yc] = gb_t[gb_rows("", x), :]
    sums[9:10] = sum_rows(g_branch[...].astype(F32))

    for index in range(3):
        part = ring.get(index)
        qkv[index] = (dot(natural[...], part[...]) + bias(index * D)).astype(BF16)
        ring.done(index)

    def attend(group, carry):
        heads = [group * TOGETHER + index for index in range(TOGETHER)]
        windows, insides, _, probs = head_probs(qkv, heads)
        values = each(
            lambda prob, at: dot(prob.astype(BF16), qkv[2, :, at]).astype(BF16), probs, windows
        )
        for at, inside, value in zip(windows, insides, values):
            natural[:, at] = jnp.where(inside, value, natural[:, at])
        return carry

    lax.fori_loop(0, HEADS // TOGETHER, attend, 0)
    att_t[...] = natural[...].T

    def att_rows(part, to):
        start = part * 576 + place.flipped(to)["l"] * 288
        return pl.ds(pl.multiple_of(start, 288), 288)

    for part in range(2):
        for to in ("l", "c"):
            links.send(
                ("t", to, part),
                to,
                lambda part=part, to=to: (
                    att_t.at[att_rows(part, "l" if to == "l" else ""), :],
                    left_t.at[part, :, here_lc],
                ),
            )
        left_t[part, :, here_lc] = att_t[att_rows(part, ""), :]
    part = ring.get(3)
    attn_out[...] = dot(natural[...], part[...]) + bias(3 * D)
    ring.done(3)

    def act_lanes(to):
        return pl.ds(pl.multiple_of(place.flipped(to)["y"] * 512, 512), WINDOW)

    def feed_forward(act_there, pre_stage, after, branch, g_mod):
        slope, act_now = grad_hidden, mixed
        for rows in row_tiles:
            after[rows, :] = hidden[0, rows, :].astype(F32) + mod(gate_a) * attn_out[rows, :]
            normed, _ = norm_rows(after[rows, :])
            natural[rows, :] = (normed * (1.0 + mod(scale_m)) + mod(shift_m)).astype(BF16)
        left_m[:, here] = natural[...].T
        for to in ("x", "c"):
            links.send(("m", to), to, lambda: (left_m.at[:, here], left_m.at[:, here]))
        for step in range(4):
            index = ff_order[step]
            up, down = ring.get(4 + 2 * step), ring.get(5 + 2 * step)
            for tile in range(3):
                lanes = pl.ds(tile * 384, 384)
                offset = pl.multiple_of(4 * D + index * D + tile * 384, 128)
                pre = dot(natural[...], up[:, lanes]) + biases[:, pl.ds(offset, 384)]
                square = pre * pre
                slant = jnp.tanh(0.7978845608028654 * pre * (1.0 + 0.044715 * square))
                half = 0.5 * (1.0 + slant)
                act_now[:, lanes] = (pre * half).astype(BF16)
                slope[:, lanes] = half + 0.5 * pre * (1.0 - slant * slant) * (
                    0.7978845608028654 * (1.0 + 0.134145 * square)
                )
            act_there[step] = act_now[:, act_lanes("y")]
            right_act[index, here_yc] = act_now[:, act_lanes("")]
            links.send(
                ("act", "y", step),
                "y",
                lambda step=step: (act_there.at[step], right_act.at[ff_order[step], here_yc]),
            )
            links.send(
                ("act", "c", step),
                "c",
                lambda step=step: (
                    right_act.at[ff_order[step], here_yc],
                    right_act.at[ff_order[step], here_yc],
                ),
            )
            for tile in range(3):
                lanes = pl.ds(tile * 384, 384)
                g_pre = (dot_rows(g_branch[...], down[lanes, :]) * slope[:, lanes]).astype(BF16)
                sums[pl.ds(10 + index, 1), lanes] = sum_rows(g_pre.astype(F32))
                if step < 3:
                    pre_stage[step, :, lanes] = g_pre
                else:
                    right_u[here, lanes] = g_pre
            if step < 3:
                g_pre_ref = pre_stage.at[step]
                links.send(
                    ("u", NEAR[step]),
                    NEAR[step],
                    lambda step=step: (pre_stage.at[step], right_u.at[here]),
                )
            else:
                g_pre_ref = right_u.at[here]
            new_mod = dot_rows(g_pre_ref[...], up[...])
            g_mod[...] = new_mod + g_mod[...] if step else new_mod
            ring.done(4 + 2 * step)
            new_branch = dot(act_now[...], down[...])
            branch[...] = new_branch + (branch[...] if step else bias(8 * D))
            ring.done(5 + 2 * step)
            if step == 1:
                forward_t()
            if step == 2:
                forward("a")
        zero = jnp.zeros((1, D), F32)
        gate_m_sum = scale_m_sum = shift_m_sum = gate_a_sum = proj_sum = zero
        for rows in row_tiles:
            cotangent = out_grad[0, rows, :].astype(F32) * live_factor
            mixed[rows, :] = (after[rows, :] + mod(gate_m) * branch[rows, :]).astype(BF16)
            gate_m_sum += sum_rows(cotangent * branch[rows, :])
            normed, inverse = norm_rows(after[rows, :])
            grads = g_mod[rows, :]
            shift_m_sum += sum_rows(grads)
            scale_m_sum += sum_rows(grads * normed)
            g_after = cotangent + norm_back(grads * (1.0 + mod(scale_m)), normed, inverse)
            grad_hidden[rows, :] = g_after
            gate_a_sum += sum_rows(g_after * attn_out[rows, :])
            g_attn = (g_after * mod(gate_a)).astype(BF16)
            natural[rows, :] = g_attn
            proj_sum += sum_rows(g_attn.astype(F32))
        sums[2:3] = gate_a_sum
        sums[3:4] = shift_m_sum
        sums[4:5] = scale_m_sum
        sums[5:6] = gate_m_sum
        sums[8:9] = proj_sum
        for step in range(2):
            forward_act(step)

    spot_x, spot_y = spot(place.m_at("x")), spot(place.pair_at("y", "y"))
    spot_l = spot(place.pair_at("l", "l"))

    def forward(name):
        target = {"a": left_a, "m": left_m}[name]
        links.arrived((name, "x"))
        links.send((name, "f"), "c", lambda: (target.at[:, spot_x], target.at[:, spot_x]))

    def forward_t():
        for part in range(2):
            links.arrived(("t", "l", part))
            links.send(
                ("t", "f", part),
                "c",
                lambda part=part: (left_t.at[part, :, spot_l], left_t.at[part, :, spot_l]),
            )

    def forward_act(step):
        def target():
            return right_act.at[ff_order[step], spot_y]

        links.arrived(("act", "y", step))
        links.send(("act", "f", step), "c", lambda: (target(), target()))

    scatter_d = Scatter(links, "d", "lxh", grad_d, first_d, second_d, third_d)
    scatter_u = Scatter(links, "u", "ylh", grad_u, first_u, second_u, third_u)
    scatter_t = Scatter(links, "t", "yxh", grad_t, first_t, second_t, third_t)

    def form_down():
        for to in ("y", "c", "yc"):
            for x in range(2):
                links.arrived(("gb", to, x))
        for step in range(4):
            links.arrived(("act", "c", step))
            links.arrived(("act", "f", step))
        for b0 in (1, 0):
            for b1, b2 in ORDER:
                flips = "l" * b0 + "x" * b1 + "h" * b2
                there = place.flipped(flips)
                wide = dot(left_b[there["x"]], right_act[there["h"] * 2 + there["l"]])
                wide = wide.astype(BF16)
                block = jnp.where(bits["y"] == 0, wide[:, :576], wide[:, 64:])
                grad_d[b0, b1, b2] = jnp.concatenate([block[:BLOCK], block[BLOCK:]], axis=1)
                if b0:
                    scatter_d.send_first((b1, b2))

    def grad_rows(flips):
        return pl.ds(pl.multiple_of(place.h_at(flips) * BLOCK, BLOCK), BLOCK)

    def form_up():
        for to in NEAR:
            links.arrived(("u", to))
        links.arrived(("m", "c"))
        links.arrived(("m", "f"))
        for b0 in (1, 0):
            for b1, b2 in ORDER:
                rows = grad_rows("y" * b0 + "l" * b1 + "h" * b2)
                grad_u[b0, b1, b2] = dot(left_m[rows, :], right_u[...]).astype(BF16)
                if b0:
                    scatter_u.send_first((b1, b2))

    def form_proj():
        for to in ("l", "c", "lc"):
            links.arrived(("ga", to))
        for part in range(2):
            links.arrived(("t", "c", part))
            links.arrived(("t", "f", part))
        for b0 in (1, 0):
            for b2 in (1, 0):
                there = place.flipped("y" * b0 + "h" * b2)
                rows = pl.ds(pl.multiple_of(there["y"] * BLOCK, BLOCK), BLOCK)
                wide = dot(left_t[there["h"], rows, :], right_t[...]).astype(BF16)
                for x in range(2):
                    block = wide[:, 288 * x : 288 * x + 288]
                    other = 1 - bits["x"] if x else bits["x"]
                    grad_t[b0, other, b2, :, :288] = block
        for pair in ORDER:
            scatter_t.send_first(pair)

    def attention_back(g_qkv, q_stage, ga_stage):
        g_attn = natural[...]
        columns = [
            jnp.concatenate(
                [
                    g_attn[:, 288 * core : 288 * core + 288],
                    g_attn[:, 576 + 288 * core : 864 + 288 * core],
                    jnp.zeros((SEQ, 64), BF16),
                ],
                axis=1,
            )
            for core in range(2)
        ]
        ga_stage[...] = jnp.where(bits["c"] == 0, columns[1], columns[0])
        right_t[here_lc, :] = jnp.where(bits["c"] == 0, columns[0], columns[1])
        for to in ("l", "lc", "c"):
            links.send(
                ("ga", to),
                to,
                lambda to=to: (
                    right_t.at[here_lc] if to == "l" else ga_stage,
                    right_t.at[here_lc],
                ),
            )
        part = ring.get(12)
        g_att = g_branch
        g_att[...] = dot_rows(natural[...], part[...]).astype(BF16)
        ring.done(12)

        def back(group, carry):
            heads = [group * TOGETHER + index for index in range(TOGETHER)]
            windows, insides, queries, probs = head_probs(qkv, heads)
            grads = each(lambda at, inside: jnp.where(inside, g_att[:, at], 0), windows, insides)
            g_probs = each(lambda grad, at: dot_rows(grad, qkv[2, :, at]), grads, windows)
            g_values = each(lambda prob, grad: dot(prob.astype(BF16).T, grad), probs, grads)
            row_dots = each(
                lambda prob, g_prob: jnp.sum(prob * g_prob, axis=-1, keepdims=True), probs, g_probs
            )
            g_scores = each(
                lambda prob, g_prob, row_dot: (prob * (g_prob - row_dot)).astype(BF16),
                probs,
                g_probs,
                row_dots,
            )
            g_queries = each(lambda g, at: dot(g, qkv[1, :, at]) * SCALE, g_scores, windows)
            g_keys = each(lambda g, query: dot(g.T, query) * SCALE, g_scores, queries)
            for index, values in enumerate((g_queries, g_keys, g_values)):
                for at, inside, value in zip(windows, insides, values):
                    g_qkv[index, :, at] = jnp.where(
                        inside, value.astype(BF16), g_qkv[index, :, at]
                    )
            return carry

        groups = HEADS // TOGETHER
        lax.fori_loop(0, groups // 2, back, 0)
        forward_act(2)
        lax.fori_loop(groups // 2, groups, back, 0)
        for index in range(GROUP):
            start, pieces = index * 864, []
            while start < index * 864 + 864:
                stop = min(index * 864 + 864, (start // D + 1) * D)
                pieces.append(g_qkv[start // D][:, start % D : start % D + stop - start])
                start = stop
            q_stage[index] = jnp.concatenate(pieces + [jnp.zeros((SEQ, 32), BF16)], axis=1)
        for to in NEAR:
            links.send(
                ("q", to), to, lambda to=to: (q_stage.at[place.m_at(to)], right_q.at[here])
            )
        right_q[here, :] = q_stage[m_here]
        sums[6:7] = sum_rows(g_qkv[0].astype(F32))
        sums[7:8] = sum_rows(g_qkv[2].astype(F32))
        forward_act(3)
        forward("m")
        form_proj()
        form_down()

        for index in range(3):
            part = ring.get(13 + index)
            product = dot_rows(g_qkv[index], part[...])
            attn_out[...] = attn_out[...] + product if index else product
        zero = jnp.zeros((1, D), F32)
        shift_sum = scale_sum = zero
        for rows in row_tiles:
            normed, inverse = norm_rows(hidden[0, rows, :].astype(F32))
            grads = attn_out[rows, :]
            shift_sum += sum_rows(grads)
            scale_sum += sum_rows(grads * normed)
            grad_hidden[rows, :] = grad_hidden[rows, :] + norm_back(
                grads * (1.0 + mod(scale_a)), normed, inverse
            )
        sums[0:1] = shift_sum
        sums[1:2] = scale_sum
        send_rows()
        form_up()
        for b2 in (1, 0):
            scatter_d.send_second(b2)
        for b2 in (1, 0):
            scatter_t.send_second(b2)
        for to in NEAR:
            links.left(("q", to))
        for to in ("l", "lc", "c"):
            links.left(("ga", to))

    def reduce_rest(grad_q, ada, spread, cond_all, cond_stage):
        scatter_q = Scatter(links, "q", "ylh", grad_q, first_q, second_q, third_q)
        load = pltpu.make_async_copy(ada_w, ada, ada_sem)
        load.start()
        gather_rows()
        for to in NEAR:
            links.arrived(("q", to))
        for to in ("c", "f"):
            links.arrived(("a", to))
        for b0 in (1, 0):
            for b1, b2 in ORDER:
                rows = grad_rows("y" * b0 + "l" * b1 + "h" * b2)
                grad_q[b0, b1, b2] = dot(left_a[rows, :], right_q[...]).astype(BF16)
                if b0:
                    scatter_q.send_first((b1, b2))
        for b2 in (1, 0):
            scatter_u.send_second(b2)
        scatter_t.send_third()
        scatter_d.send_third()
        ada_grads(load, ada, spread, cond_all, cond_stage)
        scatter_u.send_third()
        total = scatter_d.total()
        out_down[:BLOCK, :] = total[:, :576]
        out_down[BLOCK:, :] = total[:, 576:]
        out_proj[...] = scatter_t.total()[:, :288]
        for b2 in (1, 0):
            scatter_q.send_second(b2)
        out_up[...] = scatter_u.total()
        scatter_q.send_third()
        out_qkv[...] = scatter_q.total()[:, :864]
        links.drain()

    def send_rows():
        grads = jnp.concatenate([sums[index : index + 1] for index in range(6)], axis=1)
        qv = jnp.concatenate([sums[6:7], sums[7:8]], axis=1)
        for index in range(GROUP):
            row = jnp.concatenate(
                [
                    grads[:, ADA * index : ADA * index + ADA],
                    qv[:, 576 * index : 576 * index + 576],
                    sums[8:9][:, 288 * index : 288 * index + 288],
                    sums[10 + index : 11 + index],
                    sums[9:10][:, 288 * index : 288 * index + 288],
                    jnp.zeros((1, 64), F32),
                ],
                axis=1,
            )
            row_stage[index] = jnp.concatenate(
                [row[:, 128 * tile : 128 * tile + 128] for tile in range(32)], axis=0
            ).astype(BF16)
            silu_row = cond_rows[index].astype(F32)[:1]
            row_group[index, 32:48] = jnp.concatenate(
                [silu_row[:, 128 * tile : 128 * tile + 128] for tile in range(9)]
                + [jnp.zeros((7, 128), F32)],
                axis=0,
            ).astype(BF16)
        for to in NEAR:
            links.send(
                ("row", to),
                to,
                lambda to=to: (row_stage.at[place.m_at(to)], row_group.at[m_here, pl.ds(0, 32)]),
            )
        row_group[m_here, 0:32] = row_stage[m_here]

    def gather_rows():
        for to in NEAR:
            links.arrived(("row", to))
        row_all[place.h_index] = row_group[...]
        for to in FAR:
            links.send(("rows", to), to, lambda: (row_group, row_all.at[place.h_index]))

    def ada_grads(load, ada, spread, cond_all, cond_stage):
        for to in FAR:
            links.arrived(("rows", to))
        images = GROUP * INNER
        spread[...] = row_all[...].astype(F32).reshape(images * 48, 128)

        def tile(index):
            return spread[pl.ds(index, images, stride=48), :]

        columns = jnp.concatenate([tile(index) for index in range(14)], axis=1)[:, :ADA]
        columns = columns.astype(BF16)
        totals = jnp.concatenate([sum_rows(tile(index)) for index in range(32)], axis=1)
        start = 0
        for out in (out_ada_b, out_qv_b, out_proj_b, out_up_b, out_down_b):
            width = out.shape[0]
            out[...] = totals[:, start : start + width].reshape(width)
            start += width
        for to in ("y", "yc", "c"):
            for x in range(2):
                links.left(("gb", to, x))
        silu_all = jnp.concatenate([tile(32 + index) for index in range(9)], axis=1)
        gb_t[:, :images] = silu_all.T.astype(BF16)
        rows = pl.ds(pl.multiple_of(place.h_index * BLOCK, BLOCK), BLOCK)
        out_ada[...] = dot(gb_t[rows, :images], columns)
        load.wait()
        cond_all[...] = dot(columns, ada[...])
        for to in NEAR:
            row = place.h_index * GROUP + place.m_at(to)
            cond_stage[place.m_at(to)] = jnp.broadcast_to(cond_all[pl.ds(row, 1), :], (8, D))
            links.send(
                ("gc", to), to, lambda to=to: (cond_stage.at[place.m_at(to)], cond_in.at[m_here])
            )
        total = cond_all[pl.ds(place.h_index * GROUP + m_here, 1), :]
        for to in NEAR:
            links.arrived(("gc", to))
            total += cond_in[place.m_at(to)][:1]
        values = cond[...].astype(F32)
        sigmoid = jax.nn.sigmoid(values)
        grad_cond[...] = total * (sigmoid * (1.0 + values * (1.0 - sigmoid)))

    def local_work(act_there, pre_stage):
        f32_rows = pltpu.VMEM((SEQ, D), F32)
        pl.run_scoped(
            partial(feed_forward, act_there, pre_stage),
            f32_rows,
            f32_rows,
            f32_rows,
        )
        pl.run_scoped(
            attention_back,
            pltpu.VMEM((3, SEQ, D), BF16),
            pltpu.VMEM((GROUP, SEQ, 896), BF16),
            pltpu.VMEM((SEQ, WINDOW), BF16),
        )
        for step in range(4):
            links.left(("act", "y", step))
        for to in NEAR:
            links.left(("u", to))

    pl.run_scoped(
        local_work, pltpu.VMEM((4, SEQ, WINDOW), BF16), pltpu.VMEM((3, SEQ, D), BF16)
    )
    pl.run_scoped(
        reduce_rest,
        pltpu.VMEM((2, 2, 2, BLOCK, 896), BF16),
        pltpu.VMEM((ADA, D), BF16),
        pltpu.VMEM((GROUP * INNER * 48, 128), F32),
        pltpu.VMEM((GROUP * INNER, D), F32),
        pltpu.VMEM((GROUP, 8, D), F32),
    )


TOGETHER = 4


def run_block(outer, *operands):
    vmem = pl.BlockSpec(memory_space=pltpu.VMEM)
    anywhere = pl.BlockSpec(memory_space=pl.ANY)
    smem = pl.BlockSpec(memory_space=pltpu.SMEM)
    scratch = [
        ((1, 9 * D + ADA), F32),
        ((SLOTS, D, D), BF16),
        ((GROUP, 16, D), BF16),
        ((GROUP, 16, 1792), BF16),
        ((8, D), F32),
        ((D, TOKENS), BF16),
        ((2, 288, TOKENS), BF16),
        ((D, TOKENS), BF16),
        ((4, TOKENS, WINDOW), BF16),
        ((2, 288, TOKENS), BF16),
        ((TOKENS, D), BF16),
        ((TOKENS, 896), BF16),
        ((TOKENS, WINDOW), BF16),
        ((D, SEQ), BF16),
        ((SEQ, D), BF16),
        ((SEQ, D), BF16),
        ((D, SEQ), BF16),
        ((3, SEQ, D), BF16),
        ((SEQ, D), F32),
        ((16, D), F32),
        ((GROUP, 32, 128), BF16),
        ((GROUP, 48, 128), BF16),
        ((INNER, GROUP, 48, 128), BF16),
        ((GROUP, 8, D), F32),
    ]
    block = (BLOCK, D)
    scratch += [((2, 2, 2) + block, BF16)] * 2
    scratch += [((2, 2) + block, BF16)] * 2 + [((2,) + block, BF16)] * 2 + [(block, BF16)] * 2
    block = (BLOCK, 896)
    scratch += [((2, 2) + block, BF16), ((2,) + block, BF16), (block, BF16)]
    block = (BLOCK, 384)
    scratch += [((2, 2, 2) + block, BF16), ((2, 2) + block, BF16), ((2,) + block, BF16)]
    scratch += [(block, BF16)]
    outs = [
        ((SEQ, D), BF16),
        ((SEQ, D), F32),
        ((1, D), F32),
        ((BLOCK, ADA), F32),
        ((ADA,), F32),
        ((BLOCK, 864), F32),
        ((576,), F32),
        ((BLOCK, 288), F32),
        ((288,), F32),
        ((BLOCK, D), F32),
        ((D,), F32),
        ((288, 576), F32),
        ((288,), F32),
    ]
    outs = [jax.ShapeDtypeStruct(*out) for out in outs]
    results = pl.pallas_call(
        partial(block_kernel, outer),
        out_shape=outs,
        in_specs=[vmem, vmem, smem] + [vmem] * 6 + [anywhere] * 5,
        out_specs=[vmem] * len(outs),
        scratch_shapes=[pltpu.VMEM(*each) for each in scratch]
        + [
            pltpu.SemaphoreType.DMA((96,)),
            pltpu.SemaphoreType.DMA((96,)),
            pltpu.SemaphoreType.DMA((SLOTS,)),
            pltpu.SemaphoreType.DMA,
        ],
        compiler_params=pltpu.CompilerParams(
            collective_id=0, has_side_effects=True, vmem_limit_bytes=VMEM_LIMIT
        ),
    )(*operands)
    return pl.pallas_call(
        place_kernel,
        out_shape=outs,
        in_specs=[vmem] * len(outs),
        out_specs=[anywhere] * len(outs),
        scratch_shapes=[pltpu.SemaphoreType.DMA((len(outs),))],
    )(*results)


VMEM_LIMIT = 63 * 2**20 + 900 * 2**10


def place_kernel(*refs):
    count = len(refs) // 2
    copies = [
        pltpu.make_async_copy(refs[index], refs[count + index], refs[-1].at[index])
        for index in range(count)
    ]
    for copy in copies:
        copy.start()
    for copy in copies:
        copy.wait()


def on_device(
    outer,
    hidden_in,
    conditioning,
    live_images,
    out_grad,
    ada_weight,
    ada_bias,
    qkv_weight,
    qv_bias,
    proj_weight,
    proj_bias,
    up_weight,
    up_bias,
    down_weight,
    down_bias,
):
    (
        mixed,
        grad_hidden,
        grad_cond,
        out_ada_w,
        out_ada_b,
        out_qkv_w,
        out_qv_b,
        out_proj_w,
        out_proj_b,
        out_up_w,
        out_up_b,
        out_down_w,
        out_down_b,
    ) = run_block(
        outer,
        hidden_in,
        conditioning,
        live_images,
        out_grad,
        ada_bias,
        qv_bias,
        proj_bias,
        up_bias,
        down_bias,
        ada_weight.T,
        qkv_weight,
        proj_weight,
        up_weight,
        down_weight,
    )
    out_down_w = out_down_w.T
    if outer > 1:
        groups = [[h * outer + low for low in range(outer)] for h in range(INNER)]
        out_ada_w, out_down_w, out_up_w, out_qkv_w, out_proj_w = (
            lax.psum_scatter(
                part, "dp", scatter_dimension=0, tiled=True, axis_index_groups=groups
            )
            for part in (out_ada_w, out_down_w, out_up_w, out_qkv_w, out_proj_w)
        )
        out_ada_b, out_qv_b, out_proj_b, out_up_b, out_down_b = (
            jnp.sum(
                lax.all_gather(part, "dp", axis=0, axis_index_groups=groups), axis=0
            )
            for part in (out_ada_b, out_qv_b, out_proj_b, out_up_b, out_down_b)
        )
    return (
        mixed[None],
        grad_hidden[None],
        grad_cond,
        out_ada_w,
        out_ada_b,
        out_qkv_w,
        out_qv_b,
        out_proj_w,
        out_proj_b,
        out_up_w,
        out_up_b,
        out_down_w,
        out_down_b,
    )


def solution(mesh):
    in_specs = (
        P(("dp", "mp"), None, None),
        P(("dp", "mp"), None),
        P(("dp", "mp")),
        P(("dp", "mp"), None, None),
        P(None, "mp"),
        P("mp"),
        P(),
        P(),
        P(),
        P(),
        P(),
        P(),
        P(),
        P(),
    )
    out_specs = (
        P(("dp", "mp"), None, None),
        P(("dp", "mp"), None, None),
        P(("dp", "mp"), None),
        P("dp", "mp"),
        P("mp"),
        P("dp", "mp"),
        P("mp"),
        P("dp", "mp"),
        P("mp"),
        P("dp", "mp"),
        P("mp"),
        P("dp", "mp"),
        P("mp"),
    )
    return jax.shard_map(
        partial(on_device, mesh.shape["dp"] // INNER),
        mesh=mesh,
        in_specs=in_specs,
        out_specs=out_specs,
        check_vma=False,
    )
```

```python
from functools import partial

import jax
import jax.numpy as jnp
from jax import lax
from jax.experimental import pallas as pl
from jax.experimental.pallas import tpu as pltpu
from jax.sharding import PartitionSpec as P

D = 1152
HEADS = 16
HEAD_DIM = 72
FF = 4608
SEQ = 256
ADA = 1728
MESH_ID = pl.DeviceIdType.MESH
BF16 = jnp.bfloat16
F32 = jnp.float32
INNER = 8
BLOCK = D // INNER
GROUP = 4
TOKENS = GROUP * SEQ
WINDOW = 640
SLOTS = 3
SCALE = HEAD_DIM ** (-0.5)
PEERS = ("c", "x", "xc", "y", "yc", "l", "lc", "h", "yl", "yh", "lh", "ylh")
FAR = ("y", "l", "h", "yl", "yh", "lh", "ylh")
NEAR = ("xc", "x", "c")
ORDER = ((1, 1), (0, 1), (1, 0), (0, 0))
EARLY, LATE = ORDER[:2], ORDER[2:]


def dot(left, right):
    return jnp.dot(left, right, preferred_element_type=F32)


def dot_rows(left, right):
    return lax.dot_general(left, right, (((1,), (1,)), ((), ())), preferred_element_type=F32)


def norm_rows(values):
    center = values - jnp.mean(values, axis=-1, keepdims=True)
    inverse = lax.rsqrt(jnp.mean(center * center, axis=-1, keepdims=True) + 1e-06)
    return center * inverse, inverse


def norm_back(grad_normed, normed, inverse):
    mean_grad = jnp.mean(grad_normed, axis=-1, keepdims=True)
    mean_prod = jnp.mean(grad_normed * normed, axis=-1, keepdims=True)
    return inverse * (grad_normed - mean_grad - normed * mean_prod)


def sum_rows(values):
    return jnp.sum(values, axis=0, keepdims=True)


class Place:
    def __init__(self, outer):
        data, model = lax.axis_index("dp"), lax.axis_index("mp")
        self.outer = outer
        self.low = data % outer
        self.h_index = data // outer
        self.m_index = model
        self.bits = {
            "h": self.h_index // 4,
            "l": (self.h_index // 2) % 2,
            "y": self.h_index % 2,
            "x": model // 2,
            "c": model % 2,
        }

    def flipped(self, names):
        if "p" in names and "r" in names:
            names += "yl"
        bits = {key: (1 - bit if key in names else bit) for key, bit in self.bits.items()}
        if ("p" in names) != ("r" in names):
            second = bits["c"] if "p" in names else 1 - bits["c"]
            bits["y"] += second * (1 - 2 * bits["y"])
            bits["l"] += (1 - second) * (1 - 2 * bits["l"])
        return bits

    def h_at(self, names):
        bits = self.flipped(names)
        return bits["h"] * 4 + bits["l"] * 2 + bits["y"]

    def m_at(self, names):
        bits = self.flipped(names)
        return bits["x"] * 2 + bits["c"]

    def pair_at(self, axis, names):
        bits = self.flipped(names)
        return bits[axis] * 2 + bits["c"]

    def device(self, names):
        return (self.h_at(names) * self.outer + self.low, self.m_at(names))


class Links:
    def __init__(self, place, send_sems, recv_sems):
        self.place = place
        self.send_sems = send_sems
        self.recv_sems = recv_sems
        self.builders = {}
        self.gone = set()

    def send(self, name, to, ends):
        self.plan(name, to, ends)
        self.start(name)

    def start(self, name):
        self.builders[name]().start()

    def plan(self, name, to, ends):
        index = len(self.builders)

        def build(landed=False):
            source, target = ends()
            if landed:
                source = target
            return pltpu.make_async_remote_copy(
                src_ref=source,
                dst_ref=target,
                send_sem=self.send_sems.at[index],
                recv_sem=self.recv_sems.at[index],
                device_id=self.place.device(to),
                device_id_type=MESH_ID,
            )

        self.builders[name] = build

    def arrived(self, name):
        self.builders[name](landed=True).wait_recv()

    def left(self, name):
        self.gone.add(name)
        self.builders[name]().wait_send()

    def drain(self):
        for name in self.builders:
            if name not in self.gone:
                self.left(name)


class Ring:
    def __init__(self, parts, slots, sems):
        self.parts = parts
        self.slots = slots
        self.sems = sems

    def begin(self):
        for index in range(SLOTS):
            self.start(index)

    def copy(self, index):
        slot = index % SLOTS
        return pltpu.make_async_copy(self.parts[index], self.slots.at[slot], self.sems.at[slot])

    def start(self, index):
        if index < len(self.parts):
            self.copy(index).start()

    def get(self, index):
        self.copy(index).wait()
        return self.slots.at[index % SLOTS]

    def done(self, index):
        self.start(index + SLOTS)


class Scatter:
    def __init__(self, links, name, axes, grad, first, second, third):
        self.links, self.name, self.axes = links, name, axes
        self.grad, self.first, self.second, self.third = grad, first, second, third

        for b1, b2 in ORDER:
            self.links.plan(
                (name, 0, b1, b2),
                axes[0],
                lambda b1=b1, b2=b2: (grad.at[1, b1, b2], first.at[b1, b2]),
            )

    def send_first(self, *pairs):
        for b1, b2 in pairs:
            self.links.start((self.name, 0, b1, b2))

    def send_second(self, b2):
        self.links.arrived((self.name, 0, 1, b2))
        self.grad[0, 1, b2] = (
            self.grad[0, 1, b2].astype(F32) + self.first[1, b2].astype(F32)
        ).astype(BF16)
        self.links.send(
            (self.name, 1, b2), self.axes[1], lambda: (self.grad.at[0, 1, b2], self.second.at[b2])
        )

    def send_third(self):
        self.links.arrived((self.name, 0, 0, 1))
        self.links.arrived((self.name, 1, 1))
        self.grad[0, 0, 1] = (
            self.grad[0, 0, 1].astype(F32)
            + self.first[0, 1].astype(F32)
            + self.second[1].astype(F32)
        ).astype(BF16)
        self.links.send((self.name, 2), self.axes[2], lambda: (self.grad.at[0, 0, 1], self.third))

    def total(self):
        self.links.arrived((self.name, 0, 0, 0))
        self.links.arrived((self.name, 1, 0))
        self.links.arrived((self.name, 2))
        return (
            self.grad[0, 0, 0].astype(F32)
            + self.first[0, 0].astype(F32)
            + self.second[0].astype(F32)
            + self.third[...].astype(F32)
        )


def head_window(head):
    start = (head * 9) // 16 - head // 15
    offset = head * HEAD_DIM - start * 128
    lanes = lax.broadcasted_iota(jnp.int32, (SEQ, 256), 1)
    inside = (lanes >= offset) & (lanes < offset + HEAD_DIM)
    return pl.ds(pl.multiple_of(start * 128, 128), 256), inside


def each(function, *lists):
    return [function(*items) for items in zip(*lists)]


def head_probs(qkv, heads):
    windows, insides = zip(*each(head_window, heads))
    queries = each(lambda at, inside: jnp.where(inside, qkv[0, :, at], 0), windows, insides)
    scores = each(lambda query, at: dot_rows(query, qkv[1, :, at]), queries, windows)
    tops = each(lambda score: jnp.max(score, axis=-1, keepdims=True), scores)
    shifted = each(lambda score, top: jnp.exp((score - top) * SCALE), scores, tops)
    totals = each(lambda value: 1.0 / jnp.sum(value, axis=-1, keepdims=True), shifted)
    probs = each(lambda value, total: value * total, shifted, totals)
    return windows, insides, queries, probs


def block_kernel(
    outer,
    hidden_hbm,
    cond,
    live,
    out_grad_hbm,
    ada_bias,
    qv_bias,
    proj_bias,
    up_bias,
    down_bias,
    ada_w,
    qkv_w,
    proj_w,
    up_w,
    down_w,
    mixed_hbm,
    grad_hidden_hbm,
    grad_cond,
    ada_hbm,
    out_ada_b,
    qkv_hbm,
    out_qv_b,
    proj_hbm,
    out_proj_b,
    up_hbm,
    out_up_b,
    down_hbm,
    out_down_b,
    hidden,
    out_grad,
    mixed,
    grad_hidden,
    biases,
    ring_slots,
    cond_rows,
    mod_in,
    mods,
    left_a,
    left_t,
    left_m,
    right_act,
    left_b,
    right_u,
    right_q,
    right_t,
    gb_t,
    g_branch,
    natural,
    att_t,
    qkv,
    attn_out,
    sums,
    row_stage,
    row_group,
    row_all,
    silu_all,
    cond_in,
    grad_d,
    grad_u,
    first_d,
    first_u,
    second_d,
    second_u,
    third_d,
    third_u,
    first_q,
    second_q,
    third_q,
    grad_t,
    first_t,
    second_t,
    third_t,
    send_sems,
    recv_sems,
    ring_sems,
    local_sems,
):
    place = Place(outer)
    bits = place.bits
    m_here = place.m_index
    links = Links(place, send_sems, recv_sems)

    def spot(index):
        return pl.ds(pl.multiple_of(index * SEQ, SEQ), SEQ)

    here, here_yc, here_lc = spot(m_here), spot(place.pair_at("y", "")), spot(place.pair_at("l", ""))
    ff_order = [place.m_at(to) for to in NEAR] + [m_here]

    def ff_part(index):
        return pl.ds(pl.multiple_of(index * D, D), D)

    qkv_parts = [qkv_w.at[:, pl.ds(index * D, D)] for index in range(3)]
    ff_parts = []
    for index in ff_order:
        ff_parts += [up_w.at[:, ff_part(index)], down_w.at[ff_part(index), :]]
    def local(name, source, target):
        return pltpu.make_async_copy(source, target, local_sems.at[LOCAL.index(name)])

    barrier = pltpu.get_barrier_semaphore()
    for names in PEERS:
        pl.semaphore_signal(
            barrier, inc=1, device_id=place.device(names), device_id_type=MESH_ID
        )
    ring = Ring(qkv_parts + [proj_w] + ff_parts + [proj_w] + qkv_parts, ring_slots, ring_sems)
    row_tiles = [pl.ds(start, 64) for start in range(0, SEQ, 64)]

    def bias(start, width=D):
        return biases[:, pl.ds(start, width)]

    def modulation(ada, mod_out):
        silu_row = jax.nn.silu(cond[...].astype(F32))
        cond_rows[m_here] = jnp.broadcast_to(silu_row, (16, D)).astype(BF16)
        load = local("ada_in", ada_w, ada)
        load.start()
        pl.semaphore_wait(barrier, len(PEERS))
        for to in NEAR:
            links.send(("cond", to), to, lambda: (cond_rows.at[m_here], cond_rows.at[m_here]))
        copy_in = local("hidden", hidden_hbm, hidden)
        copy_in.start()
        ring.begin()
        for start, part in ((2, qv_bias), (3, proj_bias), (4, up_bias), (8, down_bias), (9, ada_bias)):
            row = part[...].astype(F32)[None, :]
            if start == 2:
                biases[:, : 2 * D] = jnp.concatenate([row[:, :D], jnp.zeros((1, D), F32)], axis=1)
                row = row[:, D:]
            biases[:, start * D : start * D + row.shape[1]] = row
        copy_in.wait()
        local("out_grad", out_grad_hbm, out_grad).start()
        for rows in row_tiles:
            grad_hidden[rows, :] = norm_rows(hidden[0, rows, :].astype(F32))[0]
        load.wait()
        for to in NEAR:
            links.arrived(("cond", to))
        columns = dot_rows(cond_rows[...].reshape(64, D), ada[...]) + bias(9 * D, ADA)
        mod_out[:, :, :ADA] = columns.astype(BF16).reshape(GROUP, 16, ADA)
        for to in NEAR:
            links.send(
                ("mod", to), to, lambda to=to: (mod_out.at[place.m_at(to)], mod_in.at[m_here])
            )
        mod_in[m_here] = mod_out[m_here]
        for to in NEAR:
            links.left(("mod", to))

    def send_silu():
        for index in range(GROUP):
            silu_row = cond_rows[index].astype(F32)[:1]
            tiles = silu_row.reshape(9, 128)
            silu_all[place.h_index, index] = jnp.concatenate(
                [tiles, jnp.zeros((7, 128), F32)], axis=0
            ).astype(BF16)
        for to in FAR:
            links.send(
                ("silu", to),
                to,
                lambda: (silu_all.at[place.h_index], silu_all.at[place.h_index]),
            )

    pl.run_scoped(
        modulation, pltpu.VMEM((ADA, D), BF16), pltpu.VMEM((GROUP, 16, 1792), BF16)
    )
    for to in NEAR:
        links.arrived(("mod", to))
    parts = [mod_in[index].astype(F32)[:1] for index in range(GROUP)]
    for index in range(2):
        low, high = parts[2 * index], parts[2 * index + 1]
        mods[3 * index : 3 * index + 1] = low[:, :D]
        mods[3 * index + 1 : 3 * index + 2] = jnp.concatenate(
            [low[:, D:ADA], high[:, : D // 2]], axis=1
        )
        mods[3 * index + 2 : 3 * index + 3] = high[:, D // 2 : ADA]
    shift_a, scale_a, gate_a, shift_m, scale_m, gate_m = range(6)

    def mod(index):
        return mods[index : index + 1]

    live_factor = live[0].astype(F32)
    local("out_grad", out_grad_hbm, out_grad).wait()
    for rows in row_tiles:
        natural[rows, :] = (
            grad_hidden[rows, :] * (1.0 + mod(scale_a)) + mod(shift_a)
        ).astype(BF16)
        g_branch[rows, :] = (
            out_grad[0, rows, :].astype(F32) * live_factor * mod(gate_m)
        ).astype(BF16)
    left_a[:, here] = natural[...].T

    def send_a(half):
        def ends():
            part = left_a.at[pl.ds(half * 576, 576), here]
            return part, part

        for to in ("x", "c"):
            links.send(("a", to, half), to, ends)

    send_a(0)
    gb_t[...] = g_branch[...].T

    def gb_rows(to, x):
        return pl.ds(pl.multiple_of((2 * x + place.flipped(to)["c"]) * 288, 288), 288)

    for to in ("l", "lc", "c"):
        for x in range(2):
            links.send(
                ("gb", to, x),
                to,
                lambda to=to, x=x: (gb_t.at[gb_rows(to, x), :], left_b.at[x, :, here_lc]),
            )
    for x in range(2):
        left_b[x, :, here_lc] = gb_t[gb_rows("", x), :]
    sums[9:10] = sum_rows(g_branch[...].astype(F32))
    send_silu()

    for index in range(3):
        part = ring.get(index)
        qkv[index] = (dot(natural[...], part[...]) + bias(index * D)).astype(BF16)
        ring.done(index)

    def attend(group, carry):
        heads = [group * TOGETHER + index for index in range(TOGETHER)]
        windows, insides, _, probs = head_probs(qkv, heads)
        values = each(
            lambda prob, at: dot(prob.astype(BF16), qkv[2, :, at]).astype(BF16), probs, windows
        )
        for at, inside, value in zip(windows, insides, values):
            natural[:, at] = jnp.where(inside, value, natural[:, at])
        return carry

    lax.fori_loop(0, HEADS // TOGETHER, attend, 0)
    att_t[...] = natural[...].T.reshape(4, 2, BLOCK, SEQ)
    for to in ("y", "c"):
        links.send(
            ("t", to),
            to,
            lambda to=to: (
                att_t.at[:, place.flipped("y" if to == "y" else "")["y"]],
                left_t.at[:, :, here_yc],
            ),
        )
    left_t[:, :, here_yc] = att_t[:, bits["y"]]
    part = ring.get(3)
    attn_out[...] = dot(natural[...], part[...]) + bias(3 * D)
    ring.done(3)

    def act_rows(pair):
        return bits["x"] if pair else 1 - bits["x"]

    def feed_forward(act_stage, pre_stage, after, branch, g_mod):
        slope = grad_hidden
        for rows in row_tiles:
            after[rows, :] = hidden[0, rows, :].astype(F32) + mod(gate_a) * attn_out[rows, :]
            normed, _ = norm_rows(after[rows, :])
            natural[rows, :] = (normed * (1.0 + mod(scale_m)) + mod(shift_m)).astype(BF16)
        left_m[:, here] = natural[...].T
        for to in ("x", "c"):
            links.send(("m", to), to, lambda: (left_m.at[:, here], left_m.at[:, here]))
        for step in range(4):
            index = ff_order[step]
            up = ring.get(4 + 2 * step)
            parity = index % 2
            away = parity + bits["l"] - 2 * parity * bits["l"]
            act_now = act_stage.at[away * (1 + step // 2)]
            for tile in range(3):
                lanes = pl.ds(tile * 384, 384)
                offset = pl.multiple_of(4 * D + index * D + tile * 384, 128)
                pre = dot(natural[...], up[:, lanes]) + biases[:, pl.ds(offset, 384)]
                square = pre * pre
                slant = jnp.tanh(0.7978845608028654 * pre * (1.0 + 0.044715 * square))
                half = 0.5 * (1.0 + slant)
                act_now[:, lanes] = (pre * half).astype(BF16)
                slope[:, lanes] = half + 0.5 * pre * (1.0 - slant * slant) * (
                    0.7978845608028654 * (1.0 + 0.134145 * square)
                )
            if step % 2:
                pair = step // 2
                right_act[act_rows(pair), here_lc] = act_stage[0]
                links.send(
                    ("act", "l", pair),
                    "l",
                    lambda pair=pair: (
                        act_stage.at[1 + pair], right_act.at[act_rows(pair), here_lc]
                    ),
                )
                links.send(
                    ("act", "c", pair),
                    "c",
                    lambda pair=pair: (
                        right_act.at[act_rows(pair), here_lc],
                        right_act.at[act_rows(pair), here_lc],
                    ),
                )
            down = ring.get(5 + 2 * step)
            for tile in range(3):
                lanes = pl.ds(tile * 384, 384)
                g_pre = (dot_rows(g_branch[...], down[lanes, :]) * slope[:, lanes]).astype(BF16)
                sums[pl.ds(10 + index, 1), lanes] = sum_rows(g_pre.astype(F32))
                if step < 3:
                    pre_stage[step, :, lanes] = g_pre
                else:
                    right_u[here, lanes] = g_pre
            if step < 3:
                g_pre_ref = pre_stage.at[step]
                links.send(
                    ("u", NEAR[step]),
                    NEAR[step],
                    lambda step=step: (pre_stage.at[step], right_u.at[here]),
                )
                if step == 1:
                    send_a(1)
            else:
                g_pre_ref = right_u.at[here]
            new_mod = dot_rows(g_pre_ref[...], up[...])
            g_mod[...] = new_mod + g_mod[...] if step else new_mod
            ring.done(4 + 2 * step)
            new_branch = dot(act_now[...], down[...])
            branch[...] = new_branch + (branch[...] if step else bias(8 * D))
            ring.done(5 + 2 * step)
            if step == 1:
                forward_t()
            if step == 2:
                forward_a(0)
        zero = jnp.zeros((1, D), F32)
        gate_m_sum = scale_m_sum = shift_m_sum = gate_a_sum = proj_sum = zero
        for rows in row_tiles:
            cotangent = out_grad[0, rows, :].astype(F32) * live_factor
            mixed[rows, :] = (after[rows, :] + mod(gate_m) * branch[rows, :]).astype(BF16)
            gate_m_sum += sum_rows(cotangent * branch[rows, :])
            normed, inverse = norm_rows(after[rows, :])
            grads = g_mod[rows, :]
            shift_m_sum += sum_rows(grads)
            scale_m_sum += sum_rows(grads * normed)
            g_after = cotangent + norm_back(grads * (1.0 + mod(scale_m)), normed, inverse)
            grad_hidden[rows, :] = g_after
            gate_a_sum += sum_rows(g_after * attn_out[rows, :])
            g_attn = (g_after * mod(gate_a)).astype(BF16)
            natural[rows, :] = g_attn
            proj_sum += sum_rows(g_attn.astype(F32))
        local("mixed", mixed, mixed_hbm).start()
        sums[2:3] = gate_a_sum
        sums[3:4] = shift_m_sum
        sums[4:5] = scale_m_sum
        sums[5:6] = gate_m_sum
        sums[8:9] = proj_sum

    spot_x, spot_y = spot(place.m_at("x")), spot(place.pair_at("y", "y"))
    spot_l = spot(place.pair_at("l", "l"))

    def forward_m():
        links.arrived(("m", "x"))
        links.send(("m", "f"), "c", lambda: (left_m.at[:, spot_x], left_m.at[:, spot_x]))

    def forward_a(half):
        def ends():
            part = left_a.at[pl.ds(half * 576, 576), spot_x]
            return part, part

        links.arrived(("a", "x", half))
        links.send(("a", "f", half), "c", ends)

    def forward_t():
        links.arrived(("t", "y"))
        links.send(
            ("t", "f"), "c", lambda: (left_t.at[:, :, spot_y], left_t.at[:, :, spot_y])
        )

    def forward_act(pair):
        def target():
            return right_act.at[act_rows(pair), spot_l]

        links.arrived(("act", "l", pair))
        links.send(("act", "f", pair), "c", lambda: (target(), target()))

    scatter_d = Scatter(links, "d", "xyh", grad_d, first_d, second_d, third_d)
    scatter_u = Scatter(links, "u", "ylh", grad_u, first_u, second_u, third_u)
    scatter_t = Scatter(links, "t", "lxh", grad_t, first_t, second_t, third_t)

    def form_down():
        for to in ("l", "c", "lc"):
            for x in range(2):
                links.arrived(("gb", to, x))
        for pair in range(2):
            links.arrived(("act", "c", pair))
            links.arrived(("act", "f", pair))
        for b0 in (1, 0):
            for b2 in (1, 0):
                there = place.flipped("x" * b0 + "h" * b2)
                wide = dot(left_b[there["x"]], right_act[there["h"]]).astype(BF16)
                for y in range(2):
                    block = wide[:, 576 * y : 576 * y + 576]
                    other = 1 - bits["y"] if y else bits["y"]
                    grad_d[b0, other, b2] = jnp.concatenate(
                        [block[:BLOCK], block[BLOCK:]], axis=1
                    )
            if b0:
                scatter_d.send_first(*ORDER)

    def grad_rows(flips):
        return pl.ds(pl.multiple_of(place.h_at(flips) * BLOCK, BLOCK), BLOCK)

    def form_up():
        for to in NEAR:
            links.arrived(("u", to))
        links.arrived(("m", "c"))
        links.arrived(("m", "f"))
        for b0 in (1, 0):
            for b1, b2 in ORDER:
                rows = grad_rows("y" * b0 + "l" * b1 + "h" * b2)
                grad_u[b0, b1, b2] = dot(left_m[rows, :], right_u[...]).astype(BF16)
                if b0:
                    scatter_u.send_first((b1, b2))

    def form_proj():
        for to in ("y", "c", "yc"):
            links.arrived(("ga", to))
        for to in ("c", "f"):
            links.arrived(("t", to))
        for b0 in (1, 0):
            for b2 in (1, 0):
                there = place.flipped("l" * b0 + "h" * b2)
                wide = dot(left_t[there["h"] * 2 + there["l"]], right_t[...]).astype(BF16)
                for x in range(2):
                    other = 1 - bits["x"] if x else bits["x"]
                    grad_t[b0, other, b2, :, :288] = wide[:, 288 * x : 288 * x + 288]
            if b0:
                scatter_t.send_first(*ORDER)

    def attention_back(g_qkv, q_stage, ga_stage):
        g_attn = natural[...]
        columns = [
            jnp.concatenate(
                [
                    g_attn[:, 288 * core : 288 * core + 288],
                    g_attn[:, 576 + 288 * core : 864 + 288 * core],
                    jnp.zeros((SEQ, 64), BF16),
                ],
                axis=1,
            )
            for core in range(2)
        ]
        ga_stage[...] = jnp.where(bits["c"] == 0, columns[1], columns[0])
        right_t[here_yc, :] = jnp.where(bits["c"] == 0, columns[0], columns[1])
        for to in ("y", "yc", "c"):
            links.send(
                ("ga", to),
                to,
                lambda to=to: (
                    right_t.at[here_yc] if to == "y" else ga_stage,
                    right_t.at[here_yc],
                ),
            )
        part = ring.get(12)
        g_att = g_branch
        g_att[...] = dot_rows(natural[...], part[...]).astype(BF16)
        ring.done(12)

        def back(group, carry):
            heads = [group * TOGETHER + index for index in range(TOGETHER)]
            windows, insides, queries, probs = head_probs(qkv, heads)
            grads = each(lambda at, inside: jnp.where(inside, g_att[:, at], 0), windows, insides)
            g_probs = each(lambda grad, at: dot_rows(grad, qkv[2, :, at]), grads, windows)
            g_values = each(lambda prob, grad: dot(prob.astype(BF16).T, grad), probs, grads)
            row_dots = each(
                lambda prob, g_prob: jnp.sum(prob * g_prob, axis=-1, keepdims=True), probs, g_probs
            )
            g_scores = each(
                lambda prob, g_prob, row_dot: (prob * (g_prob - row_dot)).astype(BF16),
                probs,
                g_probs,
                row_dots,
            )
            g_queries = each(lambda g, at: dot(g, qkv[1, :, at]) * SCALE, g_scores, windows)
            g_keys = each(lambda g, query: dot(g.T, query) * SCALE, g_scores, queries)
            for index, values in enumerate((g_queries, g_keys, g_values)):
                for at, inside, value in zip(windows, insides, values):
                    g_qkv[index, :, at] = jnp.where(
                        inside, value.astype(BF16), g_qkv[index, :, at]
                    )
            return carry

        groups = HEADS // TOGETHER
        lax.fori_loop(0, groups // 2, back, 0)
        forward_act(0)
        lax.fori_loop(groups // 2, groups, back, 0)
        for index in range(GROUP):
            start, pieces = index * 864, []
            while start < index * 864 + 864:
                stop = min(index * 864 + 864, (start // D + 1) * D)
                pieces.append(g_qkv[start // D][:, start % D : start % D + stop - start])
                start = stop
            q_stage[index] = jnp.concatenate(pieces + [jnp.zeros((SEQ, 32), BF16)], axis=1)
        right_q[here, :] = q_stage[m_here]
        sums[6:7] = sum_rows(g_qkv[0].astype(F32))
        sums[7:8] = sum_rows(g_qkv[2].astype(F32))
        for index in range(3):
            part = ring.get(13 + index)
            product = dot_rows(g_qkv[index], part[...])
            attn_out[...] = attn_out[...] + product if index else product
        zero = jnp.zeros((1, D), F32)
        shift_sum = scale_sum = zero
        for rows in row_tiles:
            normed, inverse = norm_rows(hidden[0, rows, :].astype(F32))
            grads = attn_out[rows, :]
            shift_sum += sum_rows(grads)
            scale_sum += sum_rows(grads * normed)
            grad_hidden[rows, :] = grad_hidden[rows, :] + norm_back(
                grads * (1.0 + mod(scale_a)), normed, inverse
            )
        local("grad_hidden", grad_hidden, grad_hidden_hbm).start()
        sums[0:1] = shift_sum
        sums[1:2] = scale_sum
        send_rows()
        for to in NEAR:
            links.send(
                ("q", to), to, lambda to=to: (q_stage.at[place.m_at(to)], right_q.at[here])
            )
        forward_act(1)
        forward_m()
        form_proj()
        form_down()
        form_up()
        gather_rows()
        scatter_u.send_second(1)
        forward_a(1)
        for b2 in (1, 0):
            scatter_t.send_second(b2)
        scatter_u.send_third()
        scatter_u.send_second(0)
        for to in NEAR:
            links.left(("q", to))
        for to in ("y", "yc", "c"):
            links.left(("ga", to))

    def reduce_rest(
        grad_q, ada, spread, cond_all, cond_stage, out_ada, out_qkv, out_proj, out_up, out_down
    ):
        scatter_q = Scatter(links, "q", "ylh", grad_q, first_q, second_q, third_q)
        load = local("ada_back", ada_w, ada)
        load.start()
        for to in NEAR:
            links.arrived(("q", to))
        for half in range(2):
            for to in ("c", "f"):
                links.arrived(("a", to, half))
        for b0 in (1, 0):
            for b1, b2 in ORDER:
                rows = grad_rows("y" * b0 + "l" * b1 + "h" * b2)
                grad_q[b0, b1, b2] = dot(left_a[rows, :], right_q[...]).astype(BF16)
                if b0 and (b1, b2) in EARLY:
                    scatter_q.send_first((b1, b2))
        scatter_d.send_second(1)
        scatter_q.send_first(*LATE)
        scatter_q.send_second(1)
        scatter_q.send_third()
        scatter_d.send_third()
        ada_grads(load, ada, spread, cond_all, cond_stage, out_ada)
        scatter_d.send_second(0)
        scatter_q.send_second(0)
        scatter_t.send_third()
        finish_cond(cond_all)
        total = scatter_d.total()
        out_down[:BLOCK, :] = total[:, :576]
        out_down[BLOCK:, :] = total[:, 576:]
        out_proj[...] = scatter_t.total()[:, :288]
        out_up[...] = scatter_u.total()
        results = [
            local("down", out_down, down_hbm),
            local("proj", out_proj, proj_hbm),
            local("up", out_up, up_hbm),
            local("qkv", out_qkv, qkv_hbm),
        ]
        for copy in results[:3]:
            copy.start()
        out_qkv[...] = scatter_q.total()[:, :864]
        results[3].start()
        results.append(local("mixed", mixed, mixed_hbm))
        results.append(local("grad_hidden", grad_hidden, grad_hidden_hbm))
        results.append(local("ada", out_ada, ada_hbm))
        links.drain()
        for copy in results:
            copy.wait()

    def send_rows():
        grads = jnp.concatenate([sums[index : index + 1] for index in range(6)], axis=1)
        qv = jnp.concatenate([sums[6:7], sums[7:8]], axis=1)
        for index in range(GROUP):
            row = jnp.concatenate(
                [
                    grads[:, ADA * index : ADA * index + ADA],
                    jnp.zeros((1, 64), F32),
                    qv[:, 576 * index : 576 * index + 576],
                    sums[8:9][:, 288 * index : 288 * index + 288],
                    sums[10 + index : 11 + index],
                    sums[9:10][:, 288 * index : 288 * index + 288],
                ],
                axis=1,
            )
            row_stage[index] = row.reshape(32, 128).astype(BF16)
        for to in NEAR:
            links.send(
                ("row", to),
                to,
                lambda to=to: (row_stage.at[place.m_at(to)], row_group.at[m_here]),
            )
        row_group[m_here] = row_stage[m_here]

    def gather_rows():
        for to in NEAR:
            links.arrived(("row", to))
        for index in range(GROUP):
            row_all[place.h_index, 16 * index : 16 * index + 16] = row_group[index, :16]
        biases_here = jnp.sum(row_group[...].astype(F32), axis=0)[14:]
        row_all[place.h_index, 64:96] = jnp.concatenate(
            [biases_here, jnp.zeros((14, 128), F32)], axis=0
        ).astype(BF16)
        for to in FAR:
            links.send(
                ("rows", to), to, lambda: (row_all.at[place.h_index], row_all.at[place.h_index])
            )

    def ada_grads(load, ada, spread, cond_all, cond_stage, out_ada):
        for to in FAR:
            links.arrived(("rows", to))
            links.arrived(("silu", to))
        for to in ("l", "lc", "c"):
            for x in range(2):
                links.left(("gb", to, x))
        images = GROUP * INNER
        spread[...] = silu_all[...].astype(F32).reshape(images * 16, 128)

        def tile(index):
            return spread[pl.ds(index, images, stride=16), :]

        silu_rows = jnp.concatenate([tile(index) for index in range(9)], axis=1)
        gb_t[:, :images] = silu_rows.T.astype(BF16)
        spread[...] = row_all[:, :64].astype(F32).reshape(images * 16, 128)
        columns = jnp.concatenate([tile(index) for index in range(14)], axis=1)[:, :ADA]
        out_ada_b[...] = sum_rows(columns).reshape(ADA)
        columns = columns.astype(BF16)
        rows = pl.ds(pl.multiple_of(place.h_index * BLOCK, BLOCK), BLOCK)
        out_ada[...] = dot(gb_t[rows, :images], columns)
        local("ada", out_ada, ada_hbm).start()
        totals = jnp.sum(row_all[:, 64:96].astype(F32), axis=0)
        totals = jnp.concatenate([totals[index : index + 1] for index in range(18)], axis=1)
        start = 0
        for out in (out_qv_b, out_proj_b, out_up_b, out_down_b):
            width = out.shape[0]
            out[...] = totals[:, start : start + width].reshape(width)
            start += width
        load.wait()
        cond_all[...] = dot(columns, ada[...])
        for to in NEAR:
            row = place.h_index * GROUP + place.m_at(to)
            cond_stage[place.m_at(to)] = jnp.broadcast_to(cond_all[pl.ds(row, 1), :], (8, D))
            links.send(
                ("gc", to), to, lambda to=to: (cond_stage.at[place.m_at(to)], cond_in.at[m_here])
            )

    def finish_cond(cond_all):
        total = cond_all[pl.ds(place.h_index * GROUP + m_here, 1), :]
        for to in NEAR:
            links.arrived(("gc", to))
            total += cond_in[place.m_at(to)][:1]
        values = cond[...].astype(F32)
        sigmoid = jax.nn.sigmoid(values)
        grad_cond[...] = total * (sigmoid * (1.0 + values * (1.0 - sigmoid)))

    def local_work(act_stage, pre_stage):
        f32_rows = pltpu.VMEM((SEQ, D), F32)
        pl.run_scoped(
            partial(feed_forward, act_stage, pre_stage),
            f32_rows,
            f32_rows,
            f32_rows,
        )
        pl.run_scoped(
            attention_back,
            pltpu.VMEM((3, SEQ, D), BF16),
            pltpu.VMEM((GROUP, SEQ, 896), BF16),
            pltpu.VMEM((SEQ, WINDOW), BF16),
        )
        for pair in range(2):
            links.left(("act", "l", pair))
        for to in NEAR:
            links.left(("u", to))

    pl.run_scoped(
        local_work, pltpu.VMEM((3, SEQ, D), BF16), pltpu.VMEM((3, SEQ, D), BF16)
    )
    pl.run_scoped(
        reduce_rest,
        pltpu.VMEM((2, 2, 2, BLOCK, 896), BF16),
        pltpu.VMEM((ADA, D), BF16),
        pltpu.VMEM((GROUP * INNER * 16, 128), F32),
        pltpu.VMEM((GROUP * INNER, D), F32),
        pltpu.VMEM((GROUP, 8, D), F32),
        pltpu.VMEM((BLOCK, ADA), F32),
        pltpu.VMEM((BLOCK, 864), F32),
        pltpu.VMEM((BLOCK, 288), F32),
        pltpu.VMEM((BLOCK, D), F32),
        pltpu.VMEM((288, 576), F32),
    )


TOGETHER = 4


def run_block(outer, *operands):
    vmem = pl.BlockSpec(memory_space=pltpu.VMEM)
    anywhere = pl.BlockSpec(memory_space=pl.ANY)
    smem = pl.BlockSpec(memory_space=pltpu.SMEM)
    scratch = [
        ((1, SEQ, D), BF16),
        ((1, SEQ, D), BF16),
        ((SEQ, D), BF16),
        ((SEQ, D), F32),
        ((1, 9 * D + ADA), F32),
        ((SLOTS, D, D), BF16),
        ((GROUP, 16, D), BF16),
        ((GROUP, 16, 1792), BF16),
        ((8, D), F32),
        ((D, TOKENS), BF16),
        ((4, BLOCK, TOKENS), BF16),
        ((D, TOKENS), BF16),
        ((2, TOKENS, D), BF16),
        ((2, 288, TOKENS), BF16),
        ((TOKENS, D), BF16),
        ((TOKENS, 896), BF16),
        ((TOKENS, WINDOW), BF16),
        ((D, SEQ), BF16),
        ((SEQ, D), BF16),
        ((SEQ, D), BF16),
        ((4, 2, BLOCK, SEQ), BF16),
        ((3, SEQ, D), BF16),
        ((SEQ, D), F32),
        ((16, D), F32),
        ((GROUP, 32, 128), BF16),
        ((GROUP, 32, 128), BF16),
        ((INNER, 96, 128), BF16),
        ((INNER, GROUP, 16, 128), BF16),
        ((GROUP, 8, D), F32),
    ]
    block = (BLOCK, D)
    scratch += [((2, 2, 2) + block, BF16)] * 2
    scratch += [((2, 2) + block, BF16)] * 2 + [((2,) + block, BF16)] * 2 + [(block, BF16)] * 2
    block = (BLOCK, 896)
    scratch += [((2, 2) + block, BF16), ((2,) + block, BF16), (block, BF16)]
    block = (BLOCK, 384)
    scratch += [((2, 2, 2) + block, BF16), ((2, 2) + block, BF16), ((2,) + block, BF16)]
    scratch += [(block, BF16)]
    outs = [
        ((SEQ, D), BF16),
        ((SEQ, D), F32),
        ((1, D), F32),
        ((BLOCK, ADA), F32),
        ((ADA,), F32),
        ((BLOCK, 864), F32),
        ((576,), F32),
        ((BLOCK, 288), F32),
        ((288,), F32),
        ((BLOCK, D), F32),
        ((D,), F32),
        ((288, 576), F32),
        ((288,), F32),
    ]
    outs = [jax.ShapeDtypeStruct(*out) for out in outs]
    small = [vmem if out.shape[0] == 1 or len(out.shape) == 1 else anywhere for out in outs]
    results = pl.pallas_call(
        partial(block_kernel, outer),
        out_shape=outs,
        in_specs=[anywhere, vmem, smem, anywhere] + [vmem] * 5 + [anywhere] * 5,
        out_specs=small,
        scratch_shapes=[pltpu.VMEM(*each) for each in scratch]
        + [
            pltpu.SemaphoreType.DMA((96,)),
            pltpu.SemaphoreType.DMA((96,)),
            pltpu.SemaphoreType.DMA((SLOTS,)),
            pltpu.SemaphoreType.DMA((len(LOCAL),)),
        ],
        compiler_params=pltpu.CompilerParams(
            collective_id=0, has_side_effects=True, vmem_limit_bytes=VMEM_LIMIT
        ),
    )(*operands)
    return pl.pallas_call(
        place_kernel,
        out_shape=outs,
        in_specs=[anywhere] * len(outs),
        out_specs=[anywhere] * len(outs),
        scratch_shapes=[pltpu.VMEM(out.shape, out.dtype) for out in outs]
        + [pltpu.SemaphoreType.DMA((2, len(outs)))],
    )(*results)


VMEM_LIMIT = 63 * 2**20 + 900 * 2**10
LOCAL = (
    "ada_in", "hidden", "out_grad", "mixed", "grad_hidden", "ada_back", "ada", "down", "proj",
    "up", "qkv",
)


def place_kernel(*refs):
    count = len(refs) // 3
    sems = refs[-1]
    here = [
        pltpu.make_async_copy(refs[index], refs[2 * count + index], sems.at[0, index])
        for index in range(count)
    ]
    there = [
        pltpu.make_async_copy(refs[2 * count + index], refs[count + index], sems.at[1, index])
        for index in range(count)
    ]
    for copy in here:
        copy.start()
    for first, second in zip(here, there):
        first.wait()
        second.start()
    for copy in there:
        copy.wait()


def on_device(
    outer,
    hidden_in,
    conditioning,
    live_images,
    out_grad,
    ada_weight,
    ada_bias,
    qkv_weight,
    qv_bias,
    proj_weight,
    proj_bias,
    up_weight,
    up_bias,
    down_weight,
    down_bias,
):
    (
        mixed,
        grad_hidden,
        grad_cond,
        out_ada_w,
        out_ada_b,
        out_qkv_w,
        out_qv_b,
        out_proj_w,
        out_proj_b,
        out_up_w,
        out_up_b,
        out_down_w,
        out_down_b,
    ) = run_block(
        outer,
        hidden_in,
        conditioning,
        live_images,
        out_grad,
        ada_bias,
        qv_bias,
        proj_bias,
        up_bias,
        down_bias,
        ada_weight.T,
        qkv_weight,
        proj_weight,
        up_weight,
        down_weight,
    )
    out_down_w = out_down_w.T
    if outer > 1:
        groups = [[h * outer + low for low in range(outer)] for h in range(INNER)]
        out_ada_w, out_down_w, out_up_w, out_qkv_w, out_proj_w = (
            lax.psum_scatter(
                part, "dp", scatter_dimension=0, tiled=True, axis_index_groups=groups
            )
            for part in (out_ada_w, out_down_w, out_up_w, out_qkv_w, out_proj_w)
        )
        out_ada_b, out_qv_b, out_proj_b, out_up_b, out_down_b = (
            jnp.sum(
                lax.all_gather(part, "dp", axis=0, axis_index_groups=groups), axis=0
            )
            for part in (out_ada_b, out_qv_b, out_proj_b, out_up_b, out_down_b)
        )
    return (
        mixed[None],
        grad_hidden[None],
        grad_cond,
        out_ada_w,
        out_ada_b,
        out_qkv_w,
        out_qv_b,
        out_proj_w,
        out_proj_b,
        out_up_w,
        out_up_b,
        out_down_w,
        out_down_b,
    )


def solution(mesh):
    in_specs = (
        P(("dp", "mp"), None, None),
        P(("dp", "mp"), None),
        P(("dp", "mp")),
        P(("dp", "mp"), None, None),
        P(None, "mp"),
        P("mp"),
        P(),
        P(),
        P(),
        P(),
        P(),
        P(),
        P(),
        P(),
    )
    out_specs = (
        P(("dp", "mp"), None, None),
        P(("dp", "mp"), None, None),
        P(("dp", "mp"), None),
        P("dp", "mp"),
        P("mp"),
        P("dp", "mp"),
        P("mp"),
        P("dp", "mp"),
        P("mp"),
        P("dp", "mp"),
        P("mp"),
        P("dp", "mp"),
        P("mp"),
    )
    return jax.shard_map(
        partial(on_device, mesh.shape["dp"] // INNER),
        mesh=mesh,
        in_specs=in_specs,
        out_specs=out_specs,
        check_vma=False,
    )
```

```python
from functools import partial

import jax
import jax.numpy as jnp
from jax import lax
from jax.experimental import pallas as pl
from jax.experimental.pallas import tpu as pltpu
from jax.sharding import PartitionSpec as P

D = 1152
HEADS = 16
HEAD_DIM = 72
FF = 4608
SEQ = 256
ADA = 1728
MESH_ID = pl.DeviceIdType.MESH
BF16 = jnp.bfloat16
F32 = jnp.float32
INNER = 8
BLOCK = D // INNER
GROUP = 4
TOKENS = GROUP * SEQ
WINDOW = 640
SLOTS = 3
SCALE = HEAD_DIM ** (-0.5)
PEERS = ("c", "x", "xc", "y", "yc", "l", "lc", "h", "yl", "yh", "lh", "ylh")
FAR = ("y", "l", "h", "yl", "yh", "lh", "ylh")
NEAR = ("xc", "x", "c")
ORDER = ((1, 1), (0, 1), (1, 0), (0, 0))
EARLY, LATE = ORDER[:2], ORDER[2:]


def dot(left, right):
    return jnp.dot(left, right, preferred_element_type=F32)


def dot_rows(left, right):
    return lax.dot_general(left, right, (((1,), (1,)), ((), ())), preferred_element_type=F32)


def norm_rows(values):
    center = values - jnp.mean(values, axis=-1, keepdims=True)
    inverse = lax.rsqrt(jnp.mean(center * center, axis=-1, keepdims=True) + 1e-06)
    return center * inverse, inverse


def norm_back(grad_normed, normed, inverse):
    mean_grad = jnp.mean(grad_normed, axis=-1, keepdims=True)
    mean_prod = jnp.mean(grad_normed * normed, axis=-1, keepdims=True)
    return inverse * (grad_normed - mean_grad - normed * mean_prod)


def sum_rows(values):
    return jnp.sum(values, axis=0, keepdims=True)


class Place:
    def __init__(self, outer):
        data, model = lax.axis_index("dp"), lax.axis_index("mp")
        self.outer = outer
        self.low = data % outer
        self.h_index = data // outer
        self.m_index = model
        self.bits = {
            "h": self.h_index // 4,
            "l": (self.h_index // 2) % 2,
            "y": self.h_index % 2,
            "x": model // 2,
            "c": model % 2,
        }

    def flipped(self, names):
        if "p" in names and "r" in names:
            names += "yl"
        bits = {key: (1 - bit if key in names else bit) for key, bit in self.bits.items()}
        if ("p" in names) != ("r" in names):
            second = bits["c"] if "p" in names else 1 - bits["c"]
            bits["y"] += second * (1 - 2 * bits["y"])
            bits["l"] += (1 - second) * (1 - 2 * bits["l"])
        return bits

    def h_at(self, names):
        bits = self.flipped(names)
        return bits["h"] * 4 + bits["l"] * 2 + bits["y"]

    def m_at(self, names):
        bits = self.flipped(names)
        return bits["x"] * 2 + bits["c"]

    def pair_at(self, axis, names):
        bits = self.flipped(names)
        return bits[axis] * 2 + bits["c"]

    def device(self, names):
        return (self.h_at(names) * self.outer + self.low, self.m_at(names))


class Links:
    def __init__(self, place, send_sems, recv_sems):
        self.place = place
        self.send_sems = send_sems
        self.recv_sems = recv_sems
        self.builders = {}
        self.gone = set()

    def send(self, name, to, ends):
        self.plan(name, to, ends)
        self.start(name)

    def start(self, name):
        self.builders[name]().start()

    def plan(self, name, to, ends):
        index = len(self.builders)

        def build(landed=False):
            source, target = ends()
            if landed:
                source = target
            return pltpu.make_async_remote_copy(
                src_ref=source,
                dst_ref=target,
                send_sem=self.send_sems.at[index],
                recv_sem=self.recv_sems.at[index],
                device_id=self.place.device(to),
                device_id_type=MESH_ID,
            )

        self.builders[name] = build

    def arrived(self, name):
        self.builders[name](landed=True).wait_recv()

    def left(self, name):
        self.gone.add(name)
        self.builders[name]().wait_send()

    def drain(self):
        for name in self.builders:
            if name not in self.gone:
                self.left(name)


class Ring:
    def __init__(self, parts, slots, sems):
        self.parts = parts
        self.slots = slots
        self.sems = sems

    def begin(self):
        for index in range(SLOTS):
            self.start(index)

    def copy(self, index):
        slot = index % SLOTS
        return pltpu.make_async_copy(self.parts[index], self.slots.at[slot], self.sems.at[slot])

    def start(self, index):
        if index < len(self.parts):
            self.copy(index).start()

    def get(self, index):
        self.copy(index).wait()
        return self.slots.at[index % SLOTS]

    def done(self, index):
        self.start(index + SLOTS)


class Scatter:
    def __init__(self, links, name, axes, lanes, grad, first, second, third):
        self.links, self.name, self.axes = links, name, axes
        self.lanes = pl.ds(*lanes)
        self.grad, self.first, self.second, self.third = grad, first, second, third
        for b1, b2 in ORDER:
            links.plan(
                (name, 0, b1, b2),
                axes[0],
                lambda b1=b1, b2=b2: (self.cut(grad, 1, b1, b2), self.cut(first, b1, b2)),
            )
        for b2 in range(2):
            links.plan(
                (name, 1, b2),
                axes[1],
                lambda b2=b2: (self.cut(grad, 0, 1, b2), self.cut(second, b2)),
            )
        links.plan((name, 2), axes[2], lambda: (self.cut(grad, 0, 0, 1), self.cut(third)))

    def cut(self, ref, *index):
        return ref.at[index + (slice(None), self.lanes)]

    def read(self, ref, *index):
        return self.cut(ref, *index)[...].astype(F32)

    def write(self, value, *index):
        self.grad[index + (slice(None), self.lanes)] = value.astype(BF16)

    def send_first(self, *pairs):
        for b1, b2 in pairs:
            self.links.start((self.name, 0, b1, b2))

    def send_second(self, *ends):
        for b2 in ends:
            self.links.arrived((self.name, 0, 1, b2))
            self.write(self.read(self.grad, 0, 1, b2) + self.read(self.first, 1, b2), 0, 1, b2)
            self.links.start((self.name, 1, b2))

    def send_third(self):
        self.links.arrived((self.name, 0, 0, 1))
        self.links.arrived((self.name, 1, 1))
        total = self.read(self.grad, 0, 0, 1) + self.read(self.first, 0, 1)
        self.write(total + self.read(self.second, 1), 0, 0, 1)
        self.links.start((self.name, 2))

    def send_rest(self, outer):
        @pl.when(outer == 0)
        def _():
            self.send_third()
            self.send_second(0)

        @pl.when(outer == 1)
        def _():
            self.send_second(0)
            self.send_third()

    def total(self):
        self.links.arrived((self.name, 0, 0, 0))
        self.links.arrived((self.name, 1, 0))
        self.links.arrived((self.name, 2))
        return (
            self.read(self.grad, 0, 0, 0)
            + self.read(self.first, 0, 0)
            + self.read(self.second, 0)
            + self.read(self.third)
        )


def head_window(head):
    start = (head * 9) // 16 - head // 15
    offset = head * HEAD_DIM - start * 128
    lanes = lax.broadcasted_iota(jnp.int32, (SEQ, 256), 1)
    inside = (lanes >= offset) & (lanes < offset + HEAD_DIM)
    return pl.ds(pl.multiple_of(start * 128, 128), 256), inside


def each(function, *lists):
    return [function(*items) for items in zip(*lists)]


def head_probs(qkv, heads):
    windows, insides = zip(*each(head_window, heads))
    queries = each(lambda at, inside: jnp.where(inside, qkv[0, :, at], 0), windows, insides)
    scores = each(lambda query, at: dot_rows(query, qkv[1, :, at]), queries, windows)
    tops = each(lambda score: jnp.max(score, axis=-1, keepdims=True), scores)
    shifted = each(lambda score, top: jnp.exp((score - top) * SCALE), scores, tops)
    totals = each(lambda value: 1.0 / jnp.sum(value, axis=-1, keepdims=True), shifted)
    probs = each(lambda value, total: value * total, shifted, totals)
    return windows, insides, queries, probs


def block_kernel(
    outer,
    hidden_hbm,
    cond,
    live,
    out_grad_hbm,
    ada_bias,
    qv_bias,
    proj_bias,
    up_bias,
    down_bias,
    ada_w,
    qkv_w,
    proj_w,
    up_w,
    down_w,
    mixed_hbm,
    grad_hidden_hbm,
    grad_cond,
    ada_hbm,
    out_ada_b,
    qkv_hbm,
    out_qv_b,
    proj_hbm,
    out_proj_b,
    up_hbm,
    out_up_b,
    down_hbm,
    out_down_b,
    hidden,
    out_grad,
    mixed,
    grad_hidden,
    biases,
    ring_slots,
    cond_rows,
    mod_in,
    mods,
    left_a,
    left_t,
    left_m,
    right_act,
    left_b,
    right_u,
    right_q,
    right_t,
    gb_t,
    g_branch,
    natural,
    att_t,
    qkv,
    attn_out,
    sums,
    row_stage,
    row_group,
    row_all,
    silu_all,
    cond_in,
    grad_d,
    grad_u,
    first_d,
    first_u,
    second_d,
    second_u,
    third_d,
    third_u,
    grad_q,
    first_q,
    second_q,
    third_q,
    grad_t,
    first_t,
    second_t,
    third_t,
    send_sems,
    recv_sems,
    ring_sems,
    local_sems,
):
    place = Place(outer)
    bits = place.bits
    m_here = place.m_index
    links = Links(place, send_sems, recv_sems)

    on_end = 1 - bits["h"] - bits["l"] + 2 * bits["h"] * bits["l"]

    def spot(index):
        return pl.ds(pl.multiple_of(index * SEQ, SEQ), SEQ)

    here, here_yc, here_lc = spot(m_here), spot(place.pair_at("y", "")), spot(place.pair_at("l", ""))
    ff_order = [place.m_at(to) for to in NEAR] + [m_here]

    def ff_part(index):
        return pl.ds(pl.multiple_of(index * D, D), D)

    qkv_parts = [qkv_w.at[:, pl.ds(index * D, D)] for index in range(3)]
    ff_parts = []
    for index in ff_order:
        ff_parts += [up_w.at[:, ff_part(index)], down_w.at[ff_part(index), :]]
    def local(name, source, target):
        return pltpu.make_async_copy(source, target, local_sems.at[LOCAL.index(name)])

    barrier = pltpu.get_barrier_semaphore()
    for names in PEERS:
        pl.semaphore_signal(
            barrier, inc=1, device_id=place.device(names), device_id_type=MESH_ID
        )
    ring = Ring(qkv_parts + [proj_w] + ff_parts + [proj_w] + qkv_parts, ring_slots, ring_sems)
    row_tiles = [pl.ds(start, 64) for start in range(0, SEQ, 64)]

    def bias(start, width=D):
        return biases[:, pl.ds(start, width)]

    def modulation(ada, mod_out):
        silu_row = jax.nn.silu(cond[...].astype(F32))
        cond_rows[m_here] = jnp.broadcast_to(silu_row, (16, D)).astype(BF16)
        load = local("ada_in", ada_w, ada)
        load.start()
        pl.semaphore_wait(barrier, len(PEERS))
        for to in NEAR:
            links.send(("cond", to), to, lambda: (cond_rows.at[m_here], cond_rows.at[m_here]))
        copy_in = local("hidden", hidden_hbm, hidden)
        copy_in.start()
        ring.begin()
        for start, part in ((2, qv_bias), (3, proj_bias), (4, up_bias), (8, down_bias), (9, ada_bias)):
            row = part[...].astype(F32)[None, :]
            if start == 2:
                biases[:, : 2 * D] = jnp.concatenate([row[:, :D], jnp.zeros((1, D), F32)], axis=1)
                row = row[:, D:]
            biases[:, start * D : start * D + row.shape[1]] = row
        copy_in.wait()
        local("out_grad", out_grad_hbm, out_grad).start()
        for rows in row_tiles:
            grad_hidden[rows, :] = norm_rows(hidden[0, rows, :].astype(F32))[0]
        load.wait()
        for to in NEAR:
            links.arrived(("cond", to))
        columns = dot_rows(cond_rows[...].reshape(64, D), ada[...]) + bias(9 * D, ADA)
        mod_out[:, :, :ADA] = columns.astype(BF16).reshape(GROUP, 16, ADA)
        for to in NEAR:
            links.send(
                ("mod", to), to, lambda to=to: (mod_out.at[place.m_at(to)], mod_in.at[m_here])
            )
        mod_in[m_here] = mod_out[m_here]
        for to in NEAR:
            links.left(("mod", to))

    def send_silu():
        for index in range(GROUP):
            silu_row = cond_rows[index].astype(F32)[:1]
            tiles = silu_row.reshape(9, 128)
            silu_all[place.h_index, index] = jnp.concatenate(
                [tiles, jnp.zeros((7, 128), F32)], axis=0
            ).astype(BF16)
        for to in FAR:
            links.send(
                ("silu", to),
                to,
                lambda: (silu_all.at[place.h_index], silu_all.at[place.h_index]),
            )

    pl.run_scoped(
        modulation, pltpu.VMEM((ADA, D), BF16), pltpu.VMEM((GROUP, 16, 1792), BF16)
    )
    for to in NEAR:
        links.arrived(("mod", to))
    parts = [mod_in[index].astype(F32)[:1] for index in range(GROUP)]
    for index in range(2):
        low, high = parts[2 * index], parts[2 * index + 1]
        mods[3 * index : 3 * index + 1] = low[:, :D]
        mods[3 * index + 1 : 3 * index + 2] = jnp.concatenate(
            [low[:, D:ADA], high[:, : D // 2]], axis=1
        )
        mods[3 * index + 2 : 3 * index + 3] = high[:, D // 2 : ADA]
    shift_a, scale_a, gate_a, shift_m, scale_m, gate_m = range(6)

    def mod(index):
        return mods[index : index + 1]

    live_factor = live[0].astype(F32)
    local("out_grad", out_grad_hbm, out_grad).wait()
    for rows in row_tiles:
        natural[rows, :] = (
            grad_hidden[rows, :] * (1.0 + mod(scale_a)) + mod(shift_a)
        ).astype(BF16)
        g_branch[rows, :] = (
            out_grad[0, rows, :].astype(F32) * live_factor * mod(gate_m)
        ).astype(BF16)
    left_a[:, here] = natural[...].T

    def send_a(half):
        def ends():
            part = left_a.at[pl.ds(half * 576, 576), here]
            return part, part

        for to in ("x", "c"):
            links.send(("a", to, half), to, ends)

    send_a(0)
    gb_t[...] = g_branch[...].T

    def gb_rows(to, x):
        return pl.ds(pl.multiple_of((2 * x + place.flipped(to)["c"]) * 288, 288), 288)

    for to in ("l", "lc", "c"):
        for x in range(2):
            links.send(
                ("gb", to, x),
                to,
                lambda to=to, x=x: (gb_t.at[gb_rows(to, x), :], left_b.at[x, :, here_lc]),
            )
    for x in range(2):
        left_b[x, :, here_lc] = gb_t[gb_rows("", x), :]
    sums[9:10] = sum_rows(g_branch[...].astype(F32))
    send_silu()

    for index in range(3):
        part = ring.get(index)
        qkv[index] = (dot(natural[...], part[...]) + bias(index * D)).astype(BF16)
        ring.done(index)

    def attend(group, carry):
        heads = [group * TOGETHER + index for index in range(TOGETHER)]
        windows, insides, _, probs = head_probs(qkv, heads)
        values = each(
            lambda prob, at: dot(prob.astype(BF16), qkv[2, :, at]).astype(BF16), probs, windows
        )
        for at, inside, value in zip(windows, insides, values):
            natural[:, at] = jnp.where(inside, value, natural[:, at])
        return carry

    lax.fori_loop(0, HEADS // TOGETHER, attend, 0)
    att_t[...] = natural[...].T.reshape(4, 2, BLOCK, SEQ)
    for to in ("y", "c"):
        links.send(
            ("t", to),
            to,
            lambda to=to: (
                att_t.at[:, place.flipped("y" if to == "y" else "")["y"]],
                left_t.at[:, :, here_yc],
            ),
        )
    left_t[:, :, here_yc] = att_t[:, bits["y"]]
    part = ring.get(3)
    attn_out[...] = dot(natural[...], part[...]) + bias(3 * D)
    ring.done(3)

    def act_rows(pair):
        return bits["x"] if pair else 1 - bits["x"]

    def feed_forward(act_stage, pre_stage, after, branch, g_mod):
        slope = grad_hidden
        for rows in row_tiles:
            after[rows, :] = hidden[0, rows, :].astype(F32) + mod(gate_a) * attn_out[rows, :]
            normed, _ = norm_rows(after[rows, :])
            natural[rows, :] = (normed * (1.0 + mod(scale_m)) + mod(shift_m)).astype(BF16)
        left_m[:, here] = natural[...].T
        for to in ("x", "c"):
            links.send(("m", to), to, lambda: (left_m.at[:, here], left_m.at[:, here]))
        for step in range(4):
            index = ff_order[step]
            up = ring.get(4 + 2 * step)
            parity = index % 2
            away = parity + bits["l"] - 2 * parity * bits["l"]
            act_now = act_stage.at[away * (1 + step // 2)]
            for tile in range(3):
                lanes = pl.ds(tile * 384, 384)
                offset = pl.multiple_of(4 * D + index * D + tile * 384, 128)
                pre = dot(natural[...], up[:, lanes]) + biases[:, pl.ds(offset, 384)]
                square = pre * pre
                slant = jnp.tanh(0.7978845608028654 * pre * (1.0 + 0.044715 * square))
                half = 0.5 * (1.0 + slant)
                act_now[:, lanes] = (pre * half).astype(BF16)
                slope[:, lanes] = half + 0.5 * pre * (1.0 - slant * slant) * (
                    0.7978845608028654 * (1.0 + 0.134145 * square)
                )
            if step % 2:
                pair = step // 2
                right_act[act_rows(pair), here_lc] = act_stage[0]
                links.send(
                    ("act", "l", pair),
                    "l",
                    lambda pair=pair: (
                        act_stage.at[1 + pair], right_act.at[act_rows(pair), here_lc]
                    ),
                )
                links.send(
                    ("act", "c", pair),
                    "c",
                    lambda pair=pair: (
                        right_act.at[act_rows(pair), here_lc],
                        right_act.at[act_rows(pair), here_lc],
                    ),
                )
            down = ring.get(5 + 2 * step)
            for tile in range(3):
                lanes = pl.ds(tile * 384, 384)
                g_pre = (dot_rows(g_branch[...], down[lanes, :]) * slope[:, lanes]).astype(BF16)
                sums[pl.ds(10 + index, 1), lanes] = sum_rows(g_pre.astype(F32))
                if step < 3:
                    pre_stage[step, :, lanes] = g_pre
                else:
                    right_u[here, lanes] = g_pre
            if step < 3:
                g_pre_ref = pre_stage.at[step]
                for part in range(2):
                    lanes = pl.ds(*UP_LANES[part])
                    links.plan(
                        ("u", NEAR[step], part),
                        NEAR[step],
                        lambda step=step, lanes=lanes: (
                            pre_stage.at[step, :, lanes], right_u.at[here, lanes]
                        ),
                    )
                for to, part in ((("xc", 0),), (("x", 0), ("xc", 1), ("x", 1)), (("c", 0), ("c", 1)))[step]:
                    links.start(("u", to, part))
                if step == 1:
                    send_a(1)
            else:
                g_pre_ref = right_u.at[here]
            new_mod = dot_rows(g_pre_ref[...], up[...])
            g_mod[...] = new_mod + g_mod[...] if step else new_mod
            ring.done(4 + 2 * step)
            new_branch = dot(act_now[...], down[...])
            branch[...] = new_branch + (branch[...] if step else bias(8 * D))
            ring.done(5 + 2 * step)
            if step == 1:
                forward_t()
            if step == 2:
                forward_a(0)
            if step == 3:
                forward_m()
        zero = jnp.zeros((1, D), F32)
        gate_m_sum = scale_m_sum = shift_m_sum = gate_a_sum = proj_sum = zero
        for rows in row_tiles:
            cotangent = out_grad[0, rows, :].astype(F32) * live_factor
            mixed[rows, :] = (after[rows, :] + mod(gate_m) * branch[rows, :]).astype(BF16)
            gate_m_sum += sum_rows(cotangent * branch[rows, :])
            normed, inverse = norm_rows(after[rows, :])
            grads = g_mod[rows, :]
            shift_m_sum += sum_rows(grads)
            scale_m_sum += sum_rows(grads * normed)
            g_after = cotangent + norm_back(grads * (1.0 + mod(scale_m)), normed, inverse)
            grad_hidden[rows, :] = g_after
            gate_a_sum += sum_rows(g_after * attn_out[rows, :])
            g_attn = (g_after * mod(gate_a)).astype(BF16)
            natural[rows, :] = g_attn
            proj_sum += sum_rows(g_attn.astype(F32))
        local("mixed", mixed, mixed_hbm).start()
        sums[2:3] = gate_a_sum
        sums[3:4] = shift_m_sum
        sums[4:5] = scale_m_sum
        sums[5:6] = gate_m_sum
        sums[8:9] = proj_sum

    spot_x, spot_y = spot(place.m_at("x")), spot(place.pair_at("y", "y"))
    spot_l = spot(place.pair_at("l", "l"))

    def forward_m():
        links.arrived(("m", "x"))
        links.send(("m", "f"), "c", lambda: (left_m.at[:, spot_x], left_m.at[:, spot_x]))

    def forward_a(half):
        def ends():
            part = left_a.at[pl.ds(half * 576, 576), spot_x]
            return part, part

        links.arrived(("a", "x", half))
        links.send(("a", "f", half), "c", ends)

    def forward_t():
        links.arrived(("t", "y"))
        links.send(
            ("t", "f"), "c", lambda: (left_t.at[:, :, spot_y], left_t.at[:, :, spot_y])
        )

    def forward_act(pair):
        def target():
            return right_act.at[act_rows(pair), spot_l]

        links.arrived(("act", "l", pair))
        links.send(("act", "f", pair), "c", lambda: (target(), target()))

    scatter_d = Scatter(links, "d", "xyh", (0, D), grad_d, first_d, second_d, third_d)
    scatter_t = Scatter(links, "t", "lxh", (0, 896), grad_t, first_t, second_t, third_t)
    scatter_u = [
        Scatter(links, ("u", part), axes, lanes, grad_u, first_u, second_u, third_u)
        for part, (axes, lanes) in enumerate(zip(UP_AXES, UP_LANES))
    ]
    scatter_q = [
        Scatter(links, ("q", part), axes, lanes, grad_q, first_q, second_q, third_q)
        for part, (axes, lanes) in enumerate(zip(QKV_AXES, QKV_LANES))
    ]

    def form_down():
        for to in ("l", "c", "lc"):
            for x in range(2):
                links.arrived(("gb", to, x))
        for pair in range(2):
            links.arrived(("act", "c", pair))
            links.arrived(("act", "f", pair))
        for b0 in (1, 0):
            for b2 in (1, 0):
                there = place.flipped("x" * b0 + "h" * b2)
                wide = dot(left_b[there["x"]], right_act[there["h"]]).astype(BF16)
                for y in range(2):
                    block = wide[:, 576 * y : 576 * y + 576]
                    other = 1 - bits["y"] if y else bits["y"]
                    grad_d[b0, other, b2] = jnp.concatenate(
                        [block[:BLOCK], block[BLOCK:]], axis=1
                    )
            if b0:
                scatter_d.send_first(EARLY[0])

    def grad_rows(flips):
        return pl.ds(pl.multiple_of(place.h_at(flips) * BLOCK, BLOCK), BLOCK)

    def form_up(part):
        for to in NEAR:
            links.arrived(("u", to, part))
        if part == 0:
            links.arrived(("m", "c"))
            links.arrived(("m", "f"))
        lanes = pl.ds(*UP_LANES[part])
        for b0 in (1, 0):
            for b1, b2 in ORDER:
                axes = scatter_u[part].axes
                rows = grad_rows(axes[0] * b0 + axes[1] * b1 + axes[2] * b2)
                grad_u[b0, b1, b2, :, lanes] = dot(left_m[rows, :], right_u[:, lanes]).astype(BF16)
                if b0:
                    scatter_u[part].send_first((b1, b2))

    def form_qkv(part, pairs):
        for to in NEAR:
            links.arrived(("q", to, part))
        if part == 0:
            for half in range(2):
                for to in ("c", "f"):
                    links.arrived(("a", to, half))
        lanes = pl.ds(*QKV_LANES[part])
        for b0 in (1, 0):
            for b1, b2 in ORDER:
                axes = scatter_q[part].axes
                rows = grad_rows(axes[0] * b0 + axes[1] * b1 + axes[2] * b2)
                grad_q[b0, b1, b2, :, lanes] = dot(left_a[rows, :], right_q[:, lanes]).astype(BF16)
                if b0 and (b1, b2) in pairs:
                    scatter_q[part].send_first((b1, b2))

    def form_proj():
        for to in ("y", "c", "yc"):
            links.arrived(("ga", to))
        for to in ("c", "f"):
            links.arrived(("t", to))
        for b0 in (1, 0):
            for b2 in (1, 0):
                there = place.flipped("l" * b0 + "h" * b2)
                wide = dot(left_t[there["h"] * 2 + there["l"]], right_t[...]).astype(BF16)
                for x in range(2):
                    other = 1 - bits["x"] if x else bits["x"]
                    block = wide[:, 288 * x : 288 * x + 288]
                    grad_t[b0, other, b2, :, :864] = jnp.concatenate(
                        [block[:48], block[48:96], block[96:]], axis=1
                    )

    def attention_back(g_qkv, q_stage, ga_stage):
        g_attn = natural[...]
        columns = [
            jnp.concatenate(
                [
                    g_attn[:, 288 * core : 288 * core + 288],
                    g_attn[:, 576 + 288 * core : 864 + 288 * core],
                    jnp.zeros((SEQ, 64), BF16),
                ],
                axis=1,
            )
            for core in range(2)
        ]
        ga_stage[...] = jnp.where(bits["c"] == 0, columns[1], columns[0])
        right_t[here_yc, :] = jnp.where(bits["c"] == 0, columns[0], columns[1])
        for to in ("y", "yc", "c"):
            links.send(
                ("ga", to),
                to,
                lambda to=to: (
                    right_t.at[here_yc] if to == "y" else ga_stage,
                    right_t.at[here_yc],
                ),
            )
        part = ring.get(12)
        g_att = g_branch
        g_att[...] = dot_rows(natural[...], part[...]).astype(BF16)
        ring.done(12)

        def back(group, carry):
            heads = [group * TOGETHER + index for index in range(TOGETHER)]
            windows, insides, queries, probs = head_probs(qkv, heads)
            grads = each(lambda at, inside: jnp.where(inside, g_att[:, at], 0), windows, insides)
            g_probs = each(lambda grad, at: dot_rows(grad, qkv[2, :, at]), grads, windows)
            g_values = each(lambda prob, grad: dot(prob.astype(BF16).T, grad), probs, grads)
            row_dots = each(
                lambda prob, g_prob: jnp.sum(prob * g_prob, axis=-1, keepdims=True), probs, g_probs
            )
            g_scores = each(
                lambda prob, g_prob, row_dot: (prob * (g_prob - row_dot)).astype(BF16),
                probs,
                g_probs,
                row_dots,
            )
            g_queries = each(lambda g, at: dot(g, qkv[1, :, at]) * SCALE, g_scores, windows)
            g_keys = each(lambda g, query: dot(g.T, query) * SCALE, g_scores, queries)
            for index, values in enumerate((g_queries, g_keys, g_values)):
                for at, inside, value in zip(windows, insides, values):
                    g_qkv[index, :, at] = jnp.where(
                        inside, value.astype(BF16), g_qkv[index, :, at]
                    )
            return carry

        groups = HEADS // TOGETHER
        lax.fori_loop(0, groups // 2, back, 0)
        forward_act(0)
        lax.fori_loop(groups // 2, groups, back, 0)
        sums[6:7] = sum_rows(g_qkv[0].astype(F32))
        sums[7:8] = sum_rows(g_qkv[2].astype(F32))
        form_up(0)
        forward_act(1)
        form_proj()
        scatter_t.send_first(*ORDER)
        for index in range(3):
            part = ring.get(13 + index)
            product = dot_rows(g_qkv[index], part[...])
            attn_out[...] = attn_out[...] + product if index else product
        zero = jnp.zeros((1, D), F32)
        shift_sum = scale_sum = zero
        for rows in row_tiles:
            normed, inverse = norm_rows(hidden[0, rows, :].astype(F32))
            grads = attn_out[rows, :]
            shift_sum += sum_rows(grads)
            scale_sum += sum_rows(grads * normed)
            grad_hidden[rows, :] = grad_hidden[rows, :] + norm_back(
                grads * (1.0 + mod(scale_a)), normed, inverse
            )
        local("grad_hidden", grad_hidden, grad_hidden_hbm).start()
        sums[0:1] = shift_sum
        sums[1:2] = scale_sum
        send_rows()
        for index in range(GROUP):
            start, pieces = index * 864, []
            while start < index * 864 + 864:
                stop = min(index * 864 + 864, (start // D + 1) * D)
                pieces.append(g_qkv[start // D][:, start % D : start % D + stop - start])
                start = stop
            q_stage[index] = jnp.concatenate(pieces + [jnp.zeros((SEQ, 32), BF16)], axis=1)
        def send_q(part):
            lanes = pl.ds(*QKV_LANES[part])
            for to in NEAR:
                links.send(
                    ("q", to, part),
                    to,
                    lambda to=to: (q_stage.at[place.m_at(to), :, lanes], right_q.at[here, lanes]),
                )

        right_q[here, :] = q_stage[m_here]
        scatter_u[0].send_second(1)
        form_down()
        send_q(0)
        scatter_d.send_first(EARLY[1])
        send_q(1)
        form_up(1)
        scatter_u[0].send_rest(on_end)
        forward_a(1)
        gather_rows()
        scatter_d.send_second(1)
        scatter_u[1].send_second(1)
        scatter_u[1].send_rest(on_end)
        form_qkv(0, ORDER)
        scatter_d.send_third()
        scatter_q[0].send_second(1)
        scatter_t.send_second(1, 0)
        scatter_d.send_first(*LATE)
        scatter_q[0].send_rest(on_end)
        for to in NEAR:
            for part in range(2):
                links.left(("q", to, part))
        for to in ("y", "yc", "c"):
            links.left(("ga", to))

    def reduce_rest(
        ada, spread, cond_all, cond_stage, out_ada, out_qkv, out_proj, out_up, out_down
    ):
        load = local("ada_back", ada_w, ada)
        load.start()
        form_qkv(1, ORDER)
        scatter_t.send_third()
        ada_grads(load, ada, spread, cond_all, cond_stage, out_ada)
        scatter_q[1].send_second(1, 0)
        scatter_d.send_second(0)
        scatter_q[1].send_third()
        finish_cond(cond_all)
        total = scatter_d.total()
        out_down[:BLOCK, :] = total[:, :576]
        out_down[BLOCK:, :] = total[:, 576:]
        total = scatter_t.total()
        for index in range(3):
            out_proj[48 * index : 48 * index + 48, :] = total[:, 288 * index : 288 * index + 288]
        for part in range(2):
            out_up[:, pl.ds(*UP_LANES[part])] = scatter_u[part].total()
        results = [
            local("down", out_down, down_hbm),
            local("proj", out_proj, proj_hbm),
            local("up", out_up, up_hbm),
            local("qkv", out_qkv, qkv_hbm),
        ]
        for copy in results[:3]:
            copy.start()
        out_qkv[:, :512] = scatter_q[0].total()
        out_qkv[:, 512:] = scatter_q[1].total()[:, :352]
        results[3].start()
        results.append(local("mixed", mixed, mixed_hbm))
        results.append(local("grad_hidden", grad_hidden, grad_hidden_hbm))
        results.append(local("ada", out_ada, ada_hbm))
        links.drain()
        for copy in results:
            copy.wait()

    def send_rows():
        grads = jnp.concatenate([sums[index : index + 1] for index in range(6)], axis=1)
        qv = jnp.concatenate([sums[6:7], sums[7:8]], axis=1)
        for index in range(GROUP):
            row = jnp.concatenate(
                [
                    grads[:, ADA * index : ADA * index + ADA],
                    jnp.zeros((1, 64), F32),
                    qv[:, 576 * index : 576 * index + 576],
                    sums[8:9][:, 288 * index : 288 * index + 288],
                    sums[10 + index : 11 + index],
                    sums[9:10][:, 288 * index : 288 * index + 288],
                ],
                axis=1,
            )
            row_stage[index] = row.reshape(32, 128).astype(BF16)
        for to in NEAR:
            links.send(
                ("row", to),
                to,
                lambda to=to: (row_stage.at[place.m_at(to)], row_group.at[m_here]),
            )
        row_group[m_here] = row_stage[m_here]

    def gather_rows():
        for to in NEAR:
            links.arrived(("row", to))
        for index in range(GROUP):
            row_all[place.h_index, 16 * index : 16 * index + 16] = row_group[index, :16]
        biases_here = jnp.sum(row_group[...].astype(F32), axis=0)[14:]
        row_all[place.h_index, 64:96] = jnp.concatenate(
            [biases_here, jnp.zeros((14, 128), F32)], axis=0
        ).astype(BF16)
        for to in FAR:
            links.send(
                ("rows", to), to, lambda: (row_all.at[place.h_index], row_all.at[place.h_index])
            )

    def ada_grads(load, ada, spread, cond_all, cond_stage, out_ada):
        for to in FAR:
            links.arrived(("rows", to))
            links.arrived(("silu", to))
        for to in ("l", "lc", "c"):
            for x in range(2):
                links.left(("gb", to, x))
        images = GROUP * INNER
        spread[...] = silu_all[...].astype(F32).reshape(images * 16, 128)

        def tile(index):
            return spread[pl.ds(index, images, stride=16), :]

        silu_rows = jnp.concatenate([tile(index) for index in range(9)], axis=1)
        gb_t[:, :images] = silu_rows.T.astype(BF16)
        spread[...] = row_all[:, :64].astype(F32).reshape(images * 16, 128)
        columns = jnp.concatenate([tile(index) for index in range(14)], axis=1)[:, :ADA]
        out_ada_b[...] = sum_rows(columns).reshape(ADA)
        columns = columns.astype(BF16)
        rows = pl.ds(pl.multiple_of(place.h_index * BLOCK, BLOCK), BLOCK)
        out_ada[...] = dot(gb_t[rows, :images], columns)
        local("ada", out_ada, ada_hbm).start()
        totals = jnp.sum(row_all[:, 64:96].astype(F32), axis=0)
        totals = jnp.concatenate([totals[index : index + 1] for index in range(18)], axis=1)
        start = 0
        for out in (out_qv_b, out_proj_b, out_up_b, out_down_b):
            width = out.shape[0]
            out[...] = totals[:, start : start + width].reshape(width)
            start += width
        load.wait()
        cond_all[...] = dot(columns, ada[...])
        for to in NEAR:
            row = place.h_index * GROUP + place.m_at(to)
            cond_stage[place.m_at(to)] = jnp.broadcast_to(cond_all[pl.ds(row, 1), :], (8, D))
            links.send(
                ("gc", to), to, lambda to=to: (cond_stage.at[place.m_at(to)], cond_in.at[m_here])
            )

    def finish_cond(cond_all):
        total = cond_all[pl.ds(place.h_index * GROUP + m_here, 1), :]
        for to in NEAR:
            links.arrived(("gc", to))
            total += cond_in[place.m_at(to)][:1]
        values = cond[...].astype(F32)
        sigmoid = jax.nn.sigmoid(values)
        grad_cond[...] = total * (sigmoid * (1.0 + values * (1.0 - sigmoid)))

    def local_work(act_stage, pre_stage):
        f32_rows = pltpu.VMEM((SEQ, D), F32)
        pl.run_scoped(
            partial(feed_forward, act_stage, pre_stage),
            f32_rows,
            f32_rows,
            f32_rows,
        )
        pl.run_scoped(
            attention_back,
            pltpu.VMEM((3, SEQ, D), BF16),
            pltpu.VMEM((GROUP, SEQ, 896), BF16),
            pltpu.VMEM((SEQ, WINDOW), BF16),
        )
        for pair in range(2):
            links.left(("act", "l", pair))
        for to in NEAR:
            for part in range(2):
                links.left(("u", to, part))

    pl.run_scoped(
        local_work, pltpu.VMEM((3, SEQ, D), BF16), pltpu.VMEM((3, SEQ, D), BF16)
    )
    pl.run_scoped(
        reduce_rest,
        pltpu.VMEM((ADA, D), BF16),
        pltpu.VMEM((GROUP * INNER * 16, 128), F32),
        pltpu.VMEM((GROUP * INNER, D), F32),
        pltpu.VMEM((GROUP, 8, D), F32),
        pltpu.VMEM((BLOCK, ADA), F32),
        pltpu.VMEM((BLOCK, 864), F32),
        pltpu.VMEM((BLOCK, 288), F32),
        pltpu.VMEM((BLOCK, D), F32),
        pltpu.VMEM((288, 576), F32),
    )


TOGETHER = 4
UP_AXES = ("ylh", "ylh")
UP_LANES = ((0, 640), (640, 512))
QKV_LANES = ((0, 512), (512, 384))
QKV_AXES = ("rph", "rph")


def run_block(outer, *operands):
    vmem = pl.BlockSpec(memory_space=pltpu.VMEM)
    anywhere = pl.BlockSpec(memory_space=pl.ANY)
    smem = pl.BlockSpec(memory_space=pltpu.SMEM)
    scratch = [
        ((1, SEQ, D), BF16),
        ((1, SEQ, D), BF16),
        ((SEQ, D), BF16),
        ((SEQ, D), F32),
        ((1, 9 * D + ADA), F32),
        ((SLOTS, D, D), BF16),
        ((GROUP, 16, D), BF16),
        ((GROUP, 16, 1792), BF16),
        ((8, D), F32),
        ((D, TOKENS), BF16),
        ((4, BLOCK, TOKENS), BF16),
        ((D, TOKENS), BF16),
        ((2, TOKENS, D), BF16),
        ((2, 288, TOKENS), BF16),
        ((TOKENS, D), BF16),
        ((TOKENS, 896), BF16),
        ((TOKENS, WINDOW), BF16),
        ((D, SEQ), BF16),
        ((SEQ, D), BF16),
        ((SEQ, D), BF16),
        ((4, 2, BLOCK, SEQ), BF16),
        ((3, SEQ, D), BF16),
        ((SEQ, D), F32),
        ((16, D), F32),
        ((GROUP, 32, 128), BF16),
        ((GROUP, 32, 128), BF16),
        ((INNER, 96, 128), BF16),
        ((INNER, GROUP, 16, 128), BF16),
        ((GROUP, 8, D), F32),
    ]
    block = (BLOCK, D)
    scratch += [((2, 2, 2) + block, BF16)] * 2
    scratch += [((2, 2) + block, BF16)] * 2 + [((2,) + block, BF16)] * 2 + [(block, BF16)] * 2
    block = (BLOCK, 896)
    scratch += [((2, 2, 2) + block, BF16), ((2, 2) + block, BF16), ((2,) + block, BF16)]
    scratch += [(block, BF16)]
    block = (48, 896)
    scratch += [((2, 2, 2) + block, BF16), ((2, 2) + block, BF16), ((2,) + block, BF16)]
    scratch += [(block, BF16)]
    outs = [
        ((SEQ, D), BF16),
        ((SEQ, D), F32),
        ((1, D), F32),
        ((BLOCK, ADA), F32),
        ((ADA,), F32),
        ((BLOCK, 864), F32),
        ((576,), F32),
        ((BLOCK, 288), F32),
        ((288,), F32),
        ((BLOCK, D), F32),
        ((D,), F32),
        ((288, 576), F32),
        ((288,), F32),
    ]
    outs = [jax.ShapeDtypeStruct(*out) for out in outs]
    small = [vmem if out.shape[0] == 1 or len(out.shape) == 1 else anywhere for out in outs]
    results = pl.pallas_call(
        partial(block_kernel, outer),
        out_shape=outs,
        in_specs=[anywhere, vmem, smem, anywhere] + [vmem] * 5 + [anywhere] * 5,
        out_specs=small,
        scratch_shapes=[pltpu.VMEM(*each) for each in scratch]
        + [
            pltpu.SemaphoreType.DMA((128,)),
            pltpu.SemaphoreType.DMA((128,)),
            pltpu.SemaphoreType.DMA((SLOTS,)),
            pltpu.SemaphoreType.DMA((len(LOCAL),)),
        ],
        compiler_params=pltpu.CompilerParams(
            collective_id=0, has_side_effects=True, vmem_limit_bytes=VMEM_LIMIT
        ),
    )(*operands)
    return pl.pallas_call(
        place_kernel,
        out_shape=outs,
        in_specs=[anywhere] * len(outs),
        out_specs=[anywhere] * len(outs),
        scratch_shapes=[pltpu.VMEM(out.shape, out.dtype) for out in outs]
        + [pltpu.SemaphoreType.DMA((2, len(outs)))],
    )(*results)


VMEM_LIMIT = 63 * 2**20 + 900 * 2**10
LOCAL = (
    "ada_in", "hidden", "out_grad", "mixed", "grad_hidden", "ada_back", "ada", "down", "proj",
    "up", "qkv",
)


def place_kernel(*refs):
    count = len(refs) // 3
    sems = refs[-1]
    here = [
        pltpu.make_async_copy(refs[index], refs[2 * count + index], sems.at[0, index])
        for index in range(count)
    ]
    there = [
        pltpu.make_async_copy(refs[2 * count + index], refs[count + index], sems.at[1, index])
        for index in range(count)
    ]
    for copy in here:
        copy.start()
    for first, second in zip(here, there):
        first.wait()
        second.start()
    for copy in there:
        copy.wait()


def on_device(
    outer,
    hidden_in,
    conditioning,
    live_images,
    out_grad,
    ada_weight,
    ada_bias,
    qkv_weight,
    qv_bias,
    proj_weight,
    proj_bias,
    up_weight,
    up_bias,
    down_weight,
    down_bias,
):
    (
        mixed,
        grad_hidden,
        grad_cond,
        out_ada_w,
        out_ada_b,
        out_qkv_w,
        out_qv_b,
        out_proj_w,
        out_proj_b,
        out_up_w,
        out_up_b,
        out_down_w,
        out_down_b,
    ) = run_block(
        outer,
        hidden_in,
        conditioning,
        live_images,
        out_grad,
        ada_bias,
        qv_bias,
        proj_bias,
        up_bias,
        down_bias,
        ada_weight.T,
        qkv_weight,
        proj_weight,
        up_weight,
        down_weight,
    )
    out_down_w = out_down_w.T
    if outer > 1:
        groups = [[h * outer + low for low in range(outer)] for h in range(INNER)]
        out_ada_w, out_down_w, out_up_w, out_qkv_w, out_proj_w = (
            lax.psum_scatter(
                part, "dp", scatter_dimension=0, tiled=True, axis_index_groups=groups
            )
            for part in (out_ada_w, out_down_w, out_up_w, out_qkv_w, out_proj_w)
        )
        out_ada_b, out_qv_b, out_proj_b, out_up_b, out_down_b = (
            jnp.sum(
                lax.all_gather(part, "dp", axis=0, axis_index_groups=groups), axis=0
            )
            for part in (out_ada_b, out_qv_b, out_proj_b, out_up_b, out_down_b)
        )
    return (
        mixed[None],
        grad_hidden[None],
        grad_cond,
        out_ada_w,
        out_ada_b,
        out_qkv_w,
        out_qv_b,
        out_proj_w,
        out_proj_b,
        out_up_w,
        out_up_b,
        out_down_w,
        out_down_b,
    )


def solution(mesh):
    in_specs = (
        P(("dp", "mp"), None, None),
        P(("dp", "mp"), None),
        P(("dp", "mp")),
        P(("dp", "mp"), None, None),
        P(None, "mp"),
        P("mp"),
        P(),
        P(),
        P(),
        P(),
        P(),
        P(),
        P(),
        P(),
    )
    out_specs = (
        P(("dp", "mp"), None, None),
        P(("dp", "mp"), None, None),
        P(("dp", "mp"), None),
        P("dp", "mp"),
        P("mp"),
        P("dp", "mp"),
        P("mp"),
        P("dp", "mp"),
        P("mp"),
        P("dp", "mp"),
        P("mp"),
        P("dp", "mp"),
        P("mp"),
    )
    return jax.shard_map(
        partial(on_device, mesh.shape["dp"] // INNER),
        mesh=mesh,
        in_specs=in_specs,
        out_specs=out_specs,
        check_vma=False,
    )
```

```python
from functools import partial

import jax
import jax.numpy as jnp
from jax import lax
from jax.experimental import pallas as pl
from jax.experimental.pallas import tpu as pltpu
from jax.sharding import PartitionSpec as P

D = 1152
HEADS = 16
HEAD_DIM = 72
FF = 4608
SEQ = 256
ADA = 1728
MESH_ID = pl.DeviceIdType.MESH
BF16 = jnp.bfloat16
F32 = jnp.float32
INNER = 8
BLOCK = D // INNER
GROUP = 4
TOKENS = GROUP * SEQ
WINDOW = 640
SLOTS = 3
SCALE = HEAD_DIM ** (-0.5)
PEERS = ("c", "x", "xc", "y", "yc", "l", "lc", "h", "yl", "yh", "lh", "ylh")
FAR = ("y", "l", "h", "yl", "yh", "lh", "ylh")
NEAR = ("xc", "x", "c")
ORDER = ((1, 1), (0, 1), (1, 0), (0, 0))
EARLY, LATE = ORDER[:2], ORDER[2:]


def dot(left, right):
    return jnp.dot(left, right, preferred_element_type=F32)


def dot_rows(left, right):
    return lax.dot_general(left, right, (((1,), (1,)), ((), ())), preferred_element_type=F32)


def norm_rows(values):
    center = values - jnp.mean(values, axis=-1, keepdims=True)
    inverse = lax.rsqrt(jnp.mean(center * center, axis=-1, keepdims=True) + 1e-06)
    return center * inverse, inverse


def norm_back(grad_normed, normed, inverse):
    mean_grad = jnp.mean(grad_normed, axis=-1, keepdims=True)
    mean_prod = jnp.mean(grad_normed * normed, axis=-1, keepdims=True)
    return inverse * (grad_normed - mean_grad - normed * mean_prod)


def sum_rows(values):
    return jnp.sum(values, axis=0, keepdims=True)


class Place:
    def __init__(self, outer):
        data, model = lax.axis_index("dp"), lax.axis_index("mp")
        self.outer = outer
        self.low = data % outer
        self.h_index = data // outer
        self.m_index = model
        self.bits = {
            "h": self.h_index // 4,
            "l": (self.h_index // 2) % 2,
            "y": self.h_index % 2,
            "x": model // 2,
            "c": model % 2,
        }

    def flipped(self, names):
        if "p" in names and "r" in names:
            names += "yl"
        bits = {key: (1 - bit if key in names else bit) for key, bit in self.bits.items()}
        if ("p" in names) != ("r" in names):
            second = bits["c"] if "p" in names else 1 - bits["c"]
            bits["y"] += second * (1 - 2 * bits["y"])
            bits["l"] += (1 - second) * (1 - 2 * bits["l"])
        return bits

    def h_at(self, names):
        bits = self.flipped(names)
        return bits["h"] * 4 + bits["l"] * 2 + bits["y"]

    def m_at(self, names):
        bits = self.flipped(names)
        return bits["x"] * 2 + bits["c"]

    def pair_at(self, axis, names):
        bits = self.flipped(names)
        return bits[axis] * 2 + bits["c"]

    def device(self, names):
        return (self.h_at(names) * self.outer + self.low, self.m_at(names))


class Links:
    def __init__(self, place, send_sems, recv_sems):
        self.place = place
        self.send_sems = send_sems
        self.recv_sems = recv_sems
        self.builders = {}
        self.gone = set()

    def send(self, name, to, ends):
        self.plan(name, to, ends)
        self.start(name)

    def start(self, name):
        self.builders[name]().start()

    def plan(self, name, to, ends):
        index = len(self.builders)

        def build(landed=False):
            source, target = ends()
            if landed:
                source = target
            return pltpu.make_async_remote_copy(
                src_ref=source,
                dst_ref=target,
                send_sem=self.send_sems.at[index],
                recv_sem=self.recv_sems.at[index],
                device_id=self.place.device(to),
                device_id_type=MESH_ID,
            )

        self.builders[name] = build

    def arrived(self, name):
        self.builders[name](landed=True).wait_recv()

    def left(self, name):
        self.gone.add(name)
        self.builders[name]().wait_send()

    def drain(self):
        for name in self.builders:
            if name not in self.gone:
                self.left(name)


class Ring:
    def __init__(self, parts, slots, sems):
        self.parts = parts
        self.slots = slots
        self.sems = sems

    def begin(self):
        for index in range(SLOTS):
            self.start(index)

    def copy(self, index):
        slot = index % SLOTS
        return pltpu.make_async_copy(self.parts[index], self.slots.at[slot], self.sems.at[slot])

    def start(self, index):
        if index < len(self.parts):
            self.copy(index).start()

    def get(self, index):
        self.copy(index).wait()
        return self.slots.at[index % SLOTS]

    def done(self, index):
        self.start(index + SLOTS)


class Scatter:
    def __init__(self, links, name, axes, lanes, grad, first, second, third):
        self.links, self.name, self.axes = links, name, axes
        self.lanes = pl.ds(*lanes)
        self.grad, self.first, self.second, self.third = grad, first, second, third
        for b1, b2 in ORDER:
            links.plan(
                (name, 0, b1, b2),
                axes[0],
                lambda b1=b1, b2=b2: (self.cut(grad, 1, b1, b2), self.cut(first, b1, b2)),
            )
        for b2 in range(2):
            links.plan(
                (name, 1, b2),
                axes[1],
                lambda b2=b2: (self.cut(grad, 0, 1, b2), self.cut(second, b2)),
            )
        links.plan((name, 2), axes[2], lambda: (self.cut(grad, 0, 0, 1), self.cut(third)))

    def cut(self, ref, *index):
        return ref.at[index + (slice(None), self.lanes)]

    def read(self, ref, *index):
        return self.cut(ref, *index)[...].astype(F32)

    def write(self, value, *index):
        self.grad[index + (slice(None), self.lanes)] = value.astype(BF16)

    def send_first(self, *pairs):
        for b1, b2 in pairs:
            self.links.start((self.name, 0, b1, b2))

    def send_second(self, *ends):
        for b2 in ends:
            self.links.arrived((self.name, 0, 1, b2))
            self.write(self.read(self.grad, 0, 1, b2) + self.read(self.first, 1, b2), 0, 1, b2)
            self.links.start((self.name, 1, b2))

    def send_third(self):
        self.links.arrived((self.name, 0, 0, 1))
        self.links.arrived((self.name, 1, 1))
        total = self.read(self.grad, 0, 0, 1) + self.read(self.first, 0, 1)
        self.write(total + self.read(self.second, 1), 0, 0, 1)
        self.links.start((self.name, 2))

    def send_rest(self, outer):
        @pl.when(outer == 0)
        def _():
            self.send_third()
            self.send_second(0)

        @pl.when(outer == 1)
        def _():
            self.send_second(0)
            self.send_third()

    def total(self):
        self.links.arrived((self.name, 0, 0, 0))
        self.links.arrived((self.name, 1, 0))
        self.links.arrived((self.name, 2))
        return (
            self.read(self.grad, 0, 0, 0)
            + self.read(self.first, 0, 0)
            + self.read(self.second, 0)
            + self.read(self.third)
        )


def head_window(head):
    start = (head * 9) // 16 - head // 15
    offset = head * HEAD_DIM - start * 128
    lanes = lax.broadcasted_iota(jnp.int32, (SEQ, 256), 1)
    inside = (lanes >= offset) & (lanes < offset + HEAD_DIM)
    return pl.ds(pl.multiple_of(start * 128, 128), 256), inside


def each(function, *lists):
    return [function(*items) for items in zip(*lists)]


def head_probs(qkv, heads):
    windows, insides = zip(*each(head_window, heads))
    queries = each(lambda at, inside: jnp.where(inside, qkv[0, :, at], 0), windows, insides)
    scores = each(lambda query, at: dot_rows(query, qkv[1, :, at]), queries, windows)
    tops = each(lambda score: jnp.max(score, axis=-1, keepdims=True), scores)
    shifted = each(lambda score, top: jnp.exp((score - top) * SCALE), scores, tops)
    totals = each(lambda value: 1.0 / jnp.sum(value, axis=-1, keepdims=True), shifted)
    probs = each(lambda value, total: value * total, shifted, totals)
    return windows, insides, queries, probs


def block_kernel(
    outer,
    hidden_hbm,
    cond_hbm,
    live,
    out_grad_hbm,
    ada_bias_hbm,
    qv_bias_hbm,
    proj_bias_hbm,
    up_bias_hbm,
    down_bias_hbm,
    ada_w,
    qkv_w,
    proj_w,
    up_w,
    down_w,
    mixed_hbm,
    grad_hidden_hbm,
    grad_cond_hbm,
    ada_hbm,
    ada_b_hbm,
    qkv_hbm,
    qv_b_hbm,
    proj_hbm,
    proj_b_hbm,
    up_hbm,
    up_b_hbm,
    down_hbm,
    down_b_hbm,
    cond,
    ada_bias,
    qv_bias,
    proj_bias,
    up_bias,
    down_bias,
    grad_cond,
    out_ada_b,
    out_qv_b,
    out_proj_b,
    out_up_b,
    out_down_b,
    hidden,
    out_grad,
    mixed,
    grad_hidden,
    biases,
    ring_slots,
    cond_rows,
    mod_in,
    mods,
    left_a,
    left_t,
    left_m,
    right_act,
    left_b,
    right_u,
    right_q,
    right_t,
    gb_t,
    g_branch,
    natural,
    att_t,
    qkv,
    attn_out,
    sums,
    row_stage,
    row_group,
    row_all,
    silu_all,
    cond_in,
    grad_d,
    grad_u,
    first_d,
    first_u,
    second_d,
    second_u,
    third_d,
    third_u,
    grad_q,
    first_q,
    second_q,
    third_q,
    grad_t,
    first_t,
    second_t,
    third_t,
    send_sems,
    recv_sems,
    ring_sems,
    local_sems,
):
    place = Place(outer)
    bits = place.bits
    m_here = place.m_index
    links = Links(place, send_sems, recv_sems)

    on_end = 1 - bits["h"] - bits["l"] + 2 * bits["h"] * bits["l"]

    def spot(index):
        return pl.ds(pl.multiple_of(index * SEQ, SEQ), SEQ)

    here, here_yc, here_lc = spot(m_here), spot(place.pair_at("y", "")), spot(place.pair_at("l", ""))
    ff_order = [place.m_at(to) for to in NEAR] + [m_here]

    def ff_part(index):
        return pl.ds(pl.multiple_of(index * D, D), D)

    qkv_parts = [qkv_w.at[:, pl.ds(index * D, D)] for index in range(3)]
    ff_parts = []
    for index in ff_order:
        ff_parts += [up_w.at[:, ff_part(index)], down_w.at[ff_part(index), :]]
    def local(name, source, target):
        return pltpu.make_async_copy(source, target, local_sems.at[LOCAL.index(name)])

    small_in = [
        local("cond", cond_hbm, cond),
        local("ada_bias", ada_bias_hbm, ada_bias),
        local("qv_bias", qv_bias_hbm, qv_bias),
        local("proj_bias", proj_bias_hbm, proj_bias),
        local("up_bias", up_bias_hbm, up_bias),
        local("down_bias", down_bias_hbm, down_bias),
    ]
    small_in[0].start()
    barrier = pltpu.get_barrier_semaphore()
    for names in PEERS:
        pl.semaphore_signal(
            barrier, inc=1, device_id=place.device(names), device_id_type=MESH_ID
        )
    ring = Ring(qkv_parts + [proj_w] + ff_parts + [proj_w] + qkv_parts, ring_slots, ring_sems)
    row_tiles = [pl.ds(start, 64) for start in range(0, SEQ, 64)]

    def bias(start, width=D):
        return biases[:, pl.ds(start, width)]

    def modulation(ada, mod_out):
        small_in[0].wait()
        for copy in small_in[1:]:
            copy.start()
        silu_row = jax.nn.silu(cond[...].astype(F32))
        cond_rows[m_here] = jnp.broadcast_to(silu_row, (16, D)).astype(BF16)
        load = local("ada_in", ada_w, ada)
        load.start()
        pl.semaphore_wait(barrier, len(PEERS))
        for to in NEAR:
            links.send(("cond", to), to, lambda: (cond_rows.at[m_here], cond_rows.at[m_here]))
        copy_in = local("hidden", hidden_hbm, hidden)
        copy_in.start()
        ring.begin()
        for copy in small_in[1:]:
            copy.wait()
        for start, part in ((2, qv_bias), (3, proj_bias), (4, up_bias), (8, down_bias), (9, ada_bias)):
            row = part[...].astype(F32)[None, :]
            if start == 2:
                biases[:, : 2 * D] = jnp.concatenate([row[:, :D], jnp.zeros((1, D), F32)], axis=1)
                row = row[:, D:]
            biases[:, start * D : start * D + row.shape[1]] = row
        copy_in.wait()
        local("out_grad", out_grad_hbm, out_grad).start()
        for rows in row_tiles:
            grad_hidden[rows, :] = norm_rows(hidden[0, rows, :].astype(F32))[0]
        load.wait()
        for to in NEAR:
            links.arrived(("cond", to))
        columns = dot_rows(cond_rows[...].reshape(64, D), ada[...]) + bias(9 * D, ADA)
        mod_out[:, :, :ADA] = columns.astype(BF16).reshape(GROUP, 16, ADA)
        for to in NEAR:
            links.send(
                ("mod", to), to, lambda to=to: (mod_out.at[place.m_at(to)], mod_in.at[m_here])
            )
        mod_in[m_here] = mod_out[m_here]
        for to in NEAR:
            links.left(("mod", to))

    def small_out():
        return [
            local("ada_b", out_ada_b, ada_b_hbm),
            local("qv_b", out_qv_b, qv_b_hbm),
            local("proj_b", out_proj_b, proj_b_hbm),
            local("up_b", out_up_b, up_b_hbm),
            local("down_b", out_down_b, down_b_hbm),
        ]

    def send_silu():
        for index in range(GROUP):
            silu_row = cond_rows[index].astype(F32)[:1]
            tiles = silu_row.reshape(9, 128)
            silu_all[place.h_index, index] = jnp.concatenate(
                [tiles, jnp.zeros((7, 128), F32)], axis=0
            ).astype(BF16)
        for to in FAR:
            links.send(
                ("silu", to),
                to,
                lambda: (silu_all.at[place.h_index], silu_all.at[place.h_index]),
            )

    pl.run_scoped(
        modulation, pltpu.VMEM((ADA, D), BF16), pltpu.VMEM((GROUP, 16, 1792), BF16)
    )
    for to in NEAR:
        links.arrived(("mod", to))
    parts = [mod_in[index].astype(F32)[:1] for index in range(GROUP)]
    for index in range(2):
        low, high = parts[2 * index], parts[2 * index + 1]
        mods[3 * index : 3 * index + 1] = low[:, :D]
        mods[3 * index + 1 : 3 * index + 2] = jnp.concatenate(
            [low[:, D:ADA], high[:, : D // 2]], axis=1
        )
        mods[3 * index + 2 : 3 * index + 3] = high[:, D // 2 : ADA]
    shift_a, scale_a, gate_a, shift_m, scale_m, gate_m = range(6)

    def mod(index):
        return mods[index : index + 1]

    live_factor = live[0].astype(F32)
    local("out_grad", out_grad_hbm, out_grad).wait()
    for rows in row_tiles:
        natural[rows, :] = (
            grad_hidden[rows, :] * (1.0 + mod(scale_a)) + mod(shift_a)
        ).astype(BF16)
        g_branch[rows, :] = (
            out_grad[0, rows, :].astype(F32) * live_factor * mod(gate_m)
        ).astype(BF16)
    left_a[:, here] = natural[...].T

    def send_a(half):
        def ends():
            part = left_a.at[pl.ds(half * 576, 576), here]
            return part, part

        for to in ("x", "c"):
            links.send(("a", to, half), to, ends)

    send_a(0)
    gb_t[...] = g_branch[...].T

    def gb_rows(to, x):
        return pl.ds(pl.multiple_of((2 * x + place.flipped(to)["c"]) * 288, 288), 288)

    for to in ("l", "lc", "c"):
        for x in range(2):
            links.send(
                ("gb", to, x),
                to,
                lambda to=to, x=x: (gb_t.at[gb_rows(to, x), :], left_b.at[x, :, here_lc]),
            )
    for x in range(2):
        left_b[x, :, here_lc] = gb_t[gb_rows("", x), :]
    sums[9:10] = sum_rows(g_branch[...].astype(F32))
    send_silu()

    for index in range(3):
        part = ring.get(index)
        qkv[index] = (dot(natural[...], part[...]) + bias(index * D)).astype(BF16)
        ring.done(index)

    def attend(group, carry):
        heads = [group * TOGETHER + index for index in range(TOGETHER)]
        windows, insides, _, probs = head_probs(qkv, heads)
        values = each(
            lambda prob, at: dot(prob.astype(BF16), qkv[2, :, at]).astype(BF16), probs, windows
        )
        for at, inside, value in zip(windows, insides, values):
            natural[:, at] = jnp.where(inside, value, natural[:, at])
        return carry

    lax.fori_loop(0, HEADS // TOGETHER, attend, 0)
    att_t[...] = natural[...].T.reshape(4, 2, BLOCK, SEQ)
    for to in ("y", "c"):
        links.send(
            ("t", to),
            to,
            lambda to=to: (
                att_t.at[:, place.flipped("y" if to == "y" else "")["y"]],
                left_t.at[:, :, here_yc],
            ),
        )
    left_t[:, :, here_yc] = att_t[:, bits["y"]]
    part = ring.get(3)
    attn_out[...] = dot(natural[...], part[...]) + bias(3 * D)
    ring.done(3)

    def act_rows(pair):
        return bits["x"] if pair else 1 - bits["x"]

    def feed_forward(act_stage, pre_stage, after, branch, g_mod):
        slope = grad_hidden
        for rows in row_tiles:
            after[rows, :] = hidden[0, rows, :].astype(F32) + mod(gate_a) * attn_out[rows, :]
            normed, _ = norm_rows(after[rows, :])
            natural[rows, :] = (normed * (1.0 + mod(scale_m)) + mod(shift_m)).astype(BF16)
        left_m[:, here] = natural[...].T
        for to in ("x", "c"):
            links.send(("m", to), to, lambda: (left_m.at[:, here], left_m.at[:, here]))
        for step in range(4):
            index = ff_order[step]
            up = ring.get(4 + 2 * step)
            parity = index % 2
            away = parity + bits["l"] - 2 * parity * bits["l"]
            act_now = act_stage.at[away * (1 + step // 2)]
            for tile in range(3):
                lanes = pl.ds(tile * 384, 384)
                offset = pl.multiple_of(4 * D + index * D + tile * 384, 128)
                pre = dot(natural[...], up[:, lanes]) + biases[:, pl.ds(offset, 384)]
                square = pre * pre
                slant = jnp.tanh(0.7978845608028654 * pre * (1.0 + 0.044715 * square))
                half = 0.5 * (1.0 + slant)
                act_now[:, lanes] = (pre * half).astype(BF16)
                slope[:, lanes] = half + 0.5 * pre * (1.0 - slant * slant) * (
                    0.7978845608028654 * (1.0 + 0.134145 * square)
                )
            if step % 2:
                pair = step // 2
                right_act[act_rows(pair), here_lc] = act_stage[0]
                links.send(
                    ("act", "l", pair),
                    "l",
                    lambda pair=pair: (
                        act_stage.at[1 + pair], right_act.at[act_rows(pair), here_lc]
                    ),
                )
                links.send(
                    ("act", "c", pair),
                    "c",
                    lambda pair=pair: (
                        right_act.at[act_rows(pair), here_lc],
                        right_act.at[act_rows(pair), here_lc],
                    ),
                )
            down = ring.get(5 + 2 * step)
            for tile in range(3):
                lanes = pl.ds(tile * 384, 384)
                g_pre = (dot_rows(g_branch[...], down[lanes, :]) * slope[:, lanes]).astype(BF16)
                sums[pl.ds(10 + index, 1), lanes] = sum_rows(g_pre.astype(F32))
                if step < 3:
                    pre_stage[step, :, lanes] = g_pre
                else:
                    right_u[here, lanes] = g_pre
            if step < 3:
                g_pre_ref = pre_stage.at[step]
                for part in range(2):
                    lanes = pl.ds(*UP_LANES[part])
                    links.plan(
                        ("u", NEAR[step], part),
                        NEAR[step],
                        lambda step=step, lanes=lanes: (
                            pre_stage.at[step, :, lanes], right_u.at[here, lanes]
                        ),
                    )
                for to, part in ((("xc", 0),), (("x", 0), ("xc", 1), ("x", 1)), (("c", 0), ("c", 1)))[step]:
                    links.start(("u", to, part))
                if step == 1:
                    send_a(1)
            else:
                g_pre_ref = right_u.at[here]
            new_mod = dot_rows(g_pre_ref[...], up[...])
            g_mod[...] = new_mod + g_mod[...] if step else new_mod
            ring.done(4 + 2 * step)
            new_branch = dot(act_now[...], down[...])
            branch[...] = new_branch + (branch[...] if step else bias(8 * D))
            ring.done(5 + 2 * step)
            if step == 1:
                forward_t()
            if step == 2:
                forward_a(0)
            if step == 3:
                forward_m()
        zero = jnp.zeros((1, D), F32)
        gate_m_sum = scale_m_sum = shift_m_sum = gate_a_sum = proj_sum = zero
        for rows in row_tiles:
            cotangent = out_grad[0, rows, :].astype(F32) * live_factor
            mixed[rows, :] = (after[rows, :] + mod(gate_m) * branch[rows, :]).astype(BF16)
            gate_m_sum += sum_rows(cotangent * branch[rows, :])
            normed, inverse = norm_rows(after[rows, :])
            grads = g_mod[rows, :]
            shift_m_sum += sum_rows(grads)
            scale_m_sum += sum_rows(grads * normed)
            g_after = cotangent + norm_back(grads * (1.0 + mod(scale_m)), normed, inverse)
            grad_hidden[rows, :] = g_after
            gate_a_sum += sum_rows(g_after * attn_out[rows, :])
            g_attn = (g_after * mod(gate_a)).astype(BF16)
            natural[rows, :] = g_attn
            proj_sum += sum_rows(g_attn.astype(F32))
        local("mixed", mixed, mixed_hbm).start()
        sums[2:3] = gate_a_sum
        sums[3:4] = shift_m_sum
        sums[4:5] = scale_m_sum
        sums[5:6] = gate_m_sum
        sums[8:9] = proj_sum

    spot_x, spot_y = spot(place.m_at("x")), spot(place.pair_at("y", "y"))
    spot_l = spot(place.pair_at("l", "l"))

    def forward_m():
        links.arrived(("m", "x"))
        links.send(("m", "f"), "c", lambda: (left_m.at[:, spot_x], left_m.at[:, spot_x]))

    def forward_a(half):
        def ends():
            part = left_a.at[pl.ds(half * 576, 576), spot_x]
            return part, part

        links.arrived(("a", "x", half))
        links.send(("a", "f", half), "c", ends)

    def forward_t():
        links.arrived(("t", "y"))
        links.send(
            ("t", "f"), "c", lambda: (left_t.at[:, :, spot_y], left_t.at[:, :, spot_y])
        )

    def forward_act(pair):
        def target():
            return right_act.at[act_rows(pair), spot_l]

        links.arrived(("act", "l", pair))
        links.send(("act", "f", pair), "c", lambda: (target(), target()))

    scatter_d = Scatter(links, "d", "xyh", (0, D), grad_d, first_d, second_d, third_d)
    scatter_t = Scatter(links, "t", "lxh", (0, 896), grad_t, first_t, second_t, third_t)
    scatter_u = [
        Scatter(links, ("u", part), axes, lanes, grad_u, first_u, second_u, third_u)
        for part, (axes, lanes) in enumerate(zip(UP_AXES, UP_LANES))
    ]
    scatter_q = [
        Scatter(links, ("q", part), axes, lanes, grad_q, first_q, second_q, third_q)
        for part, (axes, lanes) in enumerate(zip(QKV_AXES, QKV_LANES))
    ]

    def form_down():
        for to in ("l", "c", "lc"):
            for x in range(2):
                links.arrived(("gb", to, x))
        for pair in range(2):
            links.arrived(("act", "c", pair))
            links.arrived(("act", "f", pair))
        for b0 in (1, 0):
            for b2 in (1, 0):
                there = place.flipped("x" * b0 + "h" * b2)
                wide = dot(left_b[there["x"]], right_act[there["h"]]).astype(BF16)
                for y in range(2):
                    block = wide[:, 576 * y : 576 * y + 576]
                    other = 1 - bits["y"] if y else bits["y"]
                    grad_d[b0, other, b2] = jnp.concatenate(
                        [block[:BLOCK], block[BLOCK:]], axis=1
                    )
            if b0:
                scatter_d.send_first(EARLY[0])

    def grad_rows(flips):
        return pl.ds(pl.multiple_of(place.h_at(flips) * BLOCK, BLOCK), BLOCK)

    def form_up(part):
        for to in NEAR:
            links.arrived(("u", to, part))
        if part == 0:
            links.arrived(("m", "c"))
            links.arrived(("m", "f"))
        lanes = pl.ds(*UP_LANES[part])
        for b0 in (1, 0):
            for b1, b2 in ORDER:
                axes = scatter_u[part].axes
                rows = grad_rows(axes[0] * b0 + axes[1] * b1 + axes[2] * b2)
                grad_u[b0, b1, b2, :, lanes] = dot(left_m[rows, :], right_u[:, lanes]).astype(BF16)
                if b0:
                    scatter_u[part].send_first((b1, b2))

    def form_qkv(part, pairs):
        for to in NEAR:
            links.arrived(("q", to, part))
        if part == 0:
            for half in range(2):
                for to in ("c", "f"):
                    links.arrived(("a", to, half))
        lanes = pl.ds(*QKV_LANES[part])
        for b0 in (1, 0):
            for b1, b2 in ORDER:
                axes = scatter_q[part].axes
                rows = grad_rows(axes[0] * b0 + axes[1] * b1 + axes[2] * b2)
                grad_q[b0, b1, b2, :, lanes] = dot(left_a[rows, :], right_q[:, lanes]).astype(BF16)
                if b0 and (b1, b2) in pairs:
                    scatter_q[part].send_first((b1, b2))

    def form_proj():
        for to in ("y", "c", "yc"):
            links.arrived(("ga", to))
        for to in ("c", "f"):
            links.arrived(("t", to))
        for b0 in (1, 0):
            for b2 in (1, 0):
                there = place.flipped("l" * b0 + "h" * b2)
                wide = dot(left_t[there["h"] * 2 + there["l"]], right_t[...]).astype(BF16)
                for x in range(2):
                    other = 1 - bits["x"] if x else bits["x"]
                    block = wide[:, 288 * x : 288 * x + 288]
                    grad_t[b0, other, b2, :, :864] = jnp.concatenate(
                        [block[:48], block[48:96], block[96:]], axis=1
                    )

    def attention_back(g_qkv, q_stage, ga_stage):
        g_attn = natural[...]
        columns = [
            jnp.concatenate(
                [
                    g_attn[:, 288 * core : 288 * core + 288],
                    g_attn[:, 576 + 288 * core : 864 + 288 * core],
                    jnp.zeros((SEQ, 64), BF16),
                ],
                axis=1,
            )
            for core in range(2)
        ]
        ga_stage[...] = jnp.where(bits["c"] == 0, columns[1], columns[0])
        right_t[here_yc, :] = jnp.where(bits["c"] == 0, columns[0], columns[1])
        for to in ("y", "yc", "c"):
            links.send(
                ("ga", to),
                to,
                lambda to=to: (
                    right_t.at[here_yc] if to == "y" else ga_stage,
                    right_t.at[here_yc],
                ),
            )
        part = ring.get(12)
        g_att = g_branch
        g_att[...] = dot_rows(natural[...], part[...]).astype(BF16)
        ring.done(12)

        def back(group, carry):
            heads = [group * TOGETHER + index for index in range(TOGETHER)]
            windows, insides, queries, probs = head_probs(qkv, heads)
            grads = each(lambda at, inside: jnp.where(inside, g_att[:, at], 0), windows, insides)
            g_probs = each(lambda grad, at: dot_rows(grad, qkv[2, :, at]), grads, windows)
            g_values = each(lambda prob, grad: dot(prob.astype(BF16).T, grad), probs, grads)
            row_dots = each(
                lambda prob, g_prob: jnp.sum(prob * g_prob, axis=-1, keepdims=True), probs, g_probs
            )
            g_scores = each(
                lambda prob, g_prob, row_dot: (prob * (g_prob - row_dot)).astype(BF16),
                probs,
                g_probs,
                row_dots,
            )
            g_queries = each(lambda g, at: dot(g, qkv[1, :, at]) * SCALE, g_scores, windows)
            g_keys = each(lambda g, query: dot(g.T, query) * SCALE, g_scores, queries)
            for index, values in enumerate((g_queries, g_keys, g_values)):
                for at, inside, value in zip(windows, insides, values):
                    g_qkv[index, :, at] = jnp.where(
                        inside, value.astype(BF16), g_qkv[index, :, at]
                    )
            return carry

        groups = HEADS // TOGETHER
        lax.fori_loop(0, groups // 2, back, 0)
        forward_act(0)
        lax.fori_loop(groups // 2, groups, back, 0)
        sums[6:7] = sum_rows(g_qkv[0].astype(F32))
        sums[7:8] = sum_rows(g_qkv[2].astype(F32))
        form_up(0)
        forward_act(1)
        form_proj()
        scatter_t.send_first(*ORDER)
        for index in range(3):
            part = ring.get(13 + index)
            product = dot_rows(g_qkv[index], part[...])
            attn_out[...] = attn_out[...] + product if index else product
        zero = jnp.zeros((1, D), F32)
        shift_sum = scale_sum = zero
        for rows in row_tiles:
            normed, inverse = norm_rows(hidden[0, rows, :].astype(F32))
            grads = attn_out[rows, :]
            shift_sum += sum_rows(grads)
            scale_sum += sum_rows(grads * normed)
            grad_hidden[rows, :] = grad_hidden[rows, :] + norm_back(
                grads * (1.0 + mod(scale_a)), normed, inverse
            )
        local("grad_hidden", grad_hidden, grad_hidden_hbm).start()
        sums[0:1] = shift_sum
        sums[1:2] = scale_sum
        send_rows()
        for index in range(GROUP):
            start, pieces = index * 864, []
            while start < index * 864 + 864:
                stop = min(index * 864 + 864, (start // D + 1) * D)
                pieces.append(g_qkv[start // D][:, start % D : start % D + stop - start])
                start = stop
            q_stage[index] = jnp.concatenate(pieces + [jnp.zeros((SEQ, 32), BF16)], axis=1)
        def send_q(part):
            lanes = pl.ds(*QKV_LANES[part])
            for to in NEAR:
                links.send(
                    ("q", to, part),
                    to,
                    lambda to=to: (q_stage.at[place.m_at(to), :, lanes], right_q.at[here, lanes]),
                )

        right_q[here, :] = q_stage[m_here]
        scatter_u[0].send_second(1)
        form_down()
        send_q(0)
        scatter_d.send_first(EARLY[1])
        send_q(1)
        form_up(1)
        scatter_u[0].send_rest(on_end)
        forward_a(1)
        gather_rows()
        scatter_d.send_second(1)
        scatter_u[1].send_second(1)
        scatter_u[1].send_rest(on_end)
        form_qkv(0, ORDER)
        scatter_d.send_third()
        scatter_q[0].send_second(1)
        scatter_t.send_second(1, 0)
        scatter_d.send_first(*LATE)
        scatter_q[0].send_rest(on_end)
        for to in NEAR:
            for part in range(2):
                links.left(("q", to, part))
        for to in ("y", "yc", "c"):
            links.left(("ga", to))

    def reduce_rest(
        ada, spread, cond_all, cond_stage, out_ada, out_qkv, out_proj, out_up, out_down
    ):
        load = local("ada_back", ada_w, ada)
        load.start()
        form_qkv(1, ORDER)
        scatter_t.send_third()
        ada_grads(load, ada, spread, cond_all, cond_stage, out_ada)
        scatter_q[1].send_second(1, 0)
        scatter_d.send_second(0)
        scatter_q[1].send_third()
        finish_cond(cond_all)
        local("grad_cond", grad_cond, grad_cond_hbm).start()
        total = scatter_d.total()
        out_down[:BLOCK, :] = total[:, :576]
        out_down[BLOCK:, :] = total[:, 576:]
        total = scatter_t.total()
        for index in range(3):
            out_proj[48 * index : 48 * index + 48, :] = total[:, 288 * index : 288 * index + 288]
        for part in range(2):
            out_up[:, pl.ds(*UP_LANES[part])] = scatter_u[part].total()
        results = [
            local("down", out_down, down_hbm),
            local("proj", out_proj, proj_hbm),
            local("up", out_up, up_hbm),
            local("qkv", out_qkv, qkv_hbm),
        ]
        for copy in results[:3]:
            copy.start()
        out_qkv[:, :512] = scatter_q[0].total()
        out_qkv[:, 512:] = scatter_q[1].total()[:, :352]
        results[3].start()
        results.append(local("mixed", mixed, mixed_hbm))
        results.append(local("grad_hidden", grad_hidden, grad_hidden_hbm))
        results.append(local("ada", out_ada, ada_hbm))
        results.append(local("grad_cond", grad_cond, grad_cond_hbm))
        results += small_out()
        links.drain()
        for copy in results:
            copy.wait()

    def send_rows():
        grads = jnp.concatenate([sums[index : index + 1] for index in range(6)], axis=1)
        qv = jnp.concatenate([sums[6:7], sums[7:8]], axis=1)
        for index in range(GROUP):
            row = jnp.concatenate(
                [
                    grads[:, ADA * index : ADA * index + ADA],
                    jnp.zeros((1, 64), F32),
                    qv[:, 576 * index : 576 * index + 576],
                    sums[8:9][:, 288 * index : 288 * index + 288],
                    sums[10 + index : 11 + index],
                    sums[9:10][:, 288 * index : 288 * index + 288],
                ],
                axis=1,
            )
            row_stage[index] = row.reshape(32, 128).astype(BF16)
        for to in NEAR:
            links.send(
                ("row", to),
                to,
                lambda to=to: (row_stage.at[place.m_at(to)], row_group.at[m_here]),
            )
        row_group[m_here] = row_stage[m_here]

    def gather_rows():
        for to in NEAR:
            links.arrived(("row", to))
        for index in range(GROUP):
            row_all[place.h_index, 16 * index : 16 * index + 16] = row_group[index, :16]
        biases_here = jnp.sum(row_group[...].astype(F32), axis=0)[14:]
        row_all[place.h_index, 64:96] = jnp.concatenate(
            [biases_here, jnp.zeros((14, 128), F32)], axis=0
        ).astype(BF16)
        for to in FAR:
            links.send(
                ("rows", to), to, lambda: (row_all.at[place.h_index], row_all.at[place.h_index])
            )

    def ada_grads(load, ada, spread, cond_all, cond_stage, out_ada):
        for to in FAR:
            links.arrived(("rows", to))
            links.arrived(("silu", to))
        for to in ("l", "lc", "c"):
            for x in range(2):
                links.left(("gb", to, x))
        images = GROUP * INNER
        spread[...] = silu_all[...].astype(F32).reshape(images * 16, 128)

        def tile(index):
            return spread[pl.ds(index, images, stride=16), :]

        silu_rows = jnp.concatenate([tile(index) for index in range(9)], axis=1)
        gb_t[:, :images] = silu_rows.T.astype(BF16)
        spread[...] = row_all[:, :64].astype(F32).reshape(images * 16, 128)
        columns = jnp.concatenate([tile(index) for index in range(14)], axis=1)[:, :ADA]
        out_ada_b[...] = sum_rows(columns).reshape(ADA)
        columns = columns.astype(BF16)
        rows = pl.ds(pl.multiple_of(place.h_index * BLOCK, BLOCK), BLOCK)
        out_ada[...] = dot(gb_t[rows, :images], columns)
        local("ada", out_ada, ada_hbm).start()
        totals = jnp.sum(row_all[:, 64:96].astype(F32), axis=0)
        totals = jnp.concatenate([totals[index : index + 1] for index in range(18)], axis=1)
        start = 0
        for out in (out_qv_b, out_proj_b, out_up_b, out_down_b):
            width = out.shape[0]
            out[...] = totals[:, start : start + width].reshape(width)
            start += width
        for copy in small_out():
            copy.start()
        load.wait()
        cond_all[...] = dot(columns, ada[...])
        for to in NEAR:
            row = place.h_index * GROUP + place.m_at(to)
            cond_stage[place.m_at(to)] = jnp.broadcast_to(cond_all[pl.ds(row, 1), :], (8, D))
            links.send(
                ("gc", to), to, lambda to=to: (cond_stage.at[place.m_at(to)], cond_in.at[m_here])
            )

    def finish_cond(cond_all):
        total = cond_all[pl.ds(place.h_index * GROUP + m_here, 1), :]
        for to in NEAR:
            links.arrived(("gc", to))
            total += cond_in[place.m_at(to)][:1]
        values = cond[...].astype(F32)
        sigmoid = jax.nn.sigmoid(values)
        grad_cond[...] = total * (sigmoid * (1.0 + values * (1.0 - sigmoid)))

    def local_work(act_stage, pre_stage):
        f32_rows = pltpu.VMEM((SEQ, D), F32)
        pl.run_scoped(
            partial(feed_forward, act_stage, pre_stage),
            f32_rows,
            f32_rows,
            f32_rows,
        )
        pl.run_scoped(
            attention_back,
            pltpu.VMEM((3, SEQ, D), BF16),
            pltpu.VMEM((GROUP, SEQ, 896), BF16),
            pltpu.VMEM((SEQ, WINDOW), BF16),
        )
        for pair in range(2):
            links.left(("act", "l", pair))
        for to in NEAR:
            for part in range(2):
                links.left(("u", to, part))

    pl.run_scoped(
        local_work, pltpu.VMEM((3, SEQ, D), BF16), pltpu.VMEM((3, SEQ, D), BF16)
    )
    pl.run_scoped(
        reduce_rest,
        pltpu.VMEM((ADA, D), BF16),
        pltpu.VMEM((GROUP * INNER * 16, 128), F32),
        pltpu.VMEM((GROUP * INNER, D), F32),
        pltpu.VMEM((GROUP, 8, D), F32),
        pltpu.VMEM((BLOCK, ADA), F32),
        pltpu.VMEM((BLOCK, 864), F32),
        pltpu.VMEM((BLOCK, 288), F32),
        pltpu.VMEM((BLOCK, D), F32),
        pltpu.VMEM((288, 576), F32),
    )


TOGETHER = 4
UP_AXES = ("ylh", "ylh")
UP_LANES = ((0, 640), (640, 512))
QKV_LANES = ((0, 512), (512, 384))
QKV_AXES = ("rph", "rph")


def run_block(outer, *operands):
    anywhere = pl.BlockSpec(memory_space=pl.ANY)
    smem = pl.BlockSpec(memory_space=pltpu.SMEM)
    scratch = [((1, D), BF16)]
    scratch += [((width,), BF16) for width in (ADA, 2 * D, D, FF, D)]
    scratch += [((1, D), F32)] + [((width,), F32) for width in (ADA, 576, 288, D, 288)]
    scratch += [
        ((1, SEQ, D), BF16),
        ((1, SEQ, D), BF16),
        ((SEQ, D), BF16),
        ((SEQ, D), F32),
        ((1, 9 * D + ADA), F32),
        ((SLOTS, D, D), BF16),
        ((GROUP, 16, D), BF16),
        ((GROUP, 16, 1792), BF16),
        ((8, D), F32),
        ((D, TOKENS), BF16),
        ((4, BLOCK, TOKENS), BF16),
        ((D, TOKENS), BF16),
        ((2, TOKENS, D), BF16),
        ((2, 288, TOKENS), BF16),
        ((TOKENS, D), BF16),
        ((TOKENS, 896), BF16),
        ((TOKENS, WINDOW), BF16),
        ((D, SEQ), BF16),
        ((SEQ, D), BF16),
        ((SEQ, D), BF16),
        ((4, 2, BLOCK, SEQ), BF16),
        ((3, SEQ, D), BF16),
        ((SEQ, D), F32),
        ((16, D), F32),
        ((GROUP, 32, 128), BF16),
        ((GROUP, 32, 128), BF16),
        ((INNER, 96, 128), BF16),
        ((INNER, GROUP, 16, 128), BF16),
        ((GROUP, 8, D), F32),
    ]
    block = (BLOCK, D)
    scratch += [((2, 2, 2) + block, BF16)] * 2
    scratch += [((2, 2) + block, BF16)] * 2 + [((2,) + block, BF16)] * 2 + [(block, BF16)] * 2
    block = (BLOCK, 896)
    scratch += [((2, 2, 2) + block, BF16), ((2, 2) + block, BF16), ((2,) + block, BF16)]
    scratch += [(block, BF16)]
    block = (48, 896)
    scratch += [((2, 2, 2) + block, BF16), ((2, 2) + block, BF16), ((2,) + block, BF16)]
    scratch += [(block, BF16)]
    outs = [
        ((SEQ, D), BF16),
        ((SEQ, D), F32),
        ((1, D), F32),
        ((BLOCK, ADA), F32),
        ((ADA,), F32),
        ((BLOCK, 864), F32),
        ((576,), F32),
        ((BLOCK, 288), F32),
        ((288,), F32),
        ((BLOCK, D), F32),
        ((D,), F32),
        ((288, 576), F32),
        ((288,), F32),
    ]
    outs = [jax.ShapeDtypeStruct(*out) for out in outs]
    results = pl.pallas_call(
        partial(block_kernel, outer),
        out_shape=outs,
        in_specs=[anywhere, anywhere, smem] + [anywhere] * 11,
        out_specs=[anywhere] * len(outs),
        scratch_shapes=[pltpu.VMEM(*each) for each in scratch]
        + [
            pltpu.SemaphoreType.DMA((128,)),
            pltpu.SemaphoreType.DMA((128,)),
            pltpu.SemaphoreType.DMA((SLOTS,)),
            pltpu.SemaphoreType.DMA((len(LOCAL),)),
        ],
        compiler_params=pltpu.CompilerParams(
            collective_id=0, has_side_effects=True, vmem_limit_bytes=VMEM_LIMIT
        ),
    )(*operands)
    return pl.pallas_call(
        place_kernel,
        out_shape=outs,
        in_specs=[anywhere] * len(outs),
        out_specs=[anywhere] * len(outs),
        scratch_shapes=[pltpu.VMEM(out.shape, out.dtype) for out in outs]
        + [pltpu.SemaphoreType.DMA((2, len(outs)))],
    )(*results)


VMEM_LIMIT = 63 * 2**20 + 900 * 2**10
LOCAL = (
    "ada_in", "hidden", "out_grad", "mixed", "grad_hidden", "ada_back", "ada", "down", "proj",
    "up", "qkv", "cond", "ada_bias", "qv_bias", "proj_bias", "up_bias", "down_bias", "grad_cond",
    "ada_b", "qv_b", "proj_b", "up_b", "down_b",
)


def place_kernel(*refs):
    count = len(refs) // 3
    sems = refs[-1]
    here = [
        pltpu.make_async_copy(refs[index], refs[2 * count + index], sems.at[0, index])
        for index in range(count)
    ]
    there = [
        pltpu.make_async_copy(refs[2 * count + index], refs[count + index], sems.at[1, index])
        for index in range(count)
    ]
    for copy in here:
        copy.start()
    for first, second in zip(here, there):
        first.wait()
        second.start()
    for copy in there:
        copy.wait()


def on_device(
    outer,
    hidden_in,
    conditioning,
    live_images,
    out_grad,
    ada_weight,
    ada_bias,
    qkv_weight,
    qv_bias,
    proj_weight,
    proj_bias,
    up_weight,
    up_bias,
    down_weight,
    down_bias,
):
    (
        mixed,
        grad_hidden,
        grad_cond,
        out_ada_w,
        out_ada_b,
        out_qkv_w,
        out_qv_b,
        out_proj_w,
        out_proj_b,
        out_up_w,
        out_up_b,
        out_down_w,
        out_down_b,
    ) = run_block(
        outer,
        hidden_in,
        conditioning,
        live_images,
        out_grad,
        ada_bias,
        qv_bias,
        proj_bias,
        up_bias,
        down_bias,
        ada_weight.T,
        qkv_weight,
        proj_weight,
        up_weight,
        down_weight,
    )
    out_down_w = out_down_w.T
    if outer > 1:
        groups = [[h * outer + low for low in range(outer)] for h in range(INNER)]
        out_ada_w, out_down_w, out_up_w, out_qkv_w, out_proj_w = (
            lax.psum_scatter(
                part, "dp", scatter_dimension=0, tiled=True, axis_index_groups=groups
            )
            for part in (out_ada_w, out_down_w, out_up_w, out_qkv_w, out_proj_w)
        )
        out_ada_b, out_qv_b, out_proj_b, out_up_b, out_down_b = (
            jnp.sum(
                lax.all_gather(part, "dp", axis=0, axis_index_groups=groups), axis=0
            )
            for part in (out_ada_b, out_qv_b, out_proj_b, out_up_b, out_down_b)
        )
    return (
        mixed[None],
        grad_hidden[None],
        grad_cond,
        out_ada_w,
        out_ada_b,
        out_qkv_w,
        out_qv_b,
        out_proj_w,
        out_proj_b,
        out_up_w,
        out_up_b,
        out_down_w,
        out_down_b,
    )


def solution(mesh):
    in_specs = (
        P(("dp", "mp"), None, None),
        P(("dp", "mp"), None),
        P(("dp", "mp")),
        P(("dp", "mp"), None, None),
        P(None, "mp"),
        P("mp"),
        P(),
        P(),
        P(),
        P(),
        P(),
        P(),
        P(),
        P(),
    )
    out_specs = (
        P(("dp", "mp"), None, None),
        P(("dp", "mp"), None, None),
        P(("dp", "mp"), None),
        P("dp", "mp"),
        P("mp"),
        P("dp", "mp"),
        P("mp"),
        P("dp", "mp"),
        P("mp"),
        P("dp", "mp"),
        P("mp"),
        P("dp", "mp"),
        P("mp"),
    )
    return jax.shard_map(
        partial(on_device, mesh.shape["dp"] // INNER),
        mesh=mesh,
        in_specs=in_specs,
        out_specs=out_specs,
        check_vma=False,
    )
```
